32 devices in a mesh: groups: 2 (over x), view: 16 (over z, y, core).
Axes of the slice: x: 2, y: 2, z: 4, core: 2. Of those that a mesh axis runs over, the one named last changes fastest.
Arguments:
- query_vectors: bfloat16 [32, 16, 8, 4096], P(('groups', 'view')), parts along dimension 0, may hold values from -6 to 6
- key_vectors: bfloat16 [32, 16, 8, 4096], P(('groups', 'view')), parts along dimension 0, may hold values from -6 to 6
- value_vectors: bfloat16 [32, 16, 8, 4096], P(('groups', 'view')), parts along dimension 0, may hold values from -6 to 6
- request_of_slot: int32 [8], P('groups'), parts along dimension 0, may hold values from 0 to 2, as said below
Outputs:
- attended: bfloat16 [32, 16, 8, 4096], P(('groups', 'view')), parts along dimension 0
The draws below stay inside these ranges and needn't reach their ends.
There are 2 independent parts, one for each index of `groups`. The reference program is written for one: setup_inputs(seed, part) draws one part's arguments, and reference() takes and returns one part's arrays. A program takes and returns all parts, laid end to end along the dimension named above; each array names one. Nothing has to cross between parts.
Inputs may be any that keep to these rules, and one draw needn't show every extreme that they name: `request_of_slot`: each request holds 1 to 2 slots, not necessarily consecutive, and one holds exactly 2.
All inputs are finite; a program needn't handle non-finite values.
Results may differ from the reference program's by a relative error of at most 0.0044.
Values may be sent and summed in bfloat16 or wider, within the bound.
A program may use at most 64 MiB of HBM per device.

```python
import jax
import jax.numpy as jnp
from jax import lax

HEADS = 32
HS = 128
ROWS = 16
COLS = 8
VSLOTS = 4
IMAGES = 16
REQS = 3
MAXV = 2


def drawn_pair(key):
    full_shape = (IMAGES, ROWS, COLS, HEADS * HS)
    query_draw = jnp.clip(jax.random.normal(jax.random.fold_in(key, 701), full_shape, jnp.float32), -5.5, 5.5)
    key_draw = jnp.clip(jax.random.normal(jax.random.fold_in(key, 702), full_shape, jnp.float32), -5.5, 5.5)
    return (query_draw, key_draw)


def draw_query_vectors(key, part):
    return drawn_pair(key)[0].astype(jnp.bfloat16)


def draw_key_vectors(key, part):
    return drawn_pair(key)[1].astype(jnp.bfloat16)


def draw_request_of_slot(key, part):
    half_slots = VSLOTS // 2
    extras_count = VSLOTS - MAXV - REQS + 1
    extra_labels = jax.random.randint(jax.random.fold_in(key, 801), (extras_count,), 1, REQS).astype(jnp.int32)
    raw_labels = jnp.concatenate([jnp.zeros((MAXV,), jnp.int32), jnp.arange(1, REQS, dtype=jnp.int32), extra_labels])
    relabel = jax.random.permutation(jax.random.fold_in(key, 802), REQS).astype(jnp.int32)
    sequence = relabel[raw_labels]
    start_slot = jax.random.randint(jax.random.fold_in(key, 803), (), 0, half_slots).astype(jnp.int32)
    scores = jax.random.permutation(jax.random.fold_in(key, 804), VSLOTS).astype(jnp.int32)
    scores = scores.at[start_slot].set(-2).at[start_slot + half_slots].set(-1)
    placing = jnp.argsort(scores, stable=True).astype(jnp.int32)
    return jnp.zeros((VSLOTS,), jnp.int32).at[placing].set(sequence)


def shard_levels(key, shape, shards, least, top_value):
    loudness, own = 1.0, jax.random.fold_in(key, 6)
    for axis_at, shards_of in shards:
        draws = jnp.exp(jax.random.uniform(jax.random.fold_in(own, axis_at), (shards_of,), jnp.float32, least / len(shards), top_value / len(shards)))
        loudness = loudness * jnp.repeat(draws, shape[axis_at] // shards_of).reshape([-1 if axis == axis_at else 1 for axis in range(len(shape))])
    return loudness


def gaussian(stream_key, shape, scale, reach, shards=(), kind=jnp.bfloat16):
    gain = shard_levels(stream_key, shape, shards, -0.22, 0.18) if shards else 1.0
    array = jax.random.normal(stream_key, shape, jnp.float32) * scale * gain
    return jnp.minimum(jnp.maximum(array, -reach), reach).astype(kind)


def setup_inputs(seed: int = 0, part: int = 0) -> dict:
    arg_keys = jax.random.split(jax.random.key(seed), 5)
    part_keys = jax.random.split(jax.random.fold_in(arg_keys[4], part), 5)
    return {
        "query_vectors": draw_query_vectors(jax.random.fold_in(jax.random.fold_in(arg_keys[4], part), 71), part),
        "key_vectors": draw_key_vectors(jax.random.fold_in(jax.random.fold_in(arg_keys[4], part), 71), part),
        "value_vectors": gaussian(part_keys[2], (IMAGES, ROWS, COLS, HEADS * HS), 1.0, 6.0, ((0, 16),)),
        "request_of_slot": draw_request_of_slot(jax.random.fold_in(jax.random.fold_in(arg_keys[4], part), 71), part),
    }


NEG_FILL = -1.0e30


def partial_softmax(query_part, key_part, value_part, allowed):
    scaling = HS ** -0.5
    scores = jnp.einsum("nhx,khx->hnk", query_part.astype(jnp.float32), key_part.astype(jnp.float32)) * scaling
    scores = jnp.where(allowed[None], scores, NEG_FILL)
    maximum = jnp.max(scores, axis=2)
    raised = jnp.exp(scores - maximum[:, :, None])
    totals = jnp.sum(raised, axis=2)
    weights = lax.optimization_barrier(raised.astype(jnp.bfloat16))
    summed = jnp.einsum("hnk,khx->nhx", weights.astype(jnp.float32), value_part.astype(jnp.float32))
    return maximum.T, totals.T, summed


def combine(first_part, second_part):
    highest = jnp.maximum(first_part[0], second_part[0])
    first_scale = jnp.exp(first_part[0] - highest)
    second_scale = jnp.exp(second_part[0] - highest)
    denominator = first_part[1] * first_scale + second_part[1] * second_scale
    numerator = first_part[2] * first_scale[..., None] + second_part[2] * second_scale[..., None]
    return (numerator / denominator[..., None]).astype(jnp.bfloat16)


def reference(query_vectors, key_vectors, value_vectors, request_of_slot):
    pair_tokens = 2 * ROWS * COLS

    def by_slot(tensor):
        return tensor.reshape(2 * VSLOTS, pair_tokens, HEADS, HS)

    def by_row(tensor):
        shaped = tensor.reshape(VSLOTS, 2, 2, ROWS, COLS, HEADS, HS)
        return shaped.transpose(1, 3, 0, 2, 4, 5, 6).reshape(2 * ROWS, 2 * VSLOTS * COLS, HEADS, HS)

    def from_row(tensor):
        trailing = tensor.shape[2:]
        shaped = tensor.reshape((2, ROWS, VSLOTS, 2, COLS) + trailing)
        permuted = (2, 0, 3, 1, 4) + tuple(range(5, 5 + len(trailing)))
        return shaped.transpose(permuted).reshape((IMAGES, ROWS, COLS) + trailing)

    row_index = (jnp.arange(pair_tokens) // COLS) % ROWS
    local_allowed = row_index[:, None] != row_index[None, :]
    slot_request = jnp.broadcast_to(request_of_slot[:, None], (VSLOTS, 2 * COLS)).reshape(-1)
    row_allowed = slot_request[:, None] == slot_request[None, :]

    def local_step(triple):
        return partial_softmax(triple[0], triple[1], triple[2], local_allowed)

    def row_step(triple):
        return partial_softmax(triple[0], triple[1], triple[2], row_allowed)

    local_raw = lax.map(local_step, (by_slot(query_vectors), by_slot(key_vectors), by_slot(value_vectors)))
    local_part = tuple(part_item.reshape((IMAGES, ROWS, COLS) + part_item.shape[2:]) for part_item in local_raw)
    row_raw = lax.map(row_step, (by_row(query_vectors), by_row(key_vectors), by_row(value_vectors)))
    row_part = tuple(from_row(part_item) for part_item in row_raw)
    attended = combine(local_part, row_part)
    return attended.reshape(IMAGES, ROWS, COLS, HEADS * HS)
```

```python
import jax
import jax.numpy as jnp
from jax import lax
from jax.experimental import pallas as pl
from jax.experimental.pallas import tpu as pltpu
from jax.sharding import PartitionSpec as P

HEADS = 32
HS = 128
ROWS = 16
COLS = 8


NEG_FILL = -1e30


def partner(value, axis, distance):
    return lax.ppermute(value, axis, [(i, i ^ 1 << distance) for i in range(lax.axis_size(axis))])


def masked_softmax(scores, allowed):
    scores = jnp.where(allowed, scores, NEG_FILL)
    maximum = jnp.max(scores, axis=-1)
    raised = jnp.exp(scores - maximum[..., None])
    totals = jnp.sum(raised, axis=-1)
    return (maximum, totals, raised.astype(jnp.bfloat16))


def combine(first_part, second_part):
    highest = jnp.maximum(first_part[0], second_part[0])
    first_scale = jnp.exp(first_part[0] - highest)
    second_scale = jnp.exp(second_part[0] - highest)
    denominator = first_part[1] * first_scale + second_part[1] * second_scale
    numerator = first_part[2] * first_scale[..., None] + second_part[2] * second_scale[..., None]
    return (numerator / denominator[..., None]).astype(jnp.bfloat16)


def into_rows(tensor, row_blocks, head_groups):
    trailing = tensor.shape[3:]
    block_rows = tensor.shape[0] // row_blocks
    width_cols = tensor.shape[1]
    group_heads = tensor.shape[2] // head_groups
    shaped = tensor.reshape(
        (row_blocks, block_rows, width_cols, head_groups, group_heads) + trailing
    )
    permuted = (0, 3, 1, 2, 4) + tuple(range(5, 5 + len(trailing)))
    return shaped.transpose(permuted).reshape(
        (row_blocks * head_groups, block_rows, width_cols, group_heads) + trailing
    )


def into_tokens(tensor, row_blocks, head_groups):
    trailing = tensor.shape[4:]
    block_rows = tensor.shape[1]
    width_cols = tensor.shape[2]
    group_heads = tensor.shape[3]
    shaped = tensor.reshape(
        (row_blocks, head_groups, block_rows, width_cols, group_heads) + trailing
    )
    permuted = (0, 2, 3, 1, 4) + tuple(range(5, 5 + len(trailing)))
    return shaped.transpose(permuted).reshape(
        (row_blocks * block_rows * width_cols, head_groups * group_heads) + trailing
    )


def general_shards(query_vectors, key_vectors, value_vectors, request_of_slot):
    scaling = HS ** (-0.5)
    token_count = ROWS * COLS
    partner_key, partner_value = partner((key_vectors, value_vectors), "view", 0)
    head_blocks = 4
    block_heads = HEADS // head_blocks
    own_query = query_vectors.reshape(token_count, head_blocks, block_heads, HS)
    both_keys = jnp.concatenate(
        [
            key_vectors.reshape(token_count, head_blocks, block_heads, HS),
            partner_key.reshape(token_count, head_blocks, block_heads, HS),
        ],
        axis=0,
    )
    both_values = jnp.concatenate(
        [
            value_vectors.reshape(token_count, head_blocks, block_heads, HS),
            partner_value.reshape(token_count, head_blocks, block_heads, HS),
        ],
        axis=0,
    )
    query_row = jnp.arange(token_count) // COLS
    key_row = jnp.arange(2 * token_count) % token_count // COLS
    local_allowed = query_row[:, None] != key_row[None, :]

    def local_block(triple):
        block_scores = (
            jnp.einsum("nhx,khx->hnk", triple[0], triple[1], preferred_element_type=jnp.float32)
            * scaling
        )
        block_peak, block_total, block_weights = masked_softmax(block_scores, local_allowed[None])
        block_sum = jnp.einsum(
            "hnk,khx->nhx", block_weights, triple[2], preferred_element_type=jnp.float32
        )
        return (block_peak.T, block_total.T, block_sum)

    block_peaks, block_totals, block_sums = lax.map(
        local_block,
        (
            jnp.moveaxis(own_query, 1, 0),
            jnp.moveaxis(both_keys, 1, 0),
            jnp.moveaxis(both_values, 1, 0),
        ),
    )
    local_peak = jnp.moveaxis(block_peaks, 0, 1).reshape(token_count, HEADS)
    local_total = jnp.moveaxis(block_totals, 0, 1).reshape(token_count, HEADS)
    local_sum = jnp.moveaxis(block_sums, 0, 1).reshape(token_count, HEADS, HS)
    device_count = lax.axis_size("view")
    slot_count = device_count // 4
    pass_images = device_count // 2
    head_groups = 8
    row_blocks = device_count // head_groups
    block_rows = ROWS // row_blocks
    slot_request = jnp.broadcast_to(
        request_of_slot[:, None], (request_of_slot.shape[0], 2 * COLS)
    ).reshape(-1)
    row_allowed = slot_request[:, None] == slot_request[None, :]

    def arrange(tensor):
        shaped = tensor.reshape(slot_count, 2, 2, block_rows, COLS, HS).transpose(1, 3, 0, 2, 4, 5)
        return shaped.reshape(2 * block_rows, pass_images * COLS, HS)

    def restore(tensor):
        trailing = tensor.shape[2:]
        shaped = tensor.reshape((2, block_rows, slot_count, 2, COLS) + trailing)
        permuted = (2, 0, 3, 1, 4) + tuple(range(5, 5 + len(trailing)))
        return shaped.transpose(permuted).reshape((device_count, block_rows, COLS) + trailing)

    def one_head(triple):
        row_scores = (
            jnp.einsum(
                "bnx,bkx->bnk",
                arrange(triple[0]),
                arrange(triple[1]),
                preferred_element_type=jnp.float32,
            )
            * scaling
        )
        row_peak, row_total, row_weights = masked_softmax(row_scores, row_allowed[None])
        row_sum = jnp.einsum(
            "bnk,bkx->bnx", row_weights, arrange(triple[2]), preferred_element_type=jnp.float32
        )
        return (restore(row_peak), restore(row_total), restore(row_sum))

    query_rows = into_rows(query_vectors.reshape(ROWS, COLS, HEADS, HS), row_blocks, head_groups)
    key_rows = into_rows(key_vectors.reshape(ROWS, COLS, HEADS, HS), row_blocks, head_groups)
    value_rows = into_rows(value_vectors.reshape(ROWS, COLS, HEADS, HS), row_blocks, head_groups)
    by_head = (
        jnp.moveaxis(
            lax.all_to_all(query_rows, "view", split_axis=0, concat_axis=0, tiled=True), 3, 0
        ),
        jnp.moveaxis(
            lax.all_to_all(key_rows, "view", split_axis=0, concat_axis=0, tiled=True), 3, 0
        ),
        jnp.moveaxis(
            lax.all_to_all(value_rows, "view", split_axis=0, concat_axis=0, tiled=True), 3, 0
        ),
    )
    row_peaks, row_totals, row_sums = lax.map(one_head, by_head)
    peak_part = jnp.moveaxis(row_peaks, 0, 3)
    total_part = jnp.moveaxis(row_totals, 0, 3)
    sum_part = jnp.moveaxis(row_sums, 0, 3)
    row_peak = lax.all_to_all(peak_part, "view", split_axis=0, concat_axis=0, tiled=True)
    row_total = lax.all_to_all(total_part, "view", split_axis=0, concat_axis=0, tiled=True)
    row_sum = lax.all_to_all(sum_part, "view", split_axis=0, concat_axis=0, tiled=True)
    row_peak = into_tokens(row_peak, row_blocks, head_groups)
    row_total = into_tokens(row_total, row_blocks, head_groups)
    row_sum = into_tokens(row_sum, row_blocks, head_groups)
    attended = combine((local_peak, local_total, local_sum), (row_peak, row_total, row_sum))
    return attended.reshape(1, ROWS, COLS, HEADS * HS)


def pair_kernel(
    req_ref, q_ref, k_ref, v_ref, o_ref,
    queries, kv, outer, inner, crossing, ending, results, sums, peaks, totals,
    swap_send, swap_recv, own_send, outer_recv, cross_send, inner_recv, end_send, out_send, out_recv,
):
    half, _, tokens, size = queries.shape
    me = lax.axis_index("view")
    domain = me % 2
    slot = me // 4
    other = 1 - domain
    twin = me + other - domain
    upper = slot // 2
    end_slot = 3 * upper
    mid_slot = 1 + upper
    is_end = slot == end_slot
    is_mid = slot == mid_slot
    near = me + 4 * (end_slot + mid_slot - 2 * slot)
    across = me + 4 * (3 - 2 * slot)

    mine = req_ref[slot]
    end_same = (req_ref[end_slot] == mine).astype(jnp.int32)
    mid_same = (req_ref[mid_slot] == mine).astype(jnp.int32)
    far_same = jnp.maximum(
        (req_ref[3 - end_slot] == mine).astype(jnp.int32), (req_ref[3 - mid_slot] == mine).astype(jnp.int32)
    )
    near_same = jnp.minimum(end_same, mid_same)
    paired = jnp.maximum(near_same, far_same)

    def remote(src, dst, send, recv, device):
        return pltpu.make_async_remote_copy(
            src_ref=src, dst_ref=dst, send_sem=send, recv_sem=recv,
            device_id={"view": device}, device_id_type=pl.DeviceIdType.MESH,
        )

    def lanes(at, group):
        return pl.ds(pl.multiple_of((group * half + at) * size, size), size)

    def swap(at, which):
        source = (k_ref, v_ref, q_ref)[which].at[:, lanes(at, other)]
        target = queries.at[at, domain] if which == 2 else kv.at[at, which, domain]
        return remote(source, target, swap_send.at[which, at], swap_recv.at[which, at], twin)

    def swapped(at, which):
        source = (k_ref, v_ref, q_ref)[which].at[:, lanes(at, other)]
        target = queries.at[at, other] if which == 2 else kv.at[at, which, other]
        return remote(source, target, swap_send.at[which, at], swap_recv.at[which, at], twin)

    def own_copy(at):
        return remote(kv.at[at], outer.at[at], own_send.at[at], outer_recv.at[at], near)

    def cross_copy(at):
        return remote(crossing.at[at], inner.at[at], cross_send.at[at], inner_recv.at[at], across)

    def end_copy(at):
        return remote(ending.at[at], inner.at[at], end_send.at[at], inner_recv.at[at], near)

    def out_copy(at):
        return remote(
            results.at[at], o_ref.at[:, lanes(at, domain)], out_send.at[at], out_recv.at[at], twin
        )

    barrier = pltpu.get_barrier_semaphore()
    for device in (twin, near):
        pl.semaphore_signal(barrier, inc=1, device_id={"view": device}, device_id_type=pl.DeviceIdType.MESH)

    @pl.when(is_mid)
    def _():
        pl.semaphore_signal(barrier, inc=1, device_id={"view": across}, device_id_type=pl.DeviceIdType.MESH)
        pl.semaphore_wait(barrier, 3)

    @pl.when(is_end)
    def _():
        pl.semaphore_wait(barrier, 2)

    @pl.loop(0, half)
    def _(at):
        swap(at, 0).start()
        swap(at, 1).start()

    @pl.loop(0, half)
    def _(at):
        swap(at, 2).start()

    @pl.loop(0, half)
    def _(at):
        kv[at, 0, domain] = k_ref[:, lanes(at, domain)]
        kv[at, 1, domain] = v_ref[:, lanes(at, domain)]
        queries[at, domain] = q_ref[:, lanes(at, domain)]
        swapped(at, 0).wait_recv()
        swapped(at, 1).wait_recv()

        @pl.when(is_end)
        def _():
            own_copy(at).start()

    def pass_across(at):
        @pl.when(is_mid)
        def _():
            own_copy(at).wait_recv()
            crossing[at] = jnp.where(far_same > 0, kv[at], outer[at])
            cross_copy(at).start()

    def pass_out(at):
        cross_copy(at).wait_recv()

        @pl.when(is_mid)
        def _():
            ending[at] = jnp.where(near_same > 0, kv[at], inner[at])
            end_copy(at).start()

    scaling = size ** (-0.5)

    def scores_of(at, keys):
        return (
            lax.dot_general(
                queries[at].reshape(2 * tokens, size), keys, (((1,), (1,)), ((), ())),
                preferred_element_type=jnp.float32,
            )
            * scaling
        )

    def own_part(at):
        swapped(at, 2).wait_recv()
        scores = scores_of(at, kv[at, 0].reshape(2 * tokens, size))
        peak = jnp.max(scores, axis=1, keepdims=True)
        raised = jnp.exp(scores - peak)
        peaks[at] = peak
        totals[at] = jnp.sum(raised, axis=1, keepdims=True)
        sums[at] = jnp.dot(
            raised.astype(jnp.bfloat16), kv[at, 1].reshape(2 * tokens, size), preferred_element_type=jnp.float32
        )

    def pair_part(at, keys, values):
        scores = scores_of(at, keys.reshape(2 * tokens, size))
        query_row = lax.broadcasted_iota(jnp.int32, scores.shape, 0) % tokens // COLS
        key_row = lax.broadcasted_iota(jnp.int32, scores.shape, 1) % tokens // COLS
        scores = jnp.where(query_row == key_row, scores, NEG_FILL)
        scores = jnp.where(paired > 0, scores, NEG_FILL)
        own_peak = peaks[at]
        peak = jnp.maximum(own_peak, jnp.max(scores, axis=1, keepdims=True))
        raised = jnp.exp(scores - peak)
        kept = jnp.exp(own_peak - peak)
        total = totals[at] * kept + jnp.sum(raised, axis=1, keepdims=True)
        summed = sums[at] * kept + jnp.dot(
            raised.astype(jnp.bfloat16), values.reshape(2 * tokens, size), preferred_element_type=jnp.float32
        )
        sums[at] = summed / total
        o_ref[:, lanes(at, domain)] = sums[at, pl.ds(pl.multiple_of(domain * tokens, tokens), tokens)].astype(
            jnp.bfloat16
        )
        results[at] = sums[at, pl.ds(pl.multiple_of(other * tokens, tokens), tokens)].astype(jnp.bfloat16)
        out_copy(at).start()

    def finish(at):
        @pl.when(is_mid)
        def _():
            pair_part(
                at,
                jnp.where(near_same > 0, outer[at, 0], inner[at, 0]),
                jnp.where(near_same > 0, outer[at, 1], inner[at, 1]),
            )

        @pl.when(is_end)
        def _():
            pair_part(at, inner[at, 0], inner[at, 1])

    pass_across(0)
    own_part(0)

    @pl.loop(1, half)
    def _(at):
        pass_across(at)
        pass_out(at - 1)
        own_part(at)
        finish(at - 1)

    pass_out(half - 1)
    finish(half - 1)

    @pl.loop(0, half)
    def _(at):
        for which in range(3):
            swap(at, which).wait_send()

        @pl.when(is_end)
        def _():
            own_copy(at).wait_send()

        @pl.when(is_mid)
        def _():
            cross_copy(at).wait_send()
            end_copy(at).wait_send()

        out_copy(at).wait_send()
        remote(
            results.at[at], o_ref.at[:, lanes(at, other)], out_send.at[at], out_recv.at[at], twin
        ).wait_recv()


def pair_shards(query_vectors, key_vectors, value_vectors, request_of_slot):
    tokens = ROWS * COLS
    half = HEADS // 2
    flat = [tensor.reshape(tokens, HEADS * HS) for tensor in (query_vectors, key_vectors, value_vectors)]
    vmem = pl.BlockSpec(memory_space=pltpu.VMEM)
    bank = pltpu.VMEM((half, 2, 2, tokens, HS), jnp.bfloat16)
    column = pltpu.VMEM((half, 2 * tokens, 1), jnp.float32)
    each = pltpu.SemaphoreType.DMA((half,))
    three = pltpu.SemaphoreType.DMA((3, half))
    pair_flops = 2 * 2 * 2 * (2 * tokens) * (2 * tokens) * HS * half
    out = pl.pallas_call(
        pair_kernel,
        out_shape=jax.ShapeDtypeStruct((tokens, HEADS * HS), jnp.bfloat16),
        in_specs=[pl.BlockSpec(memory_space=pltpu.SMEM), vmem, vmem, vmem],
        out_specs=vmem,
        scratch_shapes=[
            pltpu.VMEM((half, 2, tokens, HS), jnp.bfloat16),
            bank, bank, bank, bank, bank,
            pltpu.VMEM((half, tokens, HS), jnp.bfloat16),
            pltpu.VMEM((half, 2 * tokens, HS), jnp.float32),
            column, column,
            three, three, each, each, each, each, each, each, each,
        ],
        compiler_params=pltpu.CompilerParams(
            collective_id=0, has_side_effects=True, vmem_limit_bytes=48 * 1024 * 1024
        ),
        cost_estimate=pl.CostEstimate(
            flops=pair_flops, bytes_accessed=4 * tokens * HEADS * HS * 2, transcendentals=8 * tokens * tokens * half
        ),
    )(request_of_slot, *flat)
    return out.reshape(1, ROWS, COLS, HEADS * HS)


def solution(mesh):
    slot_count = mesh.shape["view"] // 4
    shards = pair_shards if slot_count == 4 else general_shards
    return jax.shard_map(
        shards,
        mesh=mesh,
        in_specs=(
            P(("groups", "view"), None, None, None),
            P(("groups", "view"), None, None, None),
            P(("groups", "view"), None, None, None),
            P("groups"),
        ),
        out_specs=P(("groups", "view"), None, None, None),
        check_vma=False,
    )
```

```python
import jax
import jax.numpy as jnp
from jax import lax
from jax.experimental import pallas as pl
from jax.experimental.pallas import tpu as pltpu
from jax.sharding import PartitionSpec as P

HEADS = 32
HS = 128
ROWS = 16
COLS = 8
LOG2E = 1.4426950408889634
VMEM_LIMIT = 60 * 1024 * 1024


NEG_FILL = -1e30


def partner(value, axis, distance):
    return lax.ppermute(value, axis, [(i, i ^ 1 << distance) for i in range(lax.axis_size(axis))])


def masked_softmax(scores, allowed):
    scores = jnp.where(allowed, scores, NEG_FILL)
    maximum = jnp.max(scores, axis=-1)
    raised = jnp.exp(scores - maximum[..., None])
    totals = jnp.sum(raised, axis=-1)
    return (maximum, totals, raised.astype(jnp.bfloat16))


def combine(first_part, second_part):
    highest = jnp.maximum(first_part[0], second_part[0])
    first_scale = jnp.exp(first_part[0] - highest)
    second_scale = jnp.exp(second_part[0] - highest)
    denominator = first_part[1] * first_scale + second_part[1] * second_scale
    numerator = first_part[2] * first_scale[..., None] + second_part[2] * second_scale[..., None]
    return (numerator / denominator[..., None]).astype(jnp.bfloat16)


def into_rows(tensor, row_blocks, head_groups):
    trailing = tensor.shape[3:]
    block_rows = tensor.shape[0] // row_blocks
    width_cols = tensor.shape[1]
    group_heads = tensor.shape[2] // head_groups
    shaped = tensor.reshape(
        (row_blocks, block_rows, width_cols, head_groups, group_heads) + trailing
    )
    permuted = (0, 3, 1, 2, 4) + tuple(range(5, 5 + len(trailing)))
    return shaped.transpose(permuted).reshape(
        (row_blocks * head_groups, block_rows, width_cols, group_heads) + trailing
    )


def into_tokens(tensor, row_blocks, head_groups):
    trailing = tensor.shape[4:]
    block_rows = tensor.shape[1]
    width_cols = tensor.shape[2]
    group_heads = tensor.shape[3]
    shaped = tensor.reshape(
        (row_blocks, head_groups, block_rows, width_cols, group_heads) + trailing
    )
    permuted = (0, 2, 3, 1, 4) + tuple(range(5, 5 + len(trailing)))
    return shaped.transpose(permuted).reshape(
        (row_blocks * block_rows * width_cols, head_groups * group_heads) + trailing
    )


def general_shards(query_vectors, key_vectors, value_vectors, request_of_slot):
    scaling = HS ** (-0.5)
    token_count = ROWS * COLS
    partner_key, partner_value = partner((key_vectors, value_vectors), "view", 0)
    head_blocks = 4
    block_heads = HEADS // head_blocks
    own_query = query_vectors.reshape(token_count, head_blocks, block_heads, HS)
    both_keys = jnp.concatenate(
        [
            key_vectors.reshape(token_count, head_blocks, block_heads, HS),
            partner_key.reshape(token_count, head_blocks, block_heads, HS),
        ],
        axis=0,
    )
    both_values = jnp.concatenate(
        [
            value_vectors.reshape(token_count, head_blocks, block_heads, HS),
            partner_value.reshape(token_count, head_blocks, block_heads, HS),
        ],
        axis=0,
    )
    query_row = jnp.arange(token_count) // COLS
    key_row = jnp.arange(2 * token_count) % token_count // COLS
    local_allowed = query_row[:, None] != key_row[None, :]

    def local_block(triple):
        block_scores = (
            jnp.einsum("nhx,khx->hnk", triple[0], triple[1], preferred_element_type=jnp.float32)
            * scaling
        )
        block_peak, block_total, block_weights = masked_softmax(block_scores, local_allowed[None])
        block_sum = jnp.einsum(
            "hnk,khx->nhx", block_weights, triple[2], preferred_element_type=jnp.float32
        )
        return (block_peak.T, block_total.T, block_sum)

    block_peaks, block_totals, block_sums = lax.map(
        local_block,
        (
            jnp.moveaxis(own_query, 1, 0),
            jnp.moveaxis(both_keys, 1, 0),
            jnp.moveaxis(both_values, 1, 0),
        ),
    )
    local_peak = jnp.moveaxis(block_peaks, 0, 1).reshape(token_count, HEADS)
    local_total = jnp.moveaxis(block_totals, 0, 1).reshape(token_count, HEADS)
    local_sum = jnp.moveaxis(block_sums, 0, 1).reshape(token_count, HEADS, HS)
    device_count = lax.axis_size("view")
    slot_count = device_count // 4
    pass_images = device_count // 2
    head_groups = 8
    row_blocks = device_count // head_groups
    block_rows = ROWS // row_blocks
    slot_request = jnp.broadcast_to(
        request_of_slot[:, None], (request_of_slot.shape[0], 2 * COLS)
    ).reshape(-1)
    row_allowed = slot_request[:, None] == slot_request[None, :]

    def arrange(tensor):
        shaped = tensor.reshape(slot_count, 2, 2, block_rows, COLS, HS).transpose(1, 3, 0, 2, 4, 5)
        return shaped.reshape(2 * block_rows, pass_images * COLS, HS)

    def restore(tensor):
        trailing = tensor.shape[2:]
        shaped = tensor.reshape((2, block_rows, slot_count, 2, COLS) + trailing)
        permuted = (2, 0, 3, 1, 4) + tuple(range(5, 5 + len(trailing)))
        return shaped.transpose(permuted).reshape((device_count, block_rows, COLS) + trailing)

    def one_head(triple):
        row_scores = (
            jnp.einsum(
                "bnx,bkx->bnk",
                arrange(triple[0]),
                arrange(triple[1]),
                preferred_element_type=jnp.float32,
            )
            * scaling
        )
        row_peak, row_total, row_weights = masked_softmax(row_scores, row_allowed[None])
        row_sum = jnp.einsum(
            "bnk,bkx->bnx", row_weights, arrange(triple[2]), preferred_element_type=jnp.float32
        )
        return (restore(row_peak), restore(row_total), restore(row_sum))

    query_rows = into_rows(query_vectors.reshape(ROWS, COLS, HEADS, HS), row_blocks, head_groups)
    key_rows = into_rows(key_vectors.reshape(ROWS, COLS, HEADS, HS), row_blocks, head_groups)
    value_rows = into_rows(value_vectors.reshape(ROWS, COLS, HEADS, HS), row_blocks, head_groups)
    by_head = (
        jnp.moveaxis(
            lax.all_to_all(query_rows, "view", split_axis=0, concat_axis=0, tiled=True), 3, 0
        ),
        jnp.moveaxis(
            lax.all_to_all(key_rows, "view", split_axis=0, concat_axis=0, tiled=True), 3, 0
        ),
        jnp.moveaxis(
            lax.all_to_all(value_rows, "view", split_axis=0, concat_axis=0, tiled=True), 3, 0
        ),
    )
    row_peaks, row_totals, row_sums = lax.map(one_head, by_head)
    peak_part = jnp.moveaxis(row_peaks, 0, 3)
    total_part = jnp.moveaxis(row_totals, 0, 3)
    sum_part = jnp.moveaxis(row_sums, 0, 3)
    row_peak = lax.all_to_all(peak_part, "view", split_axis=0, concat_axis=0, tiled=True)
    row_total = lax.all_to_all(total_part, "view", split_axis=0, concat_axis=0, tiled=True)
    row_sum = lax.all_to_all(sum_part, "view", split_axis=0, concat_axis=0, tiled=True)
    row_peak = into_tokens(row_peak, row_blocks, head_groups)
    row_total = into_tokens(row_total, row_blocks, head_groups)
    row_sum = into_tokens(row_sum, row_blocks, head_groups)
    attended = combine((local_peak, local_total, local_sum), (row_peak, row_total, row_sum))
    return attended.reshape(1, ROWS, COLS, HEADS * HS)


PARTS = 4
SKEW = 2
AHEAD = 2


def pair_kernel(
    req_ref, q_ref, k_ref, v_ref, o_ref,
    queries, kv, outer, inner, crossing, ending, chosen, bias, results, sums, peaks, totals,
    load_sem, swap_send, swap_recv, own_send, outer_recv, cross_send, inner_recv, end_send, out_send, out_recv,
):
    half, _, tokens, size = queries.shape
    span = 4 // PARTS
    me = lax.axis_index("view")
    domain = me % 2
    slot = me // 4
    other = 1 - domain
    twin = me + other - domain
    upper = slot // 2
    end_slot = 3 * upper
    mid_slot = 1 + upper
    is_end = slot == end_slot
    is_mid = slot == mid_slot
    near = me + 4 * (end_slot + mid_slot - 2 * slot)
    across = me + 4 * (3 - 2 * slot)

    mine = req_ref[slot]
    end_same = (req_ref[end_slot] == mine).astype(jnp.int32)
    mid_same = (req_ref[mid_slot] == mine).astype(jnp.int32)
    far_same = jnp.maximum(
        (req_ref[3 - end_slot] == mine).astype(jnp.int32), (req_ref[3 - mid_slot] == mine).astype(jnp.int32)
    )
    near_same = jnp.minimum(end_same, mid_same)
    paired = jnp.maximum(near_same, far_same)

    def remote(src, dst, send, recv, device):
        return pltpu.make_async_remote_copy(
            src_ref=src, dst_ref=dst, send_sem=send, recv_sem=recv,
            device_id={"view": device}, device_id_type=pl.DeviceIdType.MESH,
        )

    def lanes(at, group):
        return pl.ds(pl.multiple_of((group * half + at) * size, size), size)

    def unit(ref, number):
        return ref.at[pl.ds(number * span, span)]

    def place(at, which, owner):
        return queries.at[at, owner] if which == 2 else kv.at[at * 4 + which * 2 + owner]

    sources = (k_ref, v_ref, q_ref)

    def load(at, which):
        return pltpu.make_async_copy(
            sources[which].at[:, lanes(at, domain)], place(at, which, domain), load_sem.at[which, at]
        )

    def swap(at, which, owner):
        return remote(
            sources[which].at[:, lanes(at, other)], place(at, which, owner),
            swap_send.at[which, at], swap_recv.at[which, at], twin,
        )

    def fetch(at, which):
        swap(at, which, domain).start()
        load(at, which).start()

    def fetched(at, which):
        swap(at, which, other).wait_recv()
        load(at, which).wait()

    def own_copy(n):
        return remote(unit(kv, n), unit(outer, n), own_send.at[n], outer_recv.at[n], near)

    def cross_copy(n):
        return remote(unit(crossing, n), unit(inner, n), cross_send.at[n], inner_recv.at[n], across)

    def end_copy(n):
        return remote(unit(ending, n), unit(inner, n), end_send.at[n], inner_recv.at[n], near)

    def out_copy(at, group):
        return remote(
            results.at[at], o_ref.at[:, lanes(at, group)], out_send.at[at], out_recv.at[at], twin
        )

    barrier = pltpu.get_barrier_semaphore()
    for device in (twin, near):
        pl.semaphore_signal(barrier, inc=1, device_id={"view": device}, device_id_type=pl.DeviceIdType.MESH)

    @pl.when(is_mid)
    def _():
        pl.semaphore_signal(barrier, inc=1, device_id={"view": across}, device_id_type=pl.DeviceIdType.MESH)
        pl.semaphore_wait(barrier, 3)

    @pl.when(is_end)
    def _():
        pl.semaphore_wait(barrier, 2)

    for at in range(AHEAD):
        for which in range(2):
            fetch(at, which)

    @pl.when(is_end)
    def _():
        @pl.loop(0, half)
        def _(at):
            @pl.when(at + AHEAD < half)
            def _():
                for which in range(2):
                    fetch(at + AHEAD, which)

            for which in range(2):
                fetched(at, which)
            for part in range(PARTS):
                own_copy(at * PARTS + part).start()

    for at in range(AHEAD):
        fetch(at, 2)

    query_row = lax.broadcasted_iota(jnp.int32, bias.shape, 0) % tokens // COLS
    key_row = lax.broadcasted_iota(jnp.int32, bias.shape, 1) % tokens // COLS
    bias[...] = jnp.where(paired > 0, jnp.where(query_row == key_row, 0.0, NEG_FILL), NEG_FILL)

    def pass_across(n):
        @pl.when(is_mid)
        def _():
            own_copy(n).wait_recv()
            at = pl.ds(n * span, span)
            crossing[at] = jnp.where(far_same > 0, kv[at], outer[at])
            cross_copy(n).start()

    def pass_out(n):
        cross_copy(n).wait_recv()

        @pl.when(is_mid)
        def _():
            at = pl.ds(n * span, span)
            ending[at] = jnp.where(near_same > 0, kv[at], inner[at])
            end_copy(n).start()

    scaling = size ** (-0.5) * LOG2E

    def scores_of(at, keys):
        return (
            lax.dot_general(
                queries[at].reshape(2 * tokens, size), keys.reshape(2 * tokens, size), (((1,), (1,)), ((), ())),
                preferred_element_type=jnp.float32,
            )
            * scaling
        )

    def weighted(raised, values):
        return jnp.dot(
            raised.astype(jnp.bfloat16), values.reshape(2 * tokens, size), preferred_element_type=jnp.float32
        )

    def own_part(at):
        fetched(at, 2)
        scores = scores_of(at, kv[pl.ds(at * 4, 2)])
        peak = jnp.max(scores, axis=1, keepdims=True)
        raised = jnp.exp2(scores - peak)
        peaks[at] = peak
        totals[at] = jnp.sum(raised, axis=1, keepdims=True)
        sums[at] = weighted(raised, kv[pl.ds(at * 4 + 2, 2)])

    def finish(at):
        @pl.when(is_mid)
        def _():
            chosen[...] = jnp.where(near_same > 0, outer[pl.ds(at * 4, 4)], inner[pl.ds(at * 4, 4)])

        @pl.when(is_end)
        def _():
            chosen[...] = inner[pl.ds(at * 4, 4)]

        scores = scores_of(at, chosen[pl.ds(0, 2)]) + bias[...]
        own_peak = peaks[at]
        peak = jnp.maximum(own_peak, jnp.max(scores, axis=1, keepdims=True))
        raised = jnp.exp2(scores - peak)
        kept = jnp.exp2(own_peak - peak)
        total = totals[at] * kept + jnp.sum(raised, axis=1, keepdims=True)
        sums[at] = (sums[at] * kept + weighted(raised, chosen[pl.ds(2, 2)])) / total
        results[at] = sums[at, pl.ds(pl.multiple_of(other * tokens, tokens), tokens)].astype(jnp.bfloat16)
        out_copy(at, domain).start()
        o_ref[:, lanes(at, domain)] = sums[at, pl.ds(pl.multiple_of(domain * tokens, tokens), tokens)].astype(
            jnp.bfloat16
        )

    def head(at, first):
        @pl.when(is_mid)
        def _():
            @pl.when(at + AHEAD < half)
            def _():
                for which in range(2):
                    fetch(at + AHEAD, which)

            for which in range(2):
                fetched(at, which)

        @pl.when(at + AHEAD < half)
        def _():
            fetch(at + AHEAD, 2)

        for part in range(PARTS):
            pass_across(at * PARTS + part)
            if part >= SKEW or not first:
                pass_out(at * PARTS + part - SKEW)
            if part == 0:
                own_part(at)
            if part == PARTS // 2 and not first:
                finish(at - 1)

    head(0, True)

    @pl.loop(1, half)
    def _(at):
        head(at, False)

    for late in range(SKEW):
        pass_out(half * PARTS - SKEW + late)
    finish(half - 1)

    @pl.loop(0, half)
    def _(at):
        for which in range(3):
            swap(at, which, domain).wait_send()

        for part in range(PARTS):

            @pl.when(is_end)
            def _():
                own_copy(at * PARTS + part).wait_send()

            @pl.when(is_mid)
            def _():
                cross_copy(at * PARTS + part).wait_send()
                end_copy(at * PARTS + part).wait_send()

        out_copy(at, domain).wait_send()
        out_copy(at, other).wait_recv()


def pair_shards(query_vectors, key_vectors, value_vectors, request_of_slot):
    tokens = ROWS * COLS
    half = HEADS // 2
    flat = [tensor.reshape(tokens, HEADS * HS) for tensor in (query_vectors, key_vectors, value_vectors)]
    vmem = pl.BlockSpec(memory_space=pltpu.VMEM)
    anywhere = pl.BlockSpec(memory_space=pl.ANY)
    bank = pltpu.VMEM((half * 4, tokens, HS), jnp.bfloat16)
    column = pltpu.VMEM((half, 2 * tokens, 1), jnp.float32)
    each = pltpu.SemaphoreType.DMA((half,))
    three = pltpu.SemaphoreType.DMA((3, half))
    units = pltpu.SemaphoreType.DMA((half * PARTS,))
    pair_flops = 2 * 2 * 2 * (2 * tokens) * (2 * tokens) * HS * half
    out = pl.pallas_call(
        pair_kernel,
        out_shape=jax.ShapeDtypeStruct((tokens, HEADS * HS), jnp.bfloat16),
        in_specs=[pl.BlockSpec(memory_space=pltpu.SMEM), anywhere, anywhere, anywhere],
        out_specs=vmem,
        scratch_shapes=[
            pltpu.VMEM((half, 2, tokens, HS), jnp.bfloat16),
            bank, bank, bank, bank, bank,
            pltpu.VMEM((4, tokens, HS), jnp.bfloat16),
            pltpu.VMEM((2 * tokens, 2 * tokens), jnp.float32),
            pltpu.VMEM((half, tokens, HS), jnp.bfloat16),
            pltpu.VMEM((half, 2 * tokens, HS), jnp.float32),
            column, column,
            three, three, three, units, units, units, units, units, each, each,
        ],
        compiler_params=pltpu.CompilerParams(
            collective_id=0, has_side_effects=True, vmem_limit_bytes=VMEM_LIMIT
        ),
        cost_estimate=pl.CostEstimate(
            flops=pair_flops, bytes_accessed=4 * tokens * HEADS * HS * 2, transcendentals=8 * tokens * tokens * half
        ),
    )(request_of_slot, *flat)
    return out.reshape(1, ROWS, COLS, HEADS * HS)


def solution(mesh):
    slot_count = mesh.shape["view"] // 4
    shards = pair_shards if slot_count == 4 else general_shards
    return jax.shard_map(
        shards,
        mesh=mesh,
        in_specs=(
            P(("groups", "view"), None, None, None),
            P(("groups", "view"), None, None, None),
            P(("groups", "view"), None, None, None),
            P("groups"),
        ),
        out_specs=P(("groups", "view"), None, None, None),
        check_vma=False,
    )
```

```python
import jax
import jax.numpy as jnp
from jax import lax
from jax.experimental import pallas as pl
from jax.experimental.pallas import tpu as pltpu
from jax.sharding import PartitionSpec as P

HEADS = 32
HS = 128
ROWS = 16
COLS = 8
LOG2E = 1.4426950408889634
VMEM_LIMIT = 209 * 256 * 1024


NEG_FILL = -1e30


def partner(value, axis, distance):
    return lax.ppermute(value, axis, [(i, i ^ 1 << distance) for i in range(lax.axis_size(axis))])


def masked_softmax(scores, allowed):
    scores = jnp.where(allowed, scores, NEG_FILL)
    maximum = jnp.max(scores, axis=-1)
    raised = jnp.exp(scores - maximum[..., None])
    totals = jnp.sum(raised, axis=-1)
    return (maximum, totals, raised.astype(jnp.bfloat16))


def combine(first_part, second_part):
    highest = jnp.maximum(first_part[0], second_part[0])
    first_scale = jnp.exp(first_part[0] - highest)
    second_scale = jnp.exp(second_part[0] - highest)
    denominator = first_part[1] * first_scale + second_part[1] * second_scale
    numerator = first_part[2] * first_scale[..., None] + second_part[2] * second_scale[..., None]
    return (numerator / denominator[..., None]).astype(jnp.bfloat16)


def into_rows(tensor, row_blocks, head_groups):
    trailing = tensor.shape[3:]
    block_rows = tensor.shape[0] // row_blocks
    width_cols = tensor.shape[1]
    group_heads = tensor.shape[2] // head_groups
    shaped = tensor.reshape(
        (row_blocks, block_rows, width_cols, head_groups, group_heads) + trailing
    )
    permuted = (0, 3, 1, 2, 4) + tuple(range(5, 5 + len(trailing)))
    return shaped.transpose(permuted).reshape(
        (row_blocks * head_groups, block_rows, width_cols, group_heads) + trailing
    )


def into_tokens(tensor, row_blocks, head_groups):
    trailing = tensor.shape[4:]
    block_rows = tensor.shape[1]
    width_cols = tensor.shape[2]
    group_heads = tensor.shape[3]
    shaped = tensor.reshape(
        (row_blocks, head_groups, block_rows, width_cols, group_heads) + trailing
    )
    permuted = (0, 2, 3, 1, 4) + tuple(range(5, 5 + len(trailing)))
    return shaped.transpose(permuted).reshape(
        (row_blocks * block_rows * width_cols, head_groups * group_heads) + trailing
    )


def general_shards(query_vectors, key_vectors, value_vectors, request_of_slot):
    scaling = HS ** (-0.5)
    token_count = ROWS * COLS
    partner_key, partner_value = partner((key_vectors, value_vectors), "view", 0)
    head_blocks = 4
    block_heads = HEADS // head_blocks
    own_query = query_vectors.reshape(token_count, head_blocks, block_heads, HS)
    both_keys = jnp.concatenate(
        [
            key_vectors.reshape(token_count, head_blocks, block_heads, HS),
            partner_key.reshape(token_count, head_blocks, block_heads, HS),
        ],
        axis=0,
    )
    both_values = jnp.concatenate(
        [
            value_vectors.reshape(token_count, head_blocks, block_heads, HS),
            partner_value.reshape(token_count, head_blocks, block_heads, HS),
        ],
        axis=0,
    )
    query_row = jnp.arange(token_count) // COLS
    key_row = jnp.arange(2 * token_count) % token_count // COLS
    local_allowed = query_row[:, None] != key_row[None, :]

    def local_block(triple):
        block_scores = (
            jnp.einsum("nhx,khx->hnk", triple[0], triple[1], preferred_element_type=jnp.float32)
            * scaling
        )
        block_peak, block_total, block_weights = masked_softmax(block_scores, local_allowed[None])
        block_sum = jnp.einsum(
            "hnk,khx->nhx", block_weights, triple[2], preferred_element_type=jnp.float32
        )
        return (block_peak.T, block_total.T, block_sum)

    block_peaks, block_totals, block_sums = lax.map(
        local_block,
        (
            jnp.moveaxis(own_query, 1, 0),
            jnp.moveaxis(both_keys, 1, 0),
            jnp.moveaxis(both_values, 1, 0),
        ),
    )
    local_peak = jnp.moveaxis(block_peaks, 0, 1).reshape(token_count, HEADS)
    local_total = jnp.moveaxis(block_totals, 0, 1).reshape(token_count, HEADS)
    local_sum = jnp.moveaxis(block_sums, 0, 1).reshape(token_count, HEADS, HS)
    device_count = lax.axis_size("view")
    slot_count = device_count // 4
    pass_images = device_count // 2
    head_groups = 8
    row_blocks = device_count // head_groups
    block_rows = ROWS // row_blocks
    slot_request = jnp.broadcast_to(
        request_of_slot[:, None], (request_of_slot.shape[0], 2 * COLS)
    ).reshape(-1)
    row_allowed = slot_request[:, None] == slot_request[None, :]

    def arrange(tensor):
        shaped = tensor.reshape(slot_count, 2, 2, block_rows, COLS, HS).transpose(1, 3, 0, 2, 4, 5)
        return shaped.reshape(2 * block_rows, pass_images * COLS, HS)

    def restore(tensor):
        trailing = tensor.shape[2:]
        shaped = tensor.reshape((2, block_rows, slot_count, 2, COLS) + trailing)
        permuted = (2, 0, 3, 1, 4) + tuple(range(5, 5 + len(trailing)))
        return shaped.transpose(permuted).reshape((device_count, block_rows, COLS) + trailing)

    def one_head(triple):
        row_scores = (
            jnp.einsum(
                "bnx,bkx->bnk",
                arrange(triple[0]),
                arrange(triple[1]),
                preferred_element_type=jnp.float32,
            )
            * scaling
        )
        row_peak, row_total, row_weights = masked_softmax(row_scores, row_allowed[None])
        row_sum = jnp.einsum(
            "bnk,bkx->bnx", row_weights, arrange(triple[2]), preferred_element_type=jnp.float32
        )
        return (restore(row_peak), restore(row_total), restore(row_sum))

    query_rows = into_rows(query_vectors.reshape(ROWS, COLS, HEADS, HS), row_blocks, head_groups)
    key_rows = into_rows(key_vectors.reshape(ROWS, COLS, HEADS, HS), row_blocks, head_groups)
    value_rows = into_rows(value_vectors.reshape(ROWS, COLS, HEADS, HS), row_blocks, head_groups)
    by_head = (
        jnp.moveaxis(
            lax.all_to_all(query_rows, "view", split_axis=0, concat_axis=0, tiled=True), 3, 0
        ),
        jnp.moveaxis(
            lax.all_to_all(key_rows, "view", split_axis=0, concat_axis=0, tiled=True), 3, 0
        ),
        jnp.moveaxis(
            lax.all_to_all(value_rows, "view", split_axis=0, concat_axis=0, tiled=True), 3, 0
        ),
    )
    row_peaks, row_totals, row_sums = lax.map(one_head, by_head)
    peak_part = jnp.moveaxis(row_peaks, 0, 3)
    total_part = jnp.moveaxis(row_totals, 0, 3)
    sum_part = jnp.moveaxis(row_sums, 0, 3)
    row_peak = lax.all_to_all(peak_part, "view", split_axis=0, concat_axis=0, tiled=True)
    row_total = lax.all_to_all(total_part, "view", split_axis=0, concat_axis=0, tiled=True)
    row_sum = lax.all_to_all(sum_part, "view", split_axis=0, concat_axis=0, tiled=True)
    row_peak = into_tokens(row_peak, row_blocks, head_groups)
    row_total = into_tokens(row_total, row_blocks, head_groups)
    row_sum = into_tokens(row_sum, row_blocks, head_groups)
    attended = combine((local_peak, local_total, local_sum), (row_peak, row_total, row_sum))
    return attended.reshape(1, ROWS, COLS, HEADS * HS)


PARTS = 4
SKEW = 4
GROUPS = 2
AHEAD = 2


def pair_kernel(
    req_hbm, q_ref, k_ref, v_ref, o_ref,
    req_ref, queries, kv, outer, inner, crossing, ending, chosen, bias, results, sums, peaks, totals,
    req_sem, load_sem, swap_send, swap_recv, own_send, outer_recv, cross_send, inner_recv, end_send, out_send, out_recv, out_sem,
):
    half, _, _, rows, size = queries.shape
    block = 2 * rows
    span = 4 // PARTS
    me = lax.axis_index("view")
    domain = me % 2
    slot = me // 4
    other = 1 - domain
    twin = me + other - domain
    upper = slot // 2
    end_slot = 3 * upper
    mid_slot = 1 + upper
    is_end = slot == end_slot
    is_mid = slot == mid_slot
    near = me + 4 * (end_slot + mid_slot - 2 * slot)
    across = me + 4 * (3 - 2 * slot)

    def remote(src, dst, send, recv, device):
        return pltpu.make_async_remote_copy(
            src_ref=src, dst_ref=dst, send_sem=send, recv_sem=recv,
            device_id={"view": device}, device_id_type=pl.DeviceIdType.MESH,
        )

    def lanes(at, group):
        return pl.ds(pl.multiple_of((group * half + at) * size, size), size)

    def unit(ref, number):
        return ref.at[pl.ds(number * span, span)]

    def place(at, which, owner):
        return queries.at[at, :, owner] if which == 2 else kv.at[at * 4 + which * 2 + owner]

    sources = (k_ref, v_ref, q_ref)

    def load(at, which):
        return pltpu.make_async_copy(
            sources[which].at[:, :, lanes(at, domain)], place(at, which, domain), load_sem.at[which, at]
        )

    def swap(at, which, owner):
        return remote(
            sources[which].at[:, :, lanes(at, other)], place(at, which, owner),
            swap_send.at[which, at], swap_recv.at[which, at], twin,
        )

    def fetch(at, which):
        swap(at, which, domain).start()
        load(at, which).start()

    def fetched(at, which):
        swap(at, which, other).wait_recv()
        load(at, which).wait()

    def own_copy(n):
        return remote(unit(kv, n), unit(outer, n), own_send.at[n], outer_recv.at[n], near)

    def cross_copy(n):
        return remote(unit(crossing, n), unit(inner, n), cross_send.at[n], inner_recv.at[n], across)

    def end_copy(n):
        return remote(unit(ending, n), unit(inner, n), end_send.at[n], inner_recv.at[n], near)

    def out_copy(at, group):
        return remote(
            results.at[at, other], o_ref.at[:, :, lanes(at, group)], out_send.at[at], out_recv.at[at], twin
        )

    def keep_copy(at):
        return pltpu.make_async_copy(results.at[at, domain], o_ref.at[:, :, lanes(at, domain)], out_sem.at[at])

    request = pltpu.make_async_copy(req_hbm, req_ref, req_sem)
    request.start()
    barrier = pltpu.get_barrier_semaphore()
    for device in (twin, near):
        pl.semaphore_signal(barrier, inc=1, device_id={"view": device}, device_id_type=pl.DeviceIdType.MESH)

    @pl.when(is_mid)
    def _():
        pl.semaphore_signal(barrier, inc=1, device_id={"view": across}, device_id_type=pl.DeviceIdType.MESH)
        pl.semaphore_wait(barrier, 3)

    @pl.when(is_end)
    def _():
        pl.semaphore_wait(barrier, 2)

    for at in range(AHEAD):
        for which in range(2):
            fetch(at, which)

    @pl.when(is_end)
    def _():
        @pl.loop(0, half)
        def _(at):
            @pl.when(at + AHEAD < half)
            def _():
                for which in range(2):
                    fetch(at + AHEAD, which)

            for which in range(2):
                fetched(at, which)
            for part in range(PARTS):
                own_copy(at * PARTS + part).start()

    for at in range(AHEAD):
        fetch(at, 2)

    request.wait()
    mine = req_ref[slot]
    end_same = (req_ref[end_slot] == mine).astype(jnp.int32)
    mid_same = (req_ref[mid_slot] == mine).astype(jnp.int32)
    far_same = jnp.maximum(
        (req_ref[3 - end_slot] == mine).astype(jnp.int32), (req_ref[3 - mid_slot] == mine).astype(jnp.int32)
    )
    near_same = jnp.minimum(end_same, mid_same)
    paired = jnp.maximum(near_same, far_same)

    query_row = lax.broadcasted_iota(jnp.int32, bias.shape, 0) % rows // COLS
    key_row = lax.broadcasted_iota(jnp.int32, bias.shape, 1) % rows // COLS
    bias[...] = jnp.where(paired > 0, jnp.where(query_row == key_row, 0.0, NEG_FILL), NEG_FILL)

    def pass_across(n):
        @pl.when(is_mid)
        def _():
            own_copy(n).wait_recv()
            at = pl.ds(n * span, span)
            crossing[at] = jnp.where(far_same > 0, kv[at], outer[at])
            cross_copy(n).start()

    def pass_out(n):
        cross_copy(n).wait_recv()

        @pl.when(is_mid)
        def _():
            at = pl.ds(n * span, span)
            ending[at] = jnp.where(near_same > 0, kv[at], inner[at])
            end_copy(n).start()

    scaling = size ** (-0.5) * LOG2E

    def scores_of(keys, asking):
        return (
            lax.dot_general(keys, asking, (((1,), (1,)), ((), ())), preferred_element_type=jnp.float32) * scaling
        )

    def weighted(raised, values):
        return lax.dot_general(
            values, raised.astype(jnp.bfloat16), (((0,), (0,)), ((), ())), preferred_element_type=jnp.float32
        )

    def own_part(at):
        fetched(at, 2)
        scores = scores_of(
            kv[pl.ds(at * 4, 2)].reshape(GROUPS * block, size), queries[at].reshape(GROUPS * block, size)
        )
        peak = jnp.max(scores, axis=0, keepdims=True)
        raised = jnp.exp2(scores - peak)
        peaks[at] = peak
        totals[at] = jnp.sum(raised, axis=0, keepdims=True)
        sums[at] = weighted(raised, kv[pl.ds(at * 4 + 2, 2)].reshape(GROUPS * block, size))

    def finish(at):
        @pl.when(is_mid)
        def _():
            chosen[...] = jnp.where(near_same > 0, outer[pl.ds(at * 4, 4)], inner[pl.ds(at * 4, 4)])

        @pl.when(is_end)
        def _():
            chosen[...] = inner[pl.ds(at * 4, 4)]

        for group in range(GROUPS):
            columns = slice(group * block, (group + 1) * block)
            scores = scores_of(
                chosen[0:2, group].reshape(block, size), queries[at, group].reshape(block, size)
            ) + bias[...]
            own_peak = peaks[at, :, columns]
            peak = jnp.maximum(own_peak, jnp.max(scores, axis=0, keepdims=True))
            raised = jnp.exp2(scores - peak)
            kept = jnp.exp2(own_peak - peak)
            total = totals[at, :, columns] * kept + jnp.sum(raised, axis=0, keepdims=True)
            summed = sums[at, :, columns] * kept + weighted(raised, chosen[2:4, group].reshape(block, size))
            attended = (summed / total).T.astype(jnp.bfloat16)
            results[at, :, group] = attended.reshape(2, rows, size)
        out_copy(at, domain).start()
        keep_copy(at).start()

    def head(at, first):
        @pl.when(is_mid)
        def _():
            @pl.when(at + AHEAD < half)
            def _():
                for which in range(2):
                    fetch(at + AHEAD, which)

            for which in range(2):
                fetched(at, which)

        @pl.when(at + AHEAD < half)
        def _():
            fetch(at + AHEAD, 2)

        for part in range(PARTS):
            pass_across(at * PARTS + part)
            if part >= SKEW or not first:
                pass_out(at * PARTS + part - SKEW)
            if part == 1:
                own_part(at)
            if part == PARTS - 1 and not first:
                finish(at - 1)

    head(0, True)

    @pl.loop(1, half)
    def _(at):
        head(at, False)

    for late in range(SKEW):
        pass_out(half * PARTS - SKEW + late)
    finish(half - 1)

    @pl.loop(0, half)
    def _(at):
        for which in range(3):
            swap(at, which, domain).wait_send()

        for part in range(PARTS):

            @pl.when(is_end)
            def _():
                own_copy(at * PARTS + part).wait_send()

            @pl.when(is_mid)
            def _():
                cross_copy(at * PARTS + part).wait_send()
                end_copy(at * PARTS + part).wait_send()

        keep_copy(at).wait()
        out_copy(at, domain).wait_send()
        out_copy(at, other).wait_recv()


def pair_shards(query_vectors, key_vectors, value_vectors, request_of_slot):
    rows = ROWS * COLS // GROUPS
    half = HEADS // 2
    flat = [tensor.reshape(GROUPS, rows, HEADS * HS) for tensor in (query_vectors, key_vectors, value_vectors)]
    vmem = pl.BlockSpec(memory_space=pltpu.VMEM)
    hbm = pl.BlockSpec(memory_space=pltpu.HBM)
    bank = pltpu.VMEM((half * 4, GROUPS, rows, HS), jnp.bfloat16)
    line = pltpu.VMEM((half, 1, GROUPS * 2 * rows), jnp.float32)
    each = pltpu.SemaphoreType.DMA((half,))
    three = pltpu.SemaphoreType.DMA((3, half))
    units = pltpu.SemaphoreType.DMA((half * PARTS,))
    scores = (2 * ROWS * COLS) ** 2 * half
    out = pl.pallas_call(
        pair_kernel,
        out_shape=jax.ShapeDtypeStruct((GROUPS, rows, HEADS * HS), jnp.bfloat16),
        in_specs=[hbm, hbm, hbm, hbm],
        out_specs=vmem,
        scratch_shapes=[
            pltpu.SMEM(request_of_slot.shape, jnp.int32),
            pltpu.VMEM((half, GROUPS, 2, rows, HS), jnp.bfloat16),
            bank, bank, bank, bank, bank,
            pltpu.VMEM((4, GROUPS, rows, HS), jnp.bfloat16),
            pltpu.VMEM((2 * rows, 2 * rows), jnp.float32),
            pltpu.VMEM((half, 2, GROUPS, rows, HS), jnp.bfloat16),
            pltpu.VMEM((half, HS, GROUPS * 2 * rows), jnp.float32),
            line, line,
            pltpu.SemaphoreType.DMA, three, three, three, units, units, units, units, units, each, each, each,
        ],
        compiler_params=pltpu.CompilerParams(
            collective_id=0, has_side_effects=True, vmem_limit_bytes=VMEM_LIMIT
        ),
        cost_estimate=pl.CostEstimate(
            flops=6 * scores * HS, bytes_accessed=8 * ROWS * COLS * HEADS * HS, transcendentals=2 * scores
        ),
    )(request_of_slot, *flat)
    return out.reshape(1, ROWS, COLS, HEADS * HS)


def solution(mesh):
    slot_count = mesh.shape["view"] // 4
    shards = pair_shards if slot_count == 4 else general_shards
    return jax.shard_map(
        shards,
        mesh=mesh,
        in_specs=(
            P(("groups", "view"), None, None, None),
            P(("groups", "view"), None, None, None),
            P(("groups", "view"), None, None, None),
            P("groups"),
        ),
        out_specs=P(("groups", "view"), None, None, None),
        check_vma=False,
    )
```

```python
import jax
import jax.numpy as jnp
from jax import lax
from jax.experimental import pallas as pl
from jax.experimental.pallas import tpu as pltpu
from jax.sharding import PartitionSpec as P

HEADS = 32
HS = 128
ROWS = 16
COLS = 8
LOG2E = 1.4426950408889634
VMEM_LIMIT = 209 * 256 * 1024


NEG_FILL = -1e30


def partner(value, axis, distance):
    return lax.ppermute(value, axis, [(i, i ^ 1 << distance) for i in range(lax.axis_size(axis))])


def masked_softmax(scores, allowed):
    scores = jnp.where(allowed, scores, NEG_FILL)
    maximum = jnp.max(scores, axis=-1)
    raised = jnp.exp(scores - maximum[..., None])
    totals = jnp.sum(raised, axis=-1)
    return (maximum, totals, raised.astype(jnp.bfloat16))


def combine(first_part, second_part):
    highest = jnp.maximum(first_part[0], second_part[0])
    first_scale = jnp.exp(first_part[0] - highest)
    second_scale = jnp.exp(second_part[0] - highest)
    denominator = first_part[1] * first_scale + second_part[1] * second_scale
    numerator = first_part[2] * first_scale[..., None] + second_part[2] * second_scale[..., None]
    return (numerator / denominator[..., None]).astype(jnp.bfloat16)


def into_rows(tensor, row_blocks, head_groups):
    trailing = tensor.shape[3:]
    block_rows = tensor.shape[0] // row_blocks
    width_cols = tensor.shape[1]
    group_heads = tensor.shape[2] // head_groups
    shaped = tensor.reshape(
        (row_blocks, block_rows, width_cols, head_groups, group_heads) + trailing
    )
    permuted = (0, 3, 1, 2, 4) + tuple(range(5, 5 + len(trailing)))
    return shaped.transpose(permuted).reshape(
        (row_blocks * head_groups, block_rows, width_cols, group_heads) + trailing
    )


def into_tokens(tensor, row_blocks, head_groups):
    trailing = tensor.shape[4:]
    block_rows = tensor.shape[1]
    width_cols = tensor.shape[2]
    group_heads = tensor.shape[3]
    shaped = tensor.reshape(
        (row_blocks, head_groups, block_rows, width_cols, group_heads) + trailing
    )
    permuted = (0, 2, 3, 1, 4) + tuple(range(5, 5 + len(trailing)))
    return shaped.transpose(permuted).reshape(
        (row_blocks * block_rows * width_cols, head_groups * group_heads) + trailing
    )


def general_shards(query_vectors, key_vectors, value_vectors, request_of_slot):
    scaling = HS ** (-0.5)
    token_count = ROWS * COLS
    partner_key, partner_value = partner((key_vectors, value_vectors), "view", 0)
    head_blocks = 4
    block_heads = HEADS // head_blocks
    own_query = query_vectors.reshape(token_count, head_blocks, block_heads, HS)
    both_keys = jnp.concatenate(
        [
            key_vectors.reshape(token_count, head_blocks, block_heads, HS),
            partner_key.reshape(token_count, head_blocks, block_heads, HS),
        ],
        axis=0,
    )
    both_values = jnp.concatenate(
        [
            value_vectors.reshape(token_count, head_blocks, block_heads, HS),
            partner_value.reshape(token_count, head_blocks, block_heads, HS),
        ],
        axis=0,
    )
    query_row = jnp.arange(token_count) // COLS
    key_row = jnp.arange(2 * token_count) % token_count // COLS
    local_allowed = query_row[:, None] != key_row[None, :]

    def local_block(triple):
        block_scores = (
            jnp.einsum("nhx,khx->hnk", triple[0], triple[1], preferred_element_type=jnp.float32)
            * scaling
        )
        block_peak, block_total, block_weights = masked_softmax(block_scores, local_allowed[None])
        block_sum = jnp.einsum(
            "hnk,khx->nhx", block_weights, triple[2], preferred_element_type=jnp.float32
        )
        return (block_peak.T, block_total.T, block_sum)

    block_peaks, block_totals, block_sums = lax.map(
        local_block,
        (
            jnp.moveaxis(own_query, 1, 0),
            jnp.moveaxis(both_keys, 1, 0),
            jnp.moveaxis(both_values, 1, 0),
        ),
    )
    local_peak = jnp.moveaxis(block_peaks, 0, 1).reshape(token_count, HEADS)
    local_total = jnp.moveaxis(block_totals, 0, 1).reshape(token_count, HEADS)
    local_sum = jnp.moveaxis(block_sums, 0, 1).reshape(token_count, HEADS, HS)
    device_count = lax.axis_size("view")
    slot_count = device_count // 4
    pass_images = device_count // 2
    head_groups = 8
    row_blocks = device_count // head_groups
    block_rows = ROWS // row_blocks
    slot_request = jnp.broadcast_to(
        request_of_slot[:, None], (request_of_slot.shape[0], 2 * COLS)
    ).reshape(-1)
    row_allowed = slot_request[:, None] == slot_request[None, :]

    def arrange(tensor):
        shaped = tensor.reshape(slot_count, 2, 2, block_rows, COLS, HS).transpose(1, 3, 0, 2, 4, 5)
        return shaped.reshape(2 * block_rows, pass_images * COLS, HS)

    def restore(tensor):
        trailing = tensor.shape[2:]
        shaped = tensor.reshape((2, block_rows, slot_count, 2, COLS) + trailing)
        permuted = (2, 0, 3, 1, 4) + tuple(range(5, 5 + len(trailing)))
        return shaped.transpose(permuted).reshape((device_count, block_rows, COLS) + trailing)

    def one_head(triple):
        row_scores = (
            jnp.einsum(
                "bnx,bkx->bnk",
                arrange(triple[0]),
                arrange(triple[1]),
                preferred_element_type=jnp.float32,
            )
            * scaling
        )
        row_peak, row_total, row_weights = masked_softmax(row_scores, row_allowed[None])
        row_sum = jnp.einsum(
            "bnk,bkx->bnx", row_weights, arrange(triple[2]), preferred_element_type=jnp.float32
        )
        return (restore(row_peak), restore(row_total), restore(row_sum))

    query_rows = into_rows(query_vectors.reshape(ROWS, COLS, HEADS, HS), row_blocks, head_groups)
    key_rows = into_rows(key_vectors.reshape(ROWS, COLS, HEADS, HS), row_blocks, head_groups)
    value_rows = into_rows(value_vectors.reshape(ROWS, COLS, HEADS, HS), row_blocks, head_groups)
    by_head = (
        jnp.moveaxis(
            lax.all_to_all(query_rows, "view", split_axis=0, concat_axis=0, tiled=True), 3, 0
        ),
        jnp.moveaxis(
            lax.all_to_all(key_rows, "view", split_axis=0, concat_axis=0, tiled=True), 3, 0
        ),
        jnp.moveaxis(
            lax.all_to_all(value_rows, "view", split_axis=0, concat_axis=0, tiled=True), 3, 0
        ),
    )
    row_peaks, row_totals, row_sums = lax.map(one_head, by_head)
    peak_part = jnp.moveaxis(row_peaks, 0, 3)
    total_part = jnp.moveaxis(row_totals, 0, 3)
    sum_part = jnp.moveaxis(row_sums, 0, 3)
    row_peak = lax.all_to_all(peak_part, "view", split_axis=0, concat_axis=0, tiled=True)
    row_total = lax.all_to_all(total_part, "view", split_axis=0, concat_axis=0, tiled=True)
    row_sum = lax.all_to_all(sum_part, "view", split_axis=0, concat_axis=0, tiled=True)
    row_peak = into_tokens(row_peak, row_blocks, head_groups)
    row_total = into_tokens(row_total, row_blocks, head_groups)
    row_sum = into_tokens(row_sum, row_blocks, head_groups)
    attended = combine((local_peak, local_total, local_sum), (row_peak, row_total, row_sum))
    return attended.reshape(1, ROWS, COLS, HEADS * HS)


PARTS = 4
SKEW = 3
GROUPS = 2
AHEAD = 2


def pair_kernel(
    req_hbm, q_ref, k_ref, v_ref, o_ref,
    req_ref, queries, kv, outer, inner, crossing, ending, chosen, bias, results, sums, peaks, totals,
    req_sem, load_sem, swap_send, swap_recv, own_send, outer_recv, cross_send, inner_recv, end_send, out_send, out_recv, out_sem,
):
    half, _, _, rows, size = queries.shape
    block = 2 * rows
    span = 4 // PARTS
    me = lax.axis_index("view")
    domain = me % 2
    slot = me // 4
    other = 1 - domain
    twin = me + other - domain
    upper = slot // 2
    end_slot = 3 * upper
    mid_slot = 1 + upper
    is_end = slot == end_slot
    is_mid = slot == mid_slot
    near = me + 4 * (end_slot + mid_slot - 2 * slot)
    across = me + 4 * (3 - 2 * slot)

    def remote(src, dst, send, recv, device):
        return pltpu.make_async_remote_copy(
            src_ref=src, dst_ref=dst, send_sem=send, recv_sem=recv,
            device_id={"view": device}, device_id_type=pl.DeviceIdType.MESH,
        )

    def lanes(at, group):
        return pl.ds(pl.multiple_of((group * half + at) * size, size), size)

    def unit(ref, number):
        return ref.at[pl.ds(number * span, span)]

    def place(at, which, whose):
        return queries.at[at, whose] if which == 2 else kv.at[at * 4 + which * 2 + whose]

    sources = (k_ref, v_ref, q_ref)

    def load(at, which):
        return pltpu.make_async_copy(
            sources[which].at[:, :, lanes(at, domain)], place(at, which, 0), load_sem.at[which, at]
        )

    def swap(at, which):
        return remote(
            sources[which].at[:, :, lanes(at, other)], place(at, which, 1),
            swap_send.at[which], swap_recv.at[which, at], twin,
        )

    def fetched(at, which):
        load(at, which).wait()
        swap(at, which).wait_recv()

    def own_copy(n):
        return remote(unit(kv, n), unit(outer, n), own_send, outer_recv.at[n], near)

    def cross_copy(n):
        return remote(unit(crossing, n), unit(inner, n), cross_send, inner_recv.at[n], across)

    def end_copy(n):
        return remote(unit(ending, n), unit(inner, n), end_send, inner_recv.at[n], near)

    def out_copy(at):
        return remote(results.at[1, at], o_ref.at[:, :, lanes(at, domain)], out_send, out_recv, twin)

    def keep_copy(at):
        return pltpu.make_async_copy(results.at[0, at], o_ref.at[:, :, lanes(at, domain)], out_sem)

    for at in range(AHEAD):
        for which in range(3):
            load(at, which).start()
    request = pltpu.make_async_copy(req_hbm, req_ref, req_sem)
    request.start()
    barrier = pltpu.get_barrier_semaphore()
    for device in (twin, near):
        pl.semaphore_signal(barrier, inc=1, device_id={"view": device}, device_id_type=pl.DeviceIdType.MESH)

    @pl.when(is_mid)
    def _():
        pl.semaphore_signal(barrier, inc=1, device_id={"view": across}, device_id_type=pl.DeviceIdType.MESH)
        pl.semaphore_wait(barrier, 3)

    @pl.when(is_end)
    def _():
        pl.semaphore_wait(barrier, 2)

    for at in range(AHEAD):
        for which in range(2):
            swap(at, which).start()

    def fetch_keys(at):
        @pl.when(at + AHEAD < half)
        def _():
            for which in range(2):
                load(at + AHEAD, which).start()
                swap(at + AHEAD, which).start()

    @pl.when(is_end)
    def _():
        @pl.loop(0, half)
        def _(at):
            for which in range(2):
                load(at, which).wait()
                own_copy(at * PARTS + which * 2).start()
                swap(at, which).wait_recv()
                own_copy(at * PARTS + which * 2 + 1).start()
            fetch_keys(at)

    for at in range(AHEAD):
        swap(at, 2).start()

    request.wait()
    mine = req_ref[slot]
    end_same = (req_ref[end_slot] == mine).astype(jnp.int32)
    mid_same = (req_ref[mid_slot] == mine).astype(jnp.int32)
    far_same = jnp.maximum(
        (req_ref[3 - end_slot] == mine).astype(jnp.int32), (req_ref[3 - mid_slot] == mine).astype(jnp.int32)
    )
    near_same = jnp.minimum(end_same, mid_same)
    paired = jnp.maximum(near_same, far_same)

    query_row = lax.broadcasted_iota(jnp.int32, bias.shape, 0) % rows // COLS
    key_row = lax.broadcasted_iota(jnp.int32, bias.shape, 1) % rows // COLS
    bias[...] = jnp.where(paired > 0, jnp.where(query_row == key_row, 0.0, NEG_FILL), NEG_FILL)

    def pass_across(n):
        @pl.when(is_mid)
        def _():
            own_copy(n).wait_recv()
            at = pl.ds(n * span, span)
            crossing[at] = jnp.where(far_same > 0, kv[at], outer[at])
            cross_copy(n).start()

    def pass_out(n):
        cross_copy(n).wait_recv()

        @pl.when(is_mid)
        def _():
            at = pl.ds(n * span, span)
            ending[at] = jnp.where(near_same > 0, kv[at], inner[at])
            end_copy(n).start()

    scaling = size ** (-0.5) * LOG2E

    def scores_of(keys, asking):
        return (
            lax.dot_general(keys, asking, (((1,), (1,)), ((), ())), preferred_element_type=jnp.float32) * scaling
        )

    def weighted(raised, values):
        return lax.dot_general(
            values, raised.astype(jnp.bfloat16), (((0,), (0,)), ((), ())), preferred_element_type=jnp.float32
        )

    def own_part(at):
        fetched(at, 2)
        scores = scores_of(
            kv[pl.ds(at * 4, 2)].reshape(GROUPS * block, size),
            jnp.concatenate([queries[at, :, group].reshape(block, size) for group in range(GROUPS)], axis=0),
        )
        peak = jnp.max(scores, axis=0, keepdims=True)
        raised = jnp.exp2(scores - peak)
        peaks[at] = peak
        totals[at] = jnp.sum(raised, axis=0, keepdims=True)
        sums[at] = weighted(raised, kv[pl.ds(at * 4 + 2, 2)].reshape(GROUPS * block, size))

    def finish(at):
        @pl.when(is_mid)
        def _():
            chosen[...] = jnp.where(near_same > 0, outer[pl.ds(at * 4, 4)], inner[pl.ds(at * 4, 4)])

        @pl.when(is_end)
        def _():
            chosen[...] = inner[pl.ds(at * 4, 4)]

        for group in range(GROUPS):
            columns = slice(group * block, (group + 1) * block)
            scores = scores_of(
                chosen[0:2, group].reshape(block, size), queries[at, :, group].reshape(block, size)
            ) + bias[...]
            own_peak = peaks[at, :, columns]
            peak = jnp.maximum(own_peak, jnp.max(scores, axis=0, keepdims=True))
            raised = jnp.exp2(scores - peak)
            kept = jnp.exp2(own_peak - peak)
            total = totals[at, :, columns] * kept + jnp.sum(raised, axis=0, keepdims=True)
            summed = sums[at, :, columns] * kept + weighted(raised, chosen[2:4, group].reshape(block, size))
            attended = (summed / total).T.astype(jnp.bfloat16)
            results[:, at, group] = attended.reshape(2, rows, size)
        out_copy(at).start()
        keep_copy(at).start()

    def head(at, first):
        @pl.when(is_mid)
        def _():
            fetch_keys(at)
            for which in range(2):
                fetched(at, which)

        @pl.when(at + AHEAD < half)
        def _():
            load(at + AHEAD, 2).start()
            swap(at + AHEAD, 2).start()

        for part in range(PARTS):
            pass_across(at * PARTS + part)
            if part >= SKEW or not first:
                pass_out(at * PARTS + part - SKEW)
            if part == 1:
                own_part(at)
            if part == PARTS - 1 and not first:
                finish(at - 1)

    head(0, True)

    @pl.loop(1, half)
    def _(at):
        head(at, False)

    for late in range(SKEW):
        pass_out(half * PARTS - SKEW + late)
    finish(half - 1)

    whole = pl.ds(0, half * size)
    for which in range(3):
        side = sources[which].at[:, :, whole]
        remote(side, side, swap_send.at[which], out_recv, twin).wait_send()

    @pl.when(is_end)
    def _():
        remote(kv, outer, own_send, out_recv, near).wait_send()

    @pl.when(is_mid)
    def _():
        remote(crossing, inner, cross_send, out_recv, across).wait_send()
        remote(ending, inner, end_send, out_recv, near).wait_send()

    pltpu.make_async_copy(results.at[0], results.at[1], out_sem).wait()
    remote(results.at[1], results.at[1], out_send, out_recv, twin).wait()


def pair_shards(query_vectors, key_vectors, value_vectors, request_of_slot):
    rows = ROWS * COLS // GROUPS
    half = HEADS // 2
    flat = [tensor.reshape(GROUPS, rows, HEADS * HS) for tensor in (query_vectors, key_vectors, value_vectors)]
    vmem = pl.BlockSpec(memory_space=pltpu.VMEM)
    hbm = pl.BlockSpec(memory_space=pltpu.HBM)
    bank = pltpu.VMEM((half * 4, GROUPS, rows, HS), jnp.bfloat16)
    line = pltpu.VMEM((half, 1, GROUPS * 2 * rows), jnp.float32)
    one = pltpu.SemaphoreType.DMA
    three = pltpu.SemaphoreType.DMA((3, half))
    units = pltpu.SemaphoreType.DMA((half * PARTS,))
    scores = (2 * ROWS * COLS) ** 2 * half
    out = pl.pallas_call(
        pair_kernel,
        out_shape=jax.ShapeDtypeStruct((GROUPS, rows, HEADS * HS), jnp.bfloat16),
        in_specs=[hbm, hbm, hbm, hbm],
        out_specs=vmem,
        scratch_shapes=[
            pltpu.SMEM(request_of_slot.shape, jnp.int32),
            pltpu.VMEM((half, 2, GROUPS, rows, HS), jnp.bfloat16),
            bank, bank, bank, bank, bank,
            pltpu.VMEM((4, GROUPS, rows, HS), jnp.bfloat16),
            pltpu.VMEM((2 * rows, 2 * rows), jnp.float32),
            pltpu.VMEM((2, half, GROUPS, rows, HS), jnp.bfloat16),
            pltpu.VMEM((half, HS, GROUPS * 2 * rows), jnp.float32),
            line, line,
            one, three, pltpu.SemaphoreType.DMA((3,)), three, one, units, one, units, one, one, one, one,
        ],
        compiler_params=pltpu.CompilerParams(
            collective_id=0, has_side_effects=True, vmem_limit_bytes=VMEM_LIMIT
        ),
        cost_estimate=pl.CostEstimate(
            flops=6 * scores * HS, bytes_accessed=8 * ROWS * COLS * HEADS * HS, transcendentals=2 * scores
        ),
    )(request_of_slot, *flat)
    return out.reshape(1, ROWS, COLS, HEADS * HS)


def solution(mesh):
    slot_count = mesh.shape["view"] // 4
    shards = pair_shards if slot_count == 4 else general_shards
    return jax.shard_map(
        shards,
        mesh=mesh,
        in_specs=(
            P(("groups", "view"), None, None, None),
            P(("groups", "view"), None, None, None),
            P(("groups", "view"), None, None, None),
            P("groups"),
        ),
        out_specs=P(("groups", "view"), None, None, None),
        check_vma=False,
    )
```

```python
import jax
import jax.numpy as jnp
from jax import lax
from jax.experimental import pallas as pl
from jax.experimental.pallas import tpu as pltpu
from jax.sharding import PartitionSpec as P

HEADS = 32
HS = 128
ROWS = 16
COLS = 8
LOG2E = 1.4426950408889634
VMEM_LIMIT = 209 * 256 * 1024


NEG_FILL = -1e30


def partner(value, axis, distance):
    return lax.ppermute(value, axis, [(i, i ^ 1 << distance) for i in range(lax.axis_size(axis))])


def masked_softmax(scores, allowed):
    scores = jnp.where(allowed, scores, NEG_FILL)
    maximum = jnp.max(scores, axis=-1)
    raised = jnp.exp(scores - maximum[..., None])
    totals = jnp.sum(raised, axis=-1)
    return (maximum, totals, raised.astype(jnp.bfloat16))


def combine(first_part, second_part):
    highest = jnp.maximum(first_part[0], second_part[0])
    first_scale = jnp.exp(first_part[0] - highest)
    second_scale = jnp.exp(second_part[0] - highest)
    denominator = first_part[1] * first_scale + second_part[1] * second_scale
    numerator = first_part[2] * first_scale[..., None] + second_part[2] * second_scale[..., None]
    return (numerator / denominator[..., None]).astype(jnp.bfloat16)


def into_rows(tensor, row_blocks, head_groups):
    trailing = tensor.shape[3:]
    block_rows = tensor.shape[0] // row_blocks
    width_cols = tensor.shape[1]
    group_heads = tensor.shape[2] // head_groups
    shaped = tensor.reshape(
        (row_blocks, block_rows, width_cols, head_groups, group_heads) + trailing
    )
    permuted = (0, 3, 1, 2, 4) + tuple(range(5, 5 + len(trailing)))
    return shaped.transpose(permuted).reshape(
        (row_blocks * head_groups, block_rows, width_cols, group_heads) + trailing
    )


def into_tokens(tensor, row_blocks, head_groups):
    trailing = tensor.shape[4:]
    block_rows = tensor.shape[1]
    width_cols = tensor.shape[2]
    group_heads = tensor.shape[3]
    shaped = tensor.reshape(
        (row_blocks, head_groups, block_rows, width_cols, group_heads) + trailing
    )
    permuted = (0, 2, 3, 1, 4) + tuple(range(5, 5 + len(trailing)))
    return shaped.transpose(permuted).reshape(
        (row_blocks * block_rows * width_cols, head_groups * group_heads) + trailing
    )


def general_shards(query_vectors, key_vectors, value_vectors, request_of_slot):
    scaling = HS ** (-0.5)
    token_count = ROWS * COLS
    partner_key, partner_value = partner((key_vectors, value_vectors), "view", 0)
    head_blocks = 4
    block_heads = HEADS // head_blocks
    own_query = query_vectors.reshape(token_count, head_blocks, block_heads, HS)
    both_keys = jnp.concatenate(
        [
            key_vectors.reshape(token_count, head_blocks, block_heads, HS),
            partner_key.reshape(token_count, head_blocks, block_heads, HS),
        ],
        axis=0,
    )
    both_values = jnp.concatenate(
        [
            value_vectors.reshape(token_count, head_blocks, block_heads, HS),
            partner_value.reshape(token_count, head_blocks, block_heads, HS),
        ],
        axis=0,
    )
    query_row = jnp.arange(token_count) // COLS
    key_row = jnp.arange(2 * token_count) % token_count // COLS
    local_allowed = query_row[:, None] != key_row[None, :]

    def local_block(triple):
        block_scores = (
            jnp.einsum("nhx,khx->hnk", triple[0], triple[1], preferred_element_type=jnp.float32)
            * scaling
        )
        block_peak, block_total, block_weights = masked_softmax(block_scores, local_allowed[None])
        block_sum = jnp.einsum(
            "hnk,khx->nhx", block_weights, triple[2], preferred_element_type=jnp.float32
        )
        return (block_peak.T, block_total.T, block_sum)

    block_peaks, block_totals, block_sums = lax.map(
        local_block,
        (
            jnp.moveaxis(own_query, 1, 0),
            jnp.moveaxis(both_keys, 1, 0),
            jnp.moveaxis(both_values, 1, 0),
        ),
    )
    local_peak = jnp.moveaxis(block_peaks, 0, 1).reshape(token_count, HEADS)
    local_total = jnp.moveaxis(block_totals, 0, 1).reshape(token_count, HEADS)
    local_sum = jnp.moveaxis(block_sums, 0, 1).reshape(token_count, HEADS, HS)
    device_count = lax.axis_size("view")
    slot_count = device_count // 4
    pass_images = device_count // 2
    head_groups = 8
    row_blocks = device_count // head_groups
    block_rows = ROWS // row_blocks
    slot_request = jnp.broadcast_to(
        request_of_slot[:, None], (request_of_slot.shape[0], 2 * COLS)
    ).reshape(-1)
    row_allowed = slot_request[:, None] == slot_request[None, :]

    def arrange(tensor):
        shaped = tensor.reshape(slot_count, 2, 2, block_rows, COLS, HS).transpose(1, 3, 0, 2, 4, 5)
        return shaped.reshape(2 * block_rows, pass_images * COLS, HS)

    def restore(tensor):
        trailing = tensor.shape[2:]
        shaped = tensor.reshape((2, block_rows, slot_count, 2, COLS) + trailing)
        permuted = (2, 0, 3, 1, 4) + tuple(range(5, 5 + len(trailing)))
        return shaped.transpose(permuted).reshape((device_count, block_rows, COLS) + trailing)

    def one_head(triple):
        row_scores = (
            jnp.einsum(
                "bnx,bkx->bnk",
                arrange(triple[0]),
                arrange(triple[1]),
                preferred_element_type=jnp.float32,
            )
            * scaling
        )
        row_peak, row_total, row_weights = masked_softmax(row_scores, row_allowed[None])
        row_sum = jnp.einsum(
            "bnk,bkx->bnx", row_weights, arrange(triple[2]), preferred_element_type=jnp.float32
        )
        return (restore(row_peak), restore(row_total), restore(row_sum))

    query_rows = into_rows(query_vectors.reshape(ROWS, COLS, HEADS, HS), row_blocks, head_groups)
    key_rows = into_rows(key_vectors.reshape(ROWS, COLS, HEADS, HS), row_blocks, head_groups)
    value_rows = into_rows(value_vectors.reshape(ROWS, COLS, HEADS, HS), row_blocks, head_groups)
    by_head = (
        jnp.moveaxis(
            lax.all_to_all(query_rows, "view", split_axis=0, concat_axis=0, tiled=True), 3, 0
        ),
        jnp.moveaxis(
            lax.all_to_all(key_rows, "view", split_axis=0, concat_axis=0, tiled=True), 3, 0
        ),
        jnp.moveaxis(
            lax.all_to_all(value_rows, "view", split_axis=0, concat_axis=0, tiled=True), 3, 0
        ),
    )
    row_peaks, row_totals, row_sums = lax.map(one_head, by_head)
    peak_part = jnp.moveaxis(row_peaks, 0, 3)
    total_part = jnp.moveaxis(row_totals, 0, 3)
    sum_part = jnp.moveaxis(row_sums, 0, 3)
    row_peak = lax.all_to_all(peak_part, "view", split_axis=0, concat_axis=0, tiled=True)
    row_total = lax.all_to_all(total_part, "view", split_axis=0, concat_axis=0, tiled=True)
    row_sum = lax.all_to_all(sum_part, "view", split_axis=0, concat_axis=0, tiled=True)
    row_peak = into_tokens(row_peak, row_blocks, head_groups)
    row_total = into_tokens(row_total, row_blocks, head_groups)
    row_sum = into_tokens(row_sum, row_blocks, head_groups)
    attended = combine((local_peak, local_total, local_sum), (row_peak, row_total, row_sum))
    return attended.reshape(1, ROWS, COLS, HEADS * HS)


PARTS = 4
SKEW = 7
LAG = 2
GROUPS = 2
AHEAD = 2


def pair_kernel(
    req_hbm, q_ref, k_ref, v_ref, o_ref,
    req_ref, queries, kv, outer, inner, crossing, ending, chosen, bias, results, sums, peaks, totals,
    req_sem, load_sem, swap_send, swap_recv, own_send, outer_recv, cross_send, inner_recv, end_send, out_send, out_recv, out_sem,
):
    half, _, _, rows, size = queries.shape
    block = 2 * rows
    span = 4 // PARTS
    me = lax.axis_index("view")
    domain = me % 2
    slot = me // 4
    other = 1 - domain
    twin = me + other - domain
    upper = slot // 2
    end_slot = 3 * upper
    mid_slot = 1 + upper
    is_end = slot == end_slot
    is_mid = slot == mid_slot
    near = me + 4 * (end_slot + mid_slot - 2 * slot)
    across = me + 4 * (3 - 2 * slot)

    def remote(src, dst, send, recv, device):
        return pltpu.make_async_remote_copy(
            src_ref=src, dst_ref=dst, send_sem=send, recv_sem=recv,
            device_id={"view": device}, device_id_type=pl.DeviceIdType.MESH,
        )

    def lanes(at, group):
        return pl.ds(pl.multiple_of((group * half + at) * size, size), size)

    def unit(ref, number):
        return ref.at[pl.ds(number * span, span)]

    def place(at, which, whose):
        return queries.at[at, whose] if which == 2 else kv.at[at * 4 + which * 2 + whose]

    sources = (k_ref, v_ref, q_ref)

    def load(at, which):
        return pltpu.make_async_copy(
            sources[which].at[:, :, lanes(at, domain)], place(at, which, 0), load_sem.at[which, at]
        )

    def swap(at, which):
        return remote(
            sources[which].at[:, :, lanes(at, other)], place(at, which, 1),
            swap_send.at[which], swap_recv.at[which, at], twin,
        )

    def fetched(at, which):
        load(at, which).wait()
        swap(at, which).wait_recv()

    def own_copy(n):
        return remote(unit(kv, n), unit(outer, n), own_send, outer_recv.at[n], near)

    def cross_copy(n):
        return remote(unit(crossing, n), unit(inner, n), cross_send, inner_recv.at[n], across)

    def end_copy(n):
        return remote(unit(ending, n), unit(inner, n), end_send, inner_recv.at[n], near)

    def out_copy(at):
        return remote(results.at[1, at], o_ref.at[:, :, lanes(at, domain)], out_send, out_recv, twin)

    def keep_copy(at):
        return pltpu.make_async_copy(results.at[0, at], o_ref.at[:, :, lanes(at, domain)], out_sem)

    for at in range(AHEAD):
        for which in range(3):
            load(at, which).start()
    request = pltpu.make_async_copy(req_hbm, req_ref, req_sem)
    request.start()
    barrier = pltpu.get_barrier_semaphore()
    for device in (twin, near):
        pl.semaphore_signal(barrier, inc=1, device_id={"view": device}, device_id_type=pl.DeviceIdType.MESH)

    @pl.when(is_mid)
    def _():
        pl.semaphore_signal(barrier, inc=1, device_id={"view": across}, device_id_type=pl.DeviceIdType.MESH)
        pl.semaphore_wait(barrier, 3)

    @pl.when(is_end)
    def _():
        pl.semaphore_wait(barrier, 2)

    for at in range(AHEAD):
        for which in range(2):
            swap(at, which).start()

    def fetch_keys(at):
        @pl.when(at + AHEAD < half)
        def _():
            for which in range(2):
                load(at + AHEAD, which).start()
                swap(at + AHEAD, which).start()

    @pl.when(is_end)
    def _():
        @pl.loop(0, half)
        def _(at):
            for which in range(2):
                load(at, which).wait()
                own_copy(at * PARTS + which * 2).start()
                swap(at, which).wait_recv()
                own_copy(at * PARTS + which * 2 + 1).start()
            fetch_keys(at)

    for at in range(AHEAD):
        swap(at, 2).start()

    request.wait()
    mine = req_ref[slot]
    end_same = (req_ref[end_slot] == mine).astype(jnp.int32)
    mid_same = (req_ref[mid_slot] == mine).astype(jnp.int32)
    far_same = jnp.maximum(
        (req_ref[3 - end_slot] == mine).astype(jnp.int32), (req_ref[3 - mid_slot] == mine).astype(jnp.int32)
    )
    near_same = jnp.minimum(end_same, mid_same)
    paired = jnp.maximum(near_same, far_same)

    query_row = lax.broadcasted_iota(jnp.int32, bias.shape, 0) % rows // COLS
    key_row = lax.broadcasted_iota(jnp.int32, bias.shape, 1) % rows // COLS
    bias[...] = jnp.where(paired > 0, jnp.where(query_row == key_row, 0.0, NEG_FILL), NEG_FILL)

    def pass_across(n):
        @pl.when(is_mid)
        def _():
            own_copy(n).wait_recv()
            at = pl.ds(n * span, span)
            crossing[at] = jnp.where(far_same > 0, kv[at], outer[at])
            cross_copy(n).start()

    def pass_out(n):
        cross_copy(n).wait_recv()

        @pl.when(is_mid)
        def _():
            at = pl.ds(n * span, span)
            ending[at] = jnp.where(near_same > 0, kv[at], inner[at])
            end_copy(n).start()

    scaling = size ** (-0.5) * LOG2E

    def scores_of(keys, asking):
        return (
            lax.dot_general(keys, asking, (((1,), (1,)), ((), ())), preferred_element_type=jnp.float32) * scaling
        )

    def weighted(raised, values):
        return lax.dot_general(
            values, raised.astype(jnp.bfloat16), (((0,), (0,)), ((), ())), preferred_element_type=jnp.float32
        )

    def own_part(at):
        fetched(at, 2)
        scores = scores_of(
            kv[pl.ds(at * 4, 2)].reshape(GROUPS * block, size),
            jnp.concatenate([queries[at, :, group].reshape(block, size) for group in range(GROUPS)], axis=0),
        )
        peak = jnp.max(scores, axis=0, keepdims=True)
        raised = jnp.exp2(scores - peak)
        peaks[at] = peak
        totals[at] = jnp.sum(raised, axis=0, keepdims=True)
        sums[at] = weighted(raised, kv[pl.ds(at * 4 + 2, 2)].reshape(GROUPS * block, size))

    def finish(at):
        @pl.when(is_mid)
        def _():
            chosen[...] = jnp.where(near_same > 0, outer[pl.ds(at * 4, 4)], inner[pl.ds(at * 4, 4)])

        @pl.when(is_end)
        def _():
            chosen[...] = inner[pl.ds(at * 4, 4)]

        for group in range(GROUPS):
            columns = slice(group * block, (group + 1) * block)
            scores = scores_of(
                chosen[0:2, group].reshape(block, size), queries[at, :, group].reshape(block, size)
            ) + bias[...]
            own_peak = peaks[at, :, columns]
            peak = jnp.maximum(own_peak, jnp.max(scores, axis=0, keepdims=True))
            raised = jnp.exp2(scores - peak)
            kept = jnp.exp2(own_peak - peak)
            total = totals[at, :, columns] * kept + jnp.sum(raised, axis=0, keepdims=True)
            summed = sums[at, :, columns] * kept + weighted(raised, chosen[2:4, group].reshape(block, size))
            attended = (summed / total).T.astype(jnp.bfloat16)
            results[:, at, group] = attended.reshape(2, rows, size)
        out_copy(at).start()
        keep_copy(at).start()

    def head(at, first):
        @pl.when(is_mid)
        def _():
            fetch_keys(at)
            for which in range(2):
                fetched(at, which)

        @pl.when(at + AHEAD < half)
        def _():
            load(at + AHEAD, 2).start()
            swap(at + AHEAD, 2).start()

        for part in range(PARTS):
            pass_across(at * PARTS + part)
            if not first or at * PARTS + part >= SKEW:
                pass_out(at * PARTS + part - SKEW)
            if part == 1:
                own_part(at)
            if part == PARTS - 1 and not first:
                finish(at - LAG)

    for at in range(LAG):
        head(at, True)

    @pl.loop(LAG, half)
    def _(at):
        head(at, False)

    for late in range(SKEW):
        number = half * PARTS - SKEW + late
        pass_out(number)
        if (number + 1) % PARTS == 0:
            finish(number // PARTS)

    whole = pl.ds(0, half * size)
    for which in range(3):
        side = sources[which].at[:, :, whole]
        remote(side, side, swap_send.at[which], out_recv, twin).wait_send()

    @pl.when(is_end)
    def _():
        remote(kv, outer, own_send, out_recv, near).wait_send()

    @pl.when(is_mid)
    def _():
        remote(crossing, inner, cross_send, out_recv, across).wait_send()
        remote(ending, inner, end_send, out_recv, near).wait_send()

    pltpu.make_async_copy(results.at[0], results.at[1], out_sem).wait()
    remote(results.at[1], results.at[1], out_send, out_recv, twin).wait()


def pair_shards(query_vectors, key_vectors, value_vectors, request_of_slot):
    rows = ROWS * COLS // GROUPS
    half = HEADS // 2
    flat = [tensor.reshape(GROUPS, rows, HEADS * HS) for tensor in (query_vectors, key_vectors, value_vectors)]
    vmem = pl.BlockSpec(memory_space=pltpu.VMEM)
    hbm = pl.BlockSpec(memory_space=pltpu.HBM)
    bank = pltpu.VMEM((half * 4, GROUPS, rows, HS), jnp.bfloat16)
    line = pltpu.VMEM((half, 1, GROUPS * 2 * rows), jnp.float32)
    one = pltpu.SemaphoreType.DMA
    three = pltpu.SemaphoreType.DMA((3, half))
    units = pltpu.SemaphoreType.DMA((half * PARTS,))
    scores = (2 * ROWS * COLS) ** 2 * half
    out = pl.pallas_call(
        pair_kernel,
        out_shape=jax.ShapeDtypeStruct((GROUPS, rows, HEADS * HS), jnp.bfloat16),
        in_specs=[hbm, hbm, hbm, hbm],
        out_specs=vmem,
        scratch_shapes=[
            pltpu.SMEM(request_of_slot.shape, jnp.int32),
            pltpu.VMEM((half, 2, GROUPS, rows, HS), jnp.bfloat16),
            bank, bank, bank, bank, bank,
            pltpu.VMEM((4, GROUPS, rows, HS), jnp.bfloat16),
            pltpu.VMEM((2 * rows, 2 * rows), jnp.float32),
            pltpu.VMEM((2, half, GROUPS, rows, HS), jnp.bfloat16),
            pltpu.VMEM((half, HS, GROUPS * 2 * rows), jnp.float32),
            line, line,
            one, three, pltpu.SemaphoreType.DMA((3,)), three, one, units, one, units, one, one, one, one,
        ],
        compiler_params=pltpu.CompilerParams(
            collective_id=0, has_side_effects=True, vmem_limit_bytes=VMEM_LIMIT
        ),
        cost_estimate=pl.CostEstimate(
            flops=6 * scores * HS, bytes_accessed=8 * ROWS * COLS * HEADS * HS, transcendentals=2 * scores
        ),
    )(request_of_slot, *flat)
    return out.reshape(1, ROWS, COLS, HEADS * HS)


def solution(mesh):
    slot_count = mesh.shape["view"] // 4
    shards = pair_shards if slot_count == 4 else general_shards
    return jax.shard_map(
        shards,
        mesh=mesh,
        in_specs=(
            P(("groups", "view"), None, None, None),
            P(("groups", "view"), None, None, None),
            P(("groups", "view"), None, None, None),
            P("groups"),
        ),
        out_specs=P(("groups", "view"), None, None, None),
        check_vma=False,
    )
```

```python
import jax
import jax.numpy as jnp
from jax import lax
from jax.experimental import pallas as pl
from jax.experimental.pallas import tpu as pltpu
from jax.sharding import PartitionSpec as P

HEADS = 32
HS = 128
ROWS = 16
COLS = 8
LOG2E = 1.4426950408889634
VMEM_LIMIT = 209 * 256 * 1024


NEG_FILL = -1e30


def partner(value, axis, distance):
    return lax.ppermute(value, axis, [(i, i ^ 1 << distance) for i in range(lax.axis_size(axis))])


def masked_softmax(scores, allowed):
    scores = jnp.where(allowed, scores, NEG_FILL)
    maximum = jnp.max(scores, axis=-1)
    raised = jnp.exp(scores - maximum[..., None])
    totals = jnp.sum(raised, axis=-1)
    return (maximum, totals, raised.astype(jnp.bfloat16))


def combine(first_part, second_part):
    highest = jnp.maximum(first_part[0], second_part[0])
    first_scale = jnp.exp(first_part[0] - highest)
    second_scale = jnp.exp(second_part[0] - highest)
    denominator = first_part[1] * first_scale + second_part[1] * second_scale
    numerator = first_part[2] * first_scale[..., None] + second_part[2] * second_scale[..., None]
    return (numerator / denominator[..., None]).astype(jnp.bfloat16)


def into_rows(tensor, row_blocks, head_groups):
    trailing = tensor.shape[3:]
    block_rows = tensor.shape[0] // row_blocks
    width_cols = tensor.shape[1]
    group_heads = tensor.shape[2] // head_groups
    shaped = tensor.reshape(
        (row_blocks, block_rows, width_cols, head_groups, group_heads) + trailing
    )
    permuted = (0, 3, 1, 2, 4) + tuple(range(5, 5 + len(trailing)))
    return shaped.transpose(permuted).reshape(
        (row_blocks * head_groups, block_rows, width_cols, group_heads) + trailing
    )


def into_tokens(tensor, row_blocks, head_groups):
    trailing = tensor.shape[4:]
    block_rows = tensor.shape[1]
    width_cols = tensor.shape[2]
    group_heads = tensor.shape[3]
    shaped = tensor.reshape(
        (row_blocks, head_groups, block_rows, width_cols, group_heads) + trailing
    )
    permuted = (0, 2, 3, 1, 4) + tuple(range(5, 5 + len(trailing)))
    return shaped.transpose(permuted).reshape(
        (row_blocks * block_rows * width_cols, head_groups * group_heads) + trailing
    )


def general_shards(query_vectors, key_vectors, value_vectors, request_of_slot):
    scaling = HS ** (-0.5)
    token_count = ROWS * COLS
    partner_key, partner_value = partner((key_vectors, value_vectors), "view", 0)
    head_blocks = 4
    block_heads = HEADS // head_blocks
    own_query = query_vectors.reshape(token_count, head_blocks, block_heads, HS)
    both_keys = jnp.concatenate(
        [
            key_vectors.reshape(token_count, head_blocks, block_heads, HS),
            partner_key.reshape(token_count, head_blocks, block_heads, HS),
        ],
        axis=0,
    )
    both_values = jnp.concatenate(
        [
            value_vectors.reshape(token_count, head_blocks, block_heads, HS),
            partner_value.reshape(token_count, head_blocks, block_heads, HS),
        ],
        axis=0,
    )
    query_row = jnp.arange(token_count) // COLS
    key_row = jnp.arange(2 * token_count) % token_count // COLS
    local_allowed = query_row[:, None] != key_row[None, :]

    def local_block(triple):
        block_scores = (
            jnp.einsum("nhx,khx->hnk", triple[0], triple[1], preferred_element_type=jnp.float32)
            * scaling
        )
        block_peak, block_total, block_weights = masked_softmax(block_scores, local_allowed[None])
        block_sum = jnp.einsum(
            "hnk,khx->nhx", block_weights, triple[2], preferred_element_type=jnp.float32
        )
        return (block_peak.T, block_total.T, block_sum)

    block_peaks, block_totals, block_sums = lax.map(
        local_block,
        (
            jnp.moveaxis(own_query, 1, 0),
            jnp.moveaxis(both_keys, 1, 0),
            jnp.moveaxis(both_values, 1, 0),
        ),
    )
    local_peak = jnp.moveaxis(block_peaks, 0, 1).reshape(token_count, HEADS)
    local_total = jnp.moveaxis(block_totals, 0, 1).reshape(token_count, HEADS)
    local_sum = jnp.moveaxis(block_sums, 0, 1).reshape(token_count, HEADS, HS)
    device_count = lax.axis_size("view")
    slot_count = device_count // 4
    pass_images = device_count // 2
    head_groups = 8
    row_blocks = device_count // head_groups
    block_rows = ROWS // row_blocks
    slot_request = jnp.broadcast_to(
        request_of_slot[:, None], (request_of_slot.shape[0], 2 * COLS)
    ).reshape(-1)
    row_allowed = slot_request[:, None] == slot_request[None, :]

    def arrange(tensor):
        shaped = tensor.reshape(slot_count, 2, 2, block_rows, COLS, HS).transpose(1, 3, 0, 2, 4, 5)
        return shaped.reshape(2 * block_rows, pass_images * COLS, HS)

    def restore(tensor):
        trailing = tensor.shape[2:]
        shaped = tensor.reshape((2, block_rows, slot_count, 2, COLS) + trailing)
        permuted = (2, 0, 3, 1, 4) + tuple(range(5, 5 + len(trailing)))
        return shaped.transpose(permuted).reshape((device_count, block_rows, COLS) + trailing)

    def one_head(triple):
        row_scores = (
            jnp.einsum(
                "bnx,bkx->bnk",
                arrange(triple[0]),
                arrange(triple[1]),
                preferred_element_type=jnp.float32,
            )
            * scaling
        )
        row_peak, row_total, row_weights = masked_softmax(row_scores, row_allowed[None])
        row_sum = jnp.einsum(
            "bnk,bkx->bnx", row_weights, arrange(triple[2]), preferred_element_type=jnp.float32
        )
        return (restore(row_peak), restore(row_total), restore(row_sum))

    query_rows = into_rows(query_vectors.reshape(ROWS, COLS, HEADS, HS), row_blocks, head_groups)
    key_rows = into_rows(key_vectors.reshape(ROWS, COLS, HEADS, HS), row_blocks, head_groups)
    value_rows = into_rows(value_vectors.reshape(ROWS, COLS, HEADS, HS), row_blocks, head_groups)
    by_head = (
        jnp.moveaxis(
            lax.all_to_all(query_rows, "view", split_axis=0, concat_axis=0, tiled=True), 3, 0
        ),
        jnp.moveaxis(
            lax.all_to_all(key_rows, "view", split_axis=0, concat_axis=0, tiled=True), 3, 0
        ),
        jnp.moveaxis(
            lax.all_to_all(value_rows, "view", split_axis=0, concat_axis=0, tiled=True), 3, 0
        ),
    )
    row_peaks, row_totals, row_sums = lax.map(one_head, by_head)
    peak_part = jnp.moveaxis(row_peaks, 0, 3)
    total_part = jnp.moveaxis(row_totals, 0, 3)
    sum_part = jnp.moveaxis(row_sums, 0, 3)
    row_peak = lax.all_to_all(peak_part, "view", split_axis=0, concat_axis=0, tiled=True)
    row_total = lax.all_to_all(total_part, "view", split_axis=0, concat_axis=0, tiled=True)
    row_sum = lax.all_to_all(sum_part, "view", split_axis=0, concat_axis=0, tiled=True)
    row_peak = into_tokens(row_peak, row_blocks, head_groups)
    row_total = into_tokens(row_total, row_blocks, head_groups)
    row_sum = into_tokens(row_sum, row_blocks, head_groups)
    attended = combine((local_peak, local_total, local_sum), (row_peak, row_total, row_sum))
    return attended.reshape(1, ROWS, COLS, HEADS * HS)


PARTS = 4
SKEW = 5
CHUNK = 4
LAG = 2
GROUPS = 2


def pair_kernel(
    req_hbm, q_ref, k_ref, v_ref, o_ref,
    req_ref, queries, kv, outer, inner, crossing, ending, chosen, bias, results, sums, peaks, totals,
    req_sem, load_sem, swap_send, swap_recv, own_send, outer_recv, cross_send, inner_recv, end_send, out_send, out_recv, out_sem,
):
    half, size, _ = sums.shape
    rows = queries.shape[2]
    block = 2 * rows
    chunks = half // CHUNK
    me = lax.axis_index("view")
    domain = me % 2
    slot = me // 4
    other = 1 - domain
    twin = me + other - domain
    upper = slot // 2
    end_slot = 3 * upper
    mid_slot = 1 + upper
    is_end = slot == end_slot
    is_mid = slot == mid_slot
    near = me + 4 * (end_slot + mid_slot - 2 * slot)
    across = me + 4 * (3 - 2 * slot)

    def remote(src, dst, send, recv, device):
        return pltpu.make_async_remote_copy(
            src_ref=src, dst_ref=dst, send_sem=send, recv_sem=recv,
            device_id={"view": device}, device_id_type=pl.DeviceIdType.MESH,
        )

    def lanes(at, group):
        return pl.ds(pl.multiple_of((group * half + at) * size, size), size)

    sources = (k_ref, v_ref, q_ref)

    def wide(chunk, group):
        return pl.ds(pl.multiple_of((group * half + chunk * CHUNK) * size, CHUNK * size), CHUNK * size)

    def place(chunk, which, whose):
        columns = wide(chunk, 0)
        return queries.at[whose, :, :, columns] if which == 2 else kv.at[which, whose, :, :, columns]

    def load(chunk, which):
        return pltpu.make_async_copy(
            sources[which].at[:, :, wide(chunk, domain)], place(chunk, which, 0), load_sem.at[which, chunk]
        )

    def swap(chunk, which):
        return remote(
            sources[which].at[:, :, wide(chunk, other)], place(chunk, which, 1),
            swap_send.at[which], swap_recv.at[which, chunk], twin,
        )

    def own_copy(at, part):
        n = at * PARTS + part
        return remote(
            kv.at[part // 2, part % 2, :, :, lanes(at, 0)], outer.at[n], own_send, outer_recv.at[n], near
        )

    def cross_copy(n):
        return remote(crossing.at[n], inner.at[n], cross_send, inner_recv.at[n], across)

    def end_copy(n):
        return remote(ending.at[n], inner.at[n], end_send, inner_recv.at[n], near)

    def out_copy(at):
        return remote(results.at[1, at], o_ref.at[:, :, lanes(at, domain)], out_send, out_recv, twin)

    def keep_copy(at):
        return pltpu.make_async_copy(results.at[0, at], o_ref.at[:, :, lanes(at, domain)], out_sem)

    request = pltpu.make_async_copy(req_hbm, req_ref, req_sem)
    request.start()
    barrier = pltpu.get_barrier_semaphore()
    for device in (twin, near):
        pl.semaphore_signal(barrier, inc=1, device_id={"view": device}, device_id_type=pl.DeviceIdType.MESH)

    @pl.when(is_mid)
    def _():
        pl.semaphore_signal(barrier, inc=1, device_id={"view": across}, device_id_type=pl.DeviceIdType.MESH)

    for chunk in range(chunks):
        for which in range(3):
            load(chunk, which).start()

    @pl.when(is_mid)
    def _():
        pl.semaphore_wait(barrier, 3)

    @pl.when(is_end)
    def _():
        pl.semaphore_wait(barrier, 2)

    for chunk in range(chunks):
        for which in range(3):
            swap(chunk, which).start()

    def fetched(at, which):
        @pl.when(at % CHUNK == 0)
        def _():
            load(at // CHUNK, which).wait()
            swap(at // CHUNK, which).wait_recv()

    @pl.when(is_end)
    def _():
        @pl.loop(0, half)
        def _(at):
            for which in range(2):
                fetched(at, which)
                for whose in range(2):
                    own_copy(at, which * 2 + whose).start()

    request.wait()
    mine = req_ref[slot]
    end_same = (req_ref[end_slot] == mine).astype(jnp.int32)
    mid_same = (req_ref[mid_slot] == mine).astype(jnp.int32)
    far_same = jnp.maximum(
        (req_ref[3 - end_slot] == mine).astype(jnp.int32), (req_ref[3 - mid_slot] == mine).astype(jnp.int32)
    )
    near_same = jnp.minimum(end_same, mid_same)
    paired = jnp.maximum(near_same, far_same)

    query_row = lax.broadcasted_iota(jnp.int32, bias.shape, 0) % rows // COLS
    key_row = lax.broadcasted_iota(jnp.int32, bias.shape, 1) % rows // COLS
    bias[...] = jnp.where(paired > 0, jnp.where(query_row == key_row, 0.0, NEG_FILL), NEG_FILL)

    def own_unit(at, part):
        return kv[part // 2, part % 2, :, :, lanes(at, 0)]

    def pass_across(at, part):
        @pl.when(is_mid)
        def _():
            n = at * PARTS + part
            own_copy(at, part).wait_recv()
            crossing[n] = jnp.where(far_same > 0, own_unit(at, part), outer[n])
            cross_copy(n).start()

    def pass_out(at, part):
        n = at * PARTS + part
        cross_copy(n).wait_recv()

        @pl.when(is_mid)
        def _():
            ending[n] = jnp.where(near_same > 0, own_unit(at, part), inner[n])
            end_copy(n).start()

    scaling = size ** (-0.5) * LOG2E

    def scores_of(keys, asking):
        return (
            lax.dot_general(keys, asking, (((1,), (1,)), ((), ())), preferred_element_type=jnp.float32) * scaling
        )

    def weighted(raised, values):
        return lax.dot_general(
            values, raised.astype(jnp.bfloat16), (((0,), (0,)), ((), ())), preferred_element_type=jnp.float32
        )

    def own_part(at):
        asking = queries[:, :, :, lanes(at, 0)]
        scores = scores_of(
            kv[0, :, :, :, lanes(at, 0)].reshape(GROUPS * block, size),
            jnp.concatenate([asking[:, group].reshape(block, size) for group in range(GROUPS)], axis=0),
        )
        peak = jnp.max(scores, axis=0, keepdims=True)
        raised = jnp.exp2(scores - peak)
        peaks[at] = peak
        totals[at] = jnp.sum(raised, axis=0, keepdims=True)
        sums[at] = weighted(raised, kv[1, :, :, :, lanes(at, 0)].reshape(GROUPS * block, size))

    def finish(at):
        @pl.when(is_mid)
        def _():
            chosen[...] = jnp.where(near_same > 0, outer[pl.ds(at * 4, 4)], inner[pl.ds(at * 4, 4)])

        @pl.when(is_end)
        def _():
            chosen[...] = inner[pl.ds(at * 4, 4)]

        for group in range(GROUPS):
            columns = slice(group * block, (group + 1) * block)
            scores = scores_of(
                chosen[0:2, group].reshape(block, size), queries[:, group, :, lanes(at, 0)].reshape(block, size)
            ) + bias[...]
            own_peak = peaks[at, :, columns]
            peak = jnp.maximum(own_peak, jnp.max(scores, axis=0, keepdims=True))
            raised = jnp.exp2(scores - peak)
            kept = jnp.exp2(own_peak - peak)
            total = totals[at, :, columns] * kept + jnp.sum(raised, axis=0, keepdims=True)
            summed = sums[at, :, columns] * kept + weighted(raised, chosen[2:4, group].reshape(block, size))
            attended = (summed / total).T.astype(jnp.bfloat16)
            results[:, at, group] = attended.reshape(2, rows, size)
        out_copy(at).start()
        keep_copy(at).start()

    def head(at, first):
        @pl.when(is_mid)
        def _():
            for which in range(2):
                fetched(at, which)

        fetched(at, 2)
        for part in range(PARTS):
            pass_across(at, part)
            behind = part - SKEW
            if not first or at * PARTS + behind >= 0:
                pass_out(at + behind // PARTS, behind % PARTS)
            if part == 1:
                own_part(at)
            if part == PARTS - 1 and not first:
                finish(at - LAG)

    for at in range(LAG):
        head(at, True)

    @pl.loop(LAG, half)
    def _(at):
        head(at, False)

    for number in range(half * PARTS - SKEW, half * PARTS):
        pass_out(number // PARTS, number % PARTS)
        if number % PARTS == PARTS - 1:
            finish(number // PARTS)

    whole = pl.ds(0, half * size)
    for which in range(3):
        side = sources[which].at[:, :, whole]
        remote(side, side, swap_send.at[which], out_recv, twin).wait_send()

    @pl.when(is_end)
    def _():
        remote(outer, outer, own_send, out_recv, near).wait_send()

    @pl.when(is_mid)
    def _():
        remote(crossing, inner, cross_send, out_recv, across).wait_send()
        remote(ending, inner, end_send, out_recv, near).wait_send()

    pltpu.make_async_copy(results.at[0], results.at[1], out_sem).wait()
    remote(results.at[1], results.at[1], out_send, out_recv, twin).wait()


def pair_shards(query_vectors, key_vectors, value_vectors, request_of_slot):
    rows = ROWS * COLS // GROUPS
    half = HEADS // 2
    flat = [tensor.reshape(GROUPS, rows, HEADS * HS) for tensor in (query_vectors, key_vectors, value_vectors)]
    vmem = pl.BlockSpec(memory_space=pltpu.VMEM)
    hbm = pl.BlockSpec(memory_space=pltpu.HBM)
    bank = pltpu.VMEM((half * 4, GROUPS, rows, HS), jnp.bfloat16)
    line = pltpu.VMEM((half, 1, GROUPS * 2 * rows), jnp.float32)
    one = pltpu.SemaphoreType.DMA
    three = pltpu.SemaphoreType.DMA((3, half // CHUNK))
    units = pltpu.SemaphoreType.DMA((half * PARTS,))
    scores = (2 * ROWS * COLS) ** 2 * half
    out = pl.pallas_call(
        pair_kernel,
        out_shape=jax.ShapeDtypeStruct((GROUPS, rows, HEADS * HS), jnp.bfloat16),
        in_specs=[hbm, hbm, hbm, hbm],
        out_specs=vmem,
        scratch_shapes=[
            pltpu.SMEM(request_of_slot.shape, jnp.int32),
            pltpu.VMEM((2, GROUPS, rows, half * HS), jnp.bfloat16),
            pltpu.VMEM((2, 2, GROUPS, rows, half * HS), jnp.bfloat16),
            bank, bank, bank, bank,
            pltpu.VMEM((4, GROUPS, rows, HS), jnp.bfloat16),
            pltpu.VMEM((2 * rows, 2 * rows), jnp.float32),
            pltpu.VMEM((2, half, GROUPS, rows, HS), jnp.bfloat16),
            pltpu.VMEM((half, HS, GROUPS * 2 * rows), jnp.float32),
            line, line,
            one, three, pltpu.SemaphoreType.DMA((3,)), three, one, units, one, units, one, one, one, one,
        ],
        compiler_params=pltpu.CompilerParams(
            collective_id=0, has_side_effects=True, vmem_limit_bytes=VMEM_LIMIT
        ),
        cost_estimate=pl.CostEstimate(
            flops=6 * scores * HS, bytes_accessed=8 * ROWS * COLS * HEADS * HS, transcendentals=2 * scores
        ),
    )(request_of_slot, *flat)
    return out.reshape(1, ROWS, COLS, HEADS * HS)


def solution(mesh):
    slot_count = mesh.shape["view"] // 4
    shards = pair_shards if slot_count == 4 else general_shards
    return jax.shard_map(
        shards,
        mesh=mesh,
        in_specs=(
            P(("groups", "view"), None, None, None),
            P(("groups", "view"), None, None, None),
            P(("groups", "view"), None, None, None),
            P("groups"),
        ),
        out_specs=P(("groups", "view"), None, None, None),
        check_vma=False,
    )
```

```python
import jax
import jax.numpy as jnp
from jax import lax
from jax.experimental import pallas as pl
from jax.experimental.pallas import tpu as pltpu
from jax.sharding import PartitionSpec as P

HEADS = 32
HS = 128
ROWS = 16
COLS = 8
LOG2E = 1.4426950408889634
VMEM_LIMIT = 209 * 256 * 1024


NEG_FILL = -1e30


def partner(value, axis, distance):
    return lax.ppermute(value, axis, [(i, i ^ 1 << distance) for i in range(lax.axis_size(axis))])


def masked_softmax(scores, allowed):
    scores = jnp.where(allowed, scores, NEG_FILL)
    maximum = jnp.max(scores, axis=-1)
    raised = jnp.exp(scores - maximum[..., None])
    totals = jnp.sum(raised, axis=-1)
    return (maximum, totals, raised.astype(jnp.bfloat16))


def combine(first_part, second_part):
    highest = jnp.maximum(first_part[0], second_part[0])
    first_scale = jnp.exp(first_part[0] - highest)
    second_scale = jnp.exp(second_part[0] - highest)
    denominator = first_part[1] * first_scale + second_part[1] * second_scale
    numerator = first_part[2] * first_scale[..., None] + second_part[2] * second_scale[..., None]
    return (numerator / denominator[..., None]).astype(jnp.bfloat16)


def into_rows(tensor, row_blocks, head_groups):
    trailing = tensor.shape[3:]
    block_rows = tensor.shape[0] // row_blocks
    width_cols = tensor.shape[1]
    group_heads = tensor.shape[2] // head_groups
    shaped = tensor.reshape(
        (row_blocks, block_rows, width_cols, head_groups, group_heads) + trailing
    )
    permuted = (0, 3, 1, 2, 4) + tuple(range(5, 5 + len(trailing)))
    return shaped.transpose(permuted).reshape(
        (row_blocks * head_groups, block_rows, width_cols, group_heads) + trailing
    )


def into_tokens(tensor, row_blocks, head_groups):
    trailing = tensor.shape[4:]
    block_rows = tensor.shape[1]
    width_cols = tensor.shape[2]
    group_heads = tensor.shape[3]
    shaped = tensor.reshape(
        (row_blocks, head_groups, block_rows, width_cols, group_heads) + trailing
    )
    permuted = (0, 2, 3, 1, 4) + tuple(range(5, 5 + len(trailing)))
    return shaped.transpose(permuted).reshape(
        (row_blocks * block_rows * width_cols, head_groups * group_heads) + trailing
    )


def general_shards(query_vectors, key_vectors, value_vectors, request_of_slot):
    scaling = HS ** (-0.5)
    token_count = ROWS * COLS
    partner_key, partner_value = partner((key_vectors, value_vectors), "view", 0)
    head_blocks = 4
    block_heads = HEADS // head_blocks
    own_query = query_vectors.reshape(token_count, head_blocks, block_heads, HS)
    both_keys = jnp.concatenate(
        [
            key_vectors.reshape(token_count, head_blocks, block_heads, HS),
            partner_key.reshape(token_count, head_blocks, block_heads, HS),
        ],
        axis=0,
    )
    both_values = jnp.concatenate(
        [
            value_vectors.reshape(token_count, head_blocks, block_heads, HS),
            partner_value.reshape(token_count, head_blocks, block_heads, HS),
        ],
        axis=0,
    )
    query_row = jnp.arange(token_count) // COLS
    key_row = jnp.arange(2 * token_count) % token_count // COLS
    local_allowed = query_row[:, None] != key_row[None, :]

    def local_block(triple):
        block_scores = (
            jnp.einsum("nhx,khx->hnk", triple[0], triple[1], preferred_element_type=jnp.float32)
            * scaling
        )
        block_peak, block_total, block_weights = masked_softmax(block_scores, local_allowed[None])
        block_sum = jnp.einsum(
            "hnk,khx->nhx", block_weights, triple[2], preferred_element_type=jnp.float32
        )
        return (block_peak.T, block_total.T, block_sum)

    block_peaks, block_totals, block_sums = lax.map(
        local_block,
        (
            jnp.moveaxis(own_query, 1, 0),
            jnp.moveaxis(both_keys, 1, 0),
            jnp.moveaxis(both_values, 1, 0),
        ),
    )
    local_peak = jnp.moveaxis(block_peaks, 0, 1).reshape(token_count, HEADS)
    local_total = jnp.moveaxis(block_totals, 0, 1).reshape(token_count, HEADS)
    local_sum = jnp.moveaxis(block_sums, 0, 1).reshape(token_count, HEADS, HS)
    device_count = lax.axis_size("view")
    slot_count = device_count // 4
    pass_images = device_count // 2
    head_groups = 8
    row_blocks = device_count // head_groups
    block_rows = ROWS // row_blocks
    slot_request = jnp.broadcast_to(
        request_of_slot[:, None], (request_of_slot.shape[0], 2 * COLS)
    ).reshape(-1)
    row_allowed = slot_request[:, None] == slot_request[None, :]

    def arrange(tensor):
        shaped = tensor.reshape(slot_count, 2, 2, block_rows, COLS, HS).transpose(1, 3, 0, 2, 4, 5)
        return shaped.reshape(2 * block_rows, pass_images * COLS, HS)

    def restore(tensor):
        trailing = tensor.shape[2:]
        shaped = tensor.reshape((2, block_rows, slot_count, 2, COLS) + trailing)
        permuted = (2, 0, 3, 1, 4) + tuple(range(5, 5 + len(trailing)))
        return shaped.transpose(permuted).reshape((device_count, block_rows, COLS) + trailing)

    def one_head(triple):
        row_scores = (
            jnp.einsum(
                "bnx,bkx->bnk",
                arrange(triple[0]),
                arrange(triple[1]),
                preferred_element_type=jnp.float32,
            )
            * scaling
        )
        row_peak, row_total, row_weights = masked_softmax(row_scores, row_allowed[None])
        row_sum = jnp.einsum(
            "bnk,bkx->bnx", row_weights, arrange(triple[2]), preferred_element_type=jnp.float32
        )
        return (restore(row_peak), restore(row_total), restore(row_sum))

    query_rows = into_rows(query_vectors.reshape(ROWS, COLS, HEADS, HS), row_blocks, head_groups)
    key_rows = into_rows(key_vectors.reshape(ROWS, COLS, HEADS, HS), row_blocks, head_groups)
    value_rows = into_rows(value_vectors.reshape(ROWS, COLS, HEADS, HS), row_blocks, head_groups)
    by_head = (
        jnp.moveaxis(
            lax.all_to_all(query_rows, "view", split_axis=0, concat_axis=0, tiled=True), 3, 0
        ),
        jnp.moveaxis(
            lax.all_to_all(key_rows, "view", split_axis=0, concat_axis=0, tiled=True), 3, 0
        ),
        jnp.moveaxis(
            lax.all_to_all(value_rows, "view", split_axis=0, concat_axis=0, tiled=True), 3, 0
        ),
    )
    row_peaks, row_totals, row_sums = lax.map(one_head, by_head)
    peak_part = jnp.moveaxis(row_peaks, 0, 3)
    total_part = jnp.moveaxis(row_totals, 0, 3)
    sum_part = jnp.moveaxis(row_sums, 0, 3)
    row_peak = lax.all_to_all(peak_part, "view", split_axis=0, concat_axis=0, tiled=True)
    row_total = lax.all_to_all(total_part, "view", split_axis=0, concat_axis=0, tiled=True)
    row_sum = lax.all_to_all(sum_part, "view", split_axis=0, concat_axis=0, tiled=True)
    row_peak = into_tokens(row_peak, row_blocks, head_groups)
    row_total = into_tokens(row_total, row_blocks, head_groups)
    row_sum = into_tokens(row_sum, row_blocks, head_groups)
    attended = combine((local_peak, local_total, local_sum), (row_peak, row_total, row_sum))
    return attended.reshape(1, ROWS, COLS, HEADS * HS)


PARTS = 4
SKEW = 5
CHUNK = 4
LAG = 2
GROUPS = 2


def pair_kernel(
    req_hbm, q_ref, k_ref, v_ref, o_ref,
    req_ref, queries, kv, outer, inner, crossing, ending, chosen, bias, results, sums, peaks, totals,
    req_sem, load_sem, swap_send, swap_recv, own_send, outer_recv, cross_send, inner_recv, end_send, out_send, out_recv, out_sem,
):
    half, size, _ = sums.shape
    rows = queries.shape[2]
    block = 2 * rows
    chunks = half // CHUNK
    me = lax.axis_index("view")
    domain = me % 2
    slot = me // 4
    other = 1 - domain
    twin = me + other - domain
    upper = slot // 2
    end_slot = 3 * upper
    mid_slot = 1 + upper
    is_end = slot == end_slot
    is_mid = slot == mid_slot
    near = me + 4 * (end_slot + mid_slot - 2 * slot)
    across = me + 4 * (3 - 2 * slot)

    def remote(src, dst, send, recv, device):
        return pltpu.make_async_remote_copy(
            src_ref=src, dst_ref=dst, send_sem=send, recv_sem=recv,
            device_id={"view": device}, device_id_type=pl.DeviceIdType.MESH,
        )

    def lanes(at, group):
        return pl.ds(pl.multiple_of((group * half + at) * size, size), size)

    sources = (k_ref, v_ref, q_ref)

    def wide(chunk, group):
        return pl.ds(pl.multiple_of((group * half + chunk * CHUNK) * size, CHUNK * size), CHUNK * size)

    def place(chunk, which, whose):
        columns = wide(chunk, 0)
        return queries.at[whose, :, :, columns] if which == 2 else kv.at[which, whose, :, :, columns]

    def load(chunk, which):
        return pltpu.make_async_copy(
            sources[which].at[:, :, wide(chunk, domain)], place(chunk, which, 0), load_sem.at[which, chunk]
        )

    def swap(chunk, which):
        return remote(
            sources[which].at[:, :, wide(chunk, other)], place(chunk, which, 1),
            swap_send.at[which], swap_recv.at[which, chunk], twin,
        )

    def own_copy(at, part):
        n = at * PARTS + part
        return remote(
            kv.at[part % 2, part // 2, :, :, lanes(at, 0)], outer.at[n], own_send, outer_recv.at[n], near
        )

    def cross_copy(n):
        return remote(crossing.at[n], inner.at[n], cross_send, inner_recv.at[n], across)

    def end_copy(n):
        return remote(ending.at[n], inner.at[n], end_send, inner_recv.at[n], near)

    def out_copy(at):
        return remote(results.at[1, at], o_ref.at[:, :, lanes(at, domain)], out_send, out_recv, twin)

    def keep_copy(at):
        return pltpu.make_async_copy(results.at[0, at], o_ref.at[:, :, lanes(at, domain)], out_sem)

    request = pltpu.make_async_copy(req_hbm, req_ref, req_sem)
    request.start()
    barrier = pltpu.get_barrier_semaphore()
    for device in (twin, near):
        pl.semaphore_signal(barrier, inc=1, device_id={"view": device}, device_id_type=pl.DeviceIdType.MESH)

    @pl.when(is_mid)
    def _():
        pl.semaphore_signal(barrier, inc=1, device_id={"view": across}, device_id_type=pl.DeviceIdType.MESH)

    for chunk in range(chunks):
        for which in range(3):
            load(chunk, which).start()

    @pl.when(is_mid)
    def _():
        pl.semaphore_wait(barrier, 3)

    @pl.when(is_end)
    def _():
        pl.semaphore_wait(barrier, 2)

    for which in range(2):
        swap(0, which).start()

    @pl.when(is_end)
    def _():
        for which in range(2):
            load(0, which).wait()
            own_copy(0, which).start()

    swap(0, 2).start()
    for chunk in range(1, chunks):
        for which in range(3):
            swap(chunk, which).start()

    def fetched(at, which):
        @pl.when(at % CHUNK == 0)
        def _():
            load(at // CHUNK, which).wait()
            swap(at // CHUNK, which).wait_recv()

    @pl.when(is_end)
    def _():
        for which in range(2):
            swap(0, which).wait_recv()
            own_copy(0, 2 + which).start()

        @pl.loop(1, half)
        def _(at):
            for which in range(2):
                fetched(at, which)
            for part in range(PARTS):
                own_copy(at, part).start()

    request.wait()
    mine = req_ref[slot]
    end_same = (req_ref[end_slot] == mine).astype(jnp.int32)
    mid_same = (req_ref[mid_slot] == mine).astype(jnp.int32)
    far_same = jnp.maximum(
        (req_ref[3 - end_slot] == mine).astype(jnp.int32), (req_ref[3 - mid_slot] == mine).astype(jnp.int32)
    )
    near_same = jnp.minimum(end_same, mid_same)
    paired = jnp.maximum(near_same, far_same)

    query_row = lax.broadcasted_iota(jnp.int32, bias.shape, 0) % rows // COLS
    key_row = lax.broadcasted_iota(jnp.int32, bias.shape, 1) % rows // COLS
    bias[...] = jnp.where(paired > 0, jnp.where(query_row == key_row, 0.0, NEG_FILL), NEG_FILL)

    def own_unit(at, part):
        return kv[part % 2, part // 2, :, :, lanes(at, 0)]

    def pass_across(at, part):
        @pl.when(is_mid)
        def _():
            n = at * PARTS + part
            own_copy(at, part).wait_recv()
            crossing[n] = jnp.where(far_same > 0, own_unit(at, part), outer[n])
            cross_copy(n).start()

    def pass_out(at, part):
        n = at * PARTS + part
        cross_copy(n).wait_recv()

        @pl.when(is_mid)
        def _():
            ending[n] = jnp.where(near_same > 0, own_unit(at, part), inner[n])
            end_copy(n).start()

    scaling = size ** (-0.5) * LOG2E

    def scores_of(keys, asking):
        return (
            lax.dot_general(keys, asking, (((1,), (1,)), ((), ())), preferred_element_type=jnp.float32) * scaling
        )

    def weighted(raised, values):
        return lax.dot_general(
            values, raised.astype(jnp.bfloat16), (((0,), (0,)), ((), ())), preferred_element_type=jnp.float32
        )

    def own_part(at):
        asking = queries[:, :, :, lanes(at, 0)]
        scores = scores_of(
            kv[0, :, :, :, lanes(at, 0)].reshape(GROUPS * block, size),
            jnp.concatenate([asking[:, group].reshape(block, size) for group in range(GROUPS)], axis=0),
        )
        peak = jnp.max(scores, axis=0, keepdims=True)
        raised = jnp.exp2(scores - peak)
        peaks[at] = peak
        totals[at] = jnp.sum(raised, axis=0, keepdims=True)
        sums[at] = weighted(raised, kv[1, :, :, :, lanes(at, 0)].reshape(GROUPS * block, size))

    def finish(at):
        @pl.when(is_mid)
        def _():
            chosen[...] = jnp.where(near_same > 0, outer[pl.ds(at * 4, 4)], inner[pl.ds(at * 4, 4)])

        @pl.when(is_end)
        def _():
            chosen[...] = inner[pl.ds(at * 4, 4)]

        def both(which, group):
            return jnp.concatenate([chosen[which, group], chosen[2 + which, group]], axis=0)

        for group in range(GROUPS):
            columns = slice(group * block, (group + 1) * block)
            scores = scores_of(
                both(0, group), queries[:, group, :, lanes(at, 0)].reshape(block, size)
            ) + bias[...]
            own_peak = peaks[at, :, columns]
            peak = jnp.maximum(own_peak, jnp.max(scores, axis=0, keepdims=True))
            raised = jnp.exp2(scores - peak)
            kept = jnp.exp2(own_peak - peak)
            total = totals[at, :, columns] * kept + jnp.sum(raised, axis=0, keepdims=True)
            summed = sums[at, :, columns] * kept + weighted(raised, both(1, group))
            attended = (summed / total).T.astype(jnp.bfloat16)
            results[:, at, group] = attended.reshape(2, rows, size)
        out_copy(at).start()
        keep_copy(at).start()

    def head(at, first):
        @pl.when(is_mid)
        def _():
            for which in range(2):
                fetched(at, which)

        fetched(at, 2)
        for part in range(PARTS):
            pass_across(at, part)
            behind = part - SKEW
            if not first or at * PARTS + behind >= 0:
                pass_out(at + behind // PARTS, behind % PARTS)
            if part == 1:
                own_part(at)
            if part == PARTS - 1 and not first:
                finish(at - LAG)

    for at in range(LAG):
        head(at, True)

    @pl.loop(LAG, half)
    def _(at):
        head(at, False)

    for number in range(half * PARTS - SKEW, half * PARTS):
        pass_out(number // PARTS, number % PARTS)
        if number % PARTS == PARTS - 1:
            finish(number // PARTS)

    whole = pl.ds(0, half * size)
    for which in range(3):
        side = sources[which].at[:, :, whole]
        remote(side, side, swap_send.at[which], out_recv, twin).wait_send()

    @pl.when(is_end)
    def _():
        remote(outer, outer, own_send, out_recv, near).wait_send()

    @pl.when(is_mid)
    def _():
        remote(crossing, inner, cross_send, out_recv, across).wait_send()
        remote(ending, inner, end_send, out_recv, near).wait_send()

    pltpu.make_async_copy(results.at[0], results.at[1], out_sem).wait()
    remote(results.at[1], results.at[1], out_send, out_recv, twin).wait()


def pair_shards(query_vectors, key_vectors, value_vectors, request_of_slot):
    rows = ROWS * COLS // GROUPS
    half = HEADS // 2
    flat = [tensor.reshape(GROUPS, rows, HEADS * HS) for tensor in (query_vectors, key_vectors, value_vectors)]
    vmem = pl.BlockSpec(memory_space=pltpu.VMEM)
    hbm = pl.BlockSpec(memory_space=pltpu.HBM)
    bank = pltpu.VMEM((half * 4, GROUPS, rows, HS), jnp.bfloat16)
    line = pltpu.VMEM((half, 1, GROUPS * 2 * rows), jnp.float32)
    one = pltpu.SemaphoreType.DMA
    three = pltpu.SemaphoreType.DMA((3, half // CHUNK))
    units = pltpu.SemaphoreType.DMA((half * PARTS,))
    scores = (2 * ROWS * COLS) ** 2 * half
    out = pl.pallas_call(
        pair_kernel,
        out_shape=jax.ShapeDtypeStruct((GROUPS, rows, HEADS * HS), jnp.bfloat16),
        in_specs=[hbm, hbm, hbm, hbm],
        out_specs=vmem,
        scratch_shapes=[
            pltpu.SMEM(request_of_slot.shape, jnp.int32),
            pltpu.VMEM((2, GROUPS, rows, half * HS), jnp.bfloat16),
            pltpu.VMEM((2, 2, GROUPS, rows, half * HS), jnp.bfloat16),
            bank, bank, bank, bank,
            pltpu.VMEM((4, GROUPS, rows, HS), jnp.bfloat16),
            pltpu.VMEM((2 * rows, 2 * rows), jnp.float32),
            pltpu.VMEM((2, half, GROUPS, rows, HS), jnp.bfloat16),
            pltpu.VMEM((half, HS, GROUPS * 2 * rows), jnp.float32),
            line, line,
            one, three, pltpu.SemaphoreType.DMA((3,)), three, one, units, one, units, one, one, one, one,
        ],
        compiler_params=pltpu.CompilerParams(
            collective_id=0, has_side_effects=True, vmem_limit_bytes=VMEM_LIMIT
        ),
        cost_estimate=pl.CostEstimate(
            flops=6 * scores * HS, bytes_accessed=8 * ROWS * COLS * HEADS * HS, transcendentals=2 * scores
        ),
    )(request_of_slot, *flat)
    return out.reshape(1, ROWS, COLS, HEADS * HS)


def solution(mesh):
    slot_count = mesh.shape["view"] // 4
    shards = pair_shards if slot_count == 4 else general_shards
    return jax.shard_map(
        shards,
        mesh=mesh,
        in_specs=(
            P(("groups", "view"), None, None, None),
            P(("groups", "view"), None, None, None),
            P(("groups", "view"), None, None, None),
            P("groups"),
        ),
        out_specs=P(("groups", "view"), None, None, None),
        check_vma=False,
    )
```

```python
import jax
import jax.numpy as jnp
from jax import lax
from jax.experimental import pallas as pl
from jax.experimental.pallas import tpu as pltpu
from jax.sharding import PartitionSpec as P

HEADS = 32
HS = 128
ROWS = 16
COLS = 8
LOG2E = 1.4426950408889634
VMEM_LIMIT = 209 * 256 * 1024


NEG_FILL = -1e30


def partner(value, axis, distance):
    return lax.ppermute(value, axis, [(i, i ^ 1 << distance) for i in range(lax.axis_size(axis))])


def masked_softmax(scores, allowed):
    scores = jnp.where(allowed, scores, NEG_FILL)
    maximum = jnp.max(scores, axis=-1)
    raised = jnp.exp(scores - maximum[..., None])
    totals = jnp.sum(raised, axis=-1)
    return (maximum, totals, raised.astype(jnp.bfloat16))


def combine(first_part, second_part):
    highest = jnp.maximum(first_part[0], second_part[0])
    first_scale = jnp.exp(first_part[0] - highest)
    second_scale = jnp.exp(second_part[0] - highest)
    denominator = first_part[1] * first_scale + second_part[1] * second_scale
    numerator = first_part[2] * first_scale[..., None] + second_part[2] * second_scale[..., None]
    return (numerator / denominator[..., None]).astype(jnp.bfloat16)


def into_rows(tensor, row_blocks, head_groups):
    trailing = tensor.shape[3:]
    block_rows = tensor.shape[0] // row_blocks
    width_cols = tensor.shape[1]
    group_heads = tensor.shape[2] // head_groups
    shaped = tensor.reshape(
        (row_blocks, block_rows, width_cols, head_groups, group_heads) + trailing
    )
    permuted = (0, 3, 1, 2, 4) + tuple(range(5, 5 + len(trailing)))
    return shaped.transpose(permuted).reshape(
        (row_blocks * head_groups, block_rows, width_cols, group_heads) + trailing
    )


def into_tokens(tensor, row_blocks, head_groups):
    trailing = tensor.shape[4:]
    block_rows = tensor.shape[1]
    width_cols = tensor.shape[2]
    group_heads = tensor.shape[3]
    shaped = tensor.reshape(
        (row_blocks, head_groups, block_rows, width_cols, group_heads) + trailing
    )
    permuted = (0, 2, 3, 1, 4) + tuple(range(5, 5 + len(trailing)))
    return shaped.transpose(permuted).reshape(
        (row_blocks * block_rows * width_cols, head_groups * group_heads) + trailing
    )


def general_shards(query_vectors, key_vectors, value_vectors, request_of_slot):
    scaling = HS ** (-0.5)
    token_count = ROWS * COLS
    partner_key, partner_value = partner((key_vectors, value_vectors), "view", 0)
    head_blocks = 4
    block_heads = HEADS // head_blocks
    own_query = query_vectors.reshape(token_count, head_blocks, block_heads, HS)
    both_keys = jnp.concatenate(
        [
            key_vectors.reshape(token_count, head_blocks, block_heads, HS),
            partner_key.reshape(token_count, head_blocks, block_heads, HS),
        ],
        axis=0,
    )
    both_values = jnp.concatenate(
        [
            value_vectors.reshape(token_count, head_blocks, block_heads, HS),
            partner_value.reshape(token_count, head_blocks, block_heads, HS),
        ],
        axis=0,
    )
    query_row = jnp.arange(token_count) // COLS
    key_row = jnp.arange(2 * token_count) % token_count // COLS
    local_allowed = query_row[:, None] != key_row[None, :]

    def local_block(triple):
        block_scores = (
            jnp.einsum("nhx,khx->hnk", triple[0], triple[1], preferred_element_type=jnp.float32)
            * scaling
        )
        block_peak, block_total, block_weights = masked_softmax(block_scores, local_allowed[None])
        block_sum = jnp.einsum(
            "hnk,khx->nhx", block_weights, triple[2], preferred_element_type=jnp.float32
        )
        return (block_peak.T, block_total.T, block_sum)

    block_peaks, block_totals, block_sums = lax.map(
        local_block,
        (
            jnp.moveaxis(own_query, 1, 0),
            jnp.moveaxis(both_keys, 1, 0),
            jnp.moveaxis(both_values, 1, 0),
        ),
    )
    local_peak = jnp.moveaxis(block_peaks, 0, 1).reshape(token_count, HEADS)
    local_total = jnp.moveaxis(block_totals, 0, 1).reshape(token_count, HEADS)
    local_sum = jnp.moveaxis(block_sums, 0, 1).reshape(token_count, HEADS, HS)
    device_count = lax.axis_size("view")
    slot_count = device_count // 4
    pass_images = device_count // 2
    head_groups = 8
    row_blocks = device_count // head_groups
    block_rows = ROWS // row_blocks
    slot_request = jnp.broadcast_to(
        request_of_slot[:, None], (request_of_slot.shape[0], 2 * COLS)
    ).reshape(-1)
    row_allowed = slot_request[:, None] == slot_request[None, :]

    def arrange(tensor):
        shaped = tensor.reshape(slot_count, 2, 2, block_rows, COLS, HS).transpose(1, 3, 0, 2, 4, 5)
        return shaped.reshape(2 * block_rows, pass_images * COLS, HS)

    def restore(tensor):
        trailing = tensor.shape[2:]
        shaped = tensor.reshape((2, block_rows, slot_count, 2, COLS) + trailing)
        permuted = (2, 0, 3, 1, 4) + tuple(range(5, 5 + len(trailing)))
        return shaped.transpose(permuted).reshape((device_count, block_rows, COLS) + trailing)

    def one_head(triple):
        row_scores = (
            jnp.einsum(
                "bnx,bkx->bnk",
                arrange(triple[0]),
                arrange(triple[1]),
                preferred_element_type=jnp.float32,
            )
            * scaling
        )
        row_peak, row_total, row_weights = masked_softmax(row_scores, row_allowed[None])
        row_sum = jnp.einsum(
            "bnk,bkx->bnx", row_weights, arrange(triple[2]), preferred_element_type=jnp.float32
        )
        return (restore(row_peak), restore(row_total), restore(row_sum))

    query_rows = into_rows(query_vectors.reshape(ROWS, COLS, HEADS, HS), row_blocks, head_groups)
    key_rows = into_rows(key_vectors.reshape(ROWS, COLS, HEADS, HS), row_blocks, head_groups)
    value_rows = into_rows(value_vectors.reshape(ROWS, COLS, HEADS, HS), row_blocks, head_groups)
    by_head = (
        jnp.moveaxis(
            lax.all_to_all(query_rows, "view", split_axis=0, concat_axis=0, tiled=True), 3, 0
        ),
        jnp.moveaxis(
            lax.all_to_all(key_rows, "view", split_axis=0, concat_axis=0, tiled=True), 3, 0
        ),
        jnp.moveaxis(
            lax.all_to_all(value_rows, "view", split_axis=0, concat_axis=0, tiled=True), 3, 0
        ),
    )
    row_peaks, row_totals, row_sums = lax.map(one_head, by_head)
    peak_part = jnp.moveaxis(row_peaks, 0, 3)
    total_part = jnp.moveaxis(row_totals, 0, 3)
    sum_part = jnp.moveaxis(row_sums, 0, 3)
    row_peak = lax.all_to_all(peak_part, "view", split_axis=0, concat_axis=0, tiled=True)
    row_total = lax.all_to_all(total_part, "view", split_axis=0, concat_axis=0, tiled=True)
    row_sum = lax.all_to_all(sum_part, "view", split_axis=0, concat_axis=0, tiled=True)
    row_peak = into_tokens(row_peak, row_blocks, head_groups)
    row_total = into_tokens(row_total, row_blocks, head_groups)
    row_sum = into_tokens(row_sum, row_blocks, head_groups)
    attended = combine((local_peak, local_total, local_sum), (row_peak, row_total, row_sum))
    return attended.reshape(1, ROWS, COLS, HEADS * HS)


PARTS = 4
SKEW = 4
CHUNK = 4
LAG = 1
GROUPS = 2


def pair_kernel(
    req_hbm, q_ref, k_ref, v_ref, o_ref,
    req_ref, queries, kv, outer, inner, crossing, ending, chosen, bias, results, sums, peaks, totals,
    req_sem, load_sem, swap_send, swap_recv, own_send, outer_recv, cross_send, inner_recv, end_send, out_send, out_recv, out_sem,
):
    half, size, _ = sums.shape
    rows = queries.shape[2]
    block = 2 * rows
    chunks = half // CHUNK
    me = lax.axis_index("view")
    domain = me % 2
    slot = me // 4
    other = 1 - domain
    twin = me + other - domain
    upper = slot // 2
    end_slot = 3 * upper
    mid_slot = 1 + upper
    is_end = slot == end_slot
    is_mid = slot == mid_slot
    near = me + 4 * (end_slot + mid_slot - 2 * slot)
    across = me + 4 * (3 - 2 * slot)

    def remote(src, dst, send, recv, device):
        return pltpu.make_async_remote_copy(
            src_ref=src, dst_ref=dst, send_sem=send, recv_sem=recv,
            device_id={"view": device}, device_id_type=pl.DeviceIdType.MESH,
        )

    def lanes(at, group):
        return pl.ds(pl.multiple_of((group * half + at) * size, size), size)

    sources = (k_ref, v_ref, q_ref)

    def wide(chunk, group):
        return pl.ds(pl.multiple_of((group * half + chunk * CHUNK) * size, CHUNK * size), CHUNK * size)

    def place(chunk, which, whose):
        columns = wide(chunk, 0)
        return queries.at[whose, :, :, columns] if which == 2 else kv.at[which, whose, :, :, columns]

    def load(chunk, which):
        return pltpu.make_async_copy(
            sources[which].at[:, :, wide(chunk, domain)], place(chunk, which, 0), load_sem.at[which, chunk]
        )

    def swap(chunk, which):
        return remote(
            sources[which].at[:, :, wide(chunk, other)], place(chunk, which, 1),
            swap_send.at[which], swap_recv.at[which, chunk], twin,
        )

    def own_copy(at, part):
        n = at * PARTS + part
        return remote(
            kv.at[part % 2, part // 2, :, :, lanes(at, 0)], outer.at[n], own_send, outer_recv.at[n], near
        )

    def cross_copy(n):
        return remote(crossing.at[n], inner.at[n], cross_send, inner_recv.at[n], across)

    def end_copy(n):
        return remote(ending.at[n], inner.at[n], end_send, inner_recv.at[n], near)

    def out_copy(at):
        return remote(results.at[1, at], o_ref.at[:, :, lanes(at, domain)], out_send, out_recv, twin)

    def keep_copy(at):
        return pltpu.make_async_copy(results.at[0, at], o_ref.at[:, :, lanes(at, domain)], out_sem)

    request = pltpu.make_async_copy(req_hbm, req_ref, req_sem)
    request.start()
    barrier = pltpu.get_barrier_semaphore()
    for device in (twin, near):
        pl.semaphore_signal(barrier, inc=1, device_id={"view": device}, device_id_type=pl.DeviceIdType.MESH)

    @pl.when(is_mid)
    def _():
        pl.semaphore_signal(barrier, inc=1, device_id={"view": across}, device_id_type=pl.DeviceIdType.MESH)

    for chunk in range(chunks):
        for which in range(3):
            load(chunk, which).start()

    @pl.when(is_mid)
    def _():
        pl.semaphore_wait(barrier, 3)

    @pl.when(is_end)
    def _():
        pl.semaphore_wait(barrier, 2)

    for which in range(2):
        swap(0, which).start()

    @pl.when(is_end)
    def _():
        for which in range(2):
            load(0, which).wait()
            own_copy(0, which).start()

    swap(0, 2).start()
    for chunk in range(1, chunks):
        for which in range(3):
            swap(chunk, which).start()

    def fetched(at, which):
        @pl.when(at % CHUNK == 0)
        def _():
            load(at // CHUNK, which).wait()
            swap(at // CHUNK, which).wait_recv()

    @pl.when(is_end)
    def _():
        for which in range(2):
            swap(0, which).wait_recv()
            own_copy(0, 2 + which).start()

        @pl.loop(1, half)
        def _(at):
            for which in range(2):
                fetched(at, which)
            for part in range(PARTS):
                own_copy(at, part).start()

    request.wait()
    mine = req_ref[slot]
    end_same = (req_ref[end_slot] == mine).astype(jnp.int32)
    mid_same = (req_ref[mid_slot] == mine).astype(jnp.int32)
    far_same = jnp.maximum(
        (req_ref[3 - end_slot] == mine).astype(jnp.int32), (req_ref[3 - mid_slot] == mine).astype(jnp.int32)
    )
    near_same = jnp.minimum(end_same, mid_same)
    paired = jnp.maximum(near_same, far_same)

    query_row = lax.broadcasted_iota(jnp.int32, bias.shape, 0) % rows // COLS
    key_row = lax.broadcasted_iota(jnp.int32, bias.shape, 1) % rows // COLS
    bias[...] = jnp.where(paired > 0, jnp.where(query_row == key_row, 0.0, NEG_FILL), NEG_FILL)

    def own_unit(at, part):
        return kv[part % 2, part // 2, :, :, lanes(at, 0)]

    def pass_across(at, part):
        @pl.when(is_mid)
        def _():
            n = at * PARTS + part
            own_copy(at, part).wait_recv()
            crossing[n] = jnp.where(far_same > 0, own_unit(at, part), outer[n])
            cross_copy(n).start()

    def pass_out(at, part):
        n = at * PARTS + part
        cross_copy(n).wait_recv()

        @pl.when(is_mid)
        def _():
            ending[n] = jnp.where(near_same > 0, own_unit(at, part), inner[n])
            end_copy(n).start()

    scaling = size ** (-0.5) * LOG2E

    def scores_of(keys, asking):
        return (
            lax.dot_general(keys, asking, (((1,), (1,)), ((), ())), preferred_element_type=jnp.float32) * scaling
        )

    def weighted(raised, values):
        return lax.dot_general(
            values, raised.astype(jnp.bfloat16), (((0,), (0,)), ((), ())), preferred_element_type=jnp.float32
        )

    def own_part(at):
        asking = queries[:, :, :, lanes(at, 0)]
        scores = scores_of(
            kv[0, :, :, :, lanes(at, 0)].reshape(GROUPS * block, size),
            jnp.concatenate([asking[:, group].reshape(block, size) for group in range(GROUPS)], axis=0),
        )
        peak = jnp.max(scores, axis=0, keepdims=True)
        raised = jnp.exp2(scores - peak)
        total = jnp.sum(raised, axis=0, keepdims=True)
        return peak, total, weighted(raised, kv[1, :, :, :, lanes(at, 0)].reshape(GROUPS * block, size))

    def choose(at):
        @pl.when(is_mid)
        def _():
            chosen[...] = jnp.where(near_same > 0, outer[pl.ds(at * 4, 4)], inner[pl.ds(at * 4, 4)])

        @pl.when(is_end)
        def _():
            chosen[...] = inner[pl.ds(at * 4, 4)]

    def pair_part(at):
        def both(which, group):
            return jnp.concatenate([chosen[which, group], chosen[2 + which, group]], axis=0)

        attended = []
        for group in range(GROUPS):
            columns = slice(group * block, (group + 1) * block)
            scores = scores_of(both(0, group), queries[:, group, :, lanes(at, 0)].reshape(block, size)) + bias[...]
            own_peak = peaks[at, :, columns]
            peak = jnp.maximum(own_peak, jnp.max(scores, axis=0, keepdims=True))
            raised = jnp.exp2(scores - peak)
            kept = jnp.exp2(own_peak - peak)
            total = totals[at, :, columns] * kept + jnp.sum(raised, axis=0, keepdims=True)
            summed = sums[at, :, columns] * kept + weighted(raised, both(1, group))
            attended.append((summed * (1.0 / total)).T.astype(jnp.bfloat16).reshape(2, rows, size))
        return attended

    def compute(own, done):
        if done is not None:
            choose(done)
            attended = pair_part(done)
        if own is not None:
            peaks_own, totals_own, sums_own = own_part(own)
            peaks[own] = peaks_own
            totals[own] = totals_own
            sums[own] = sums_own
        if done is not None:
            for group in range(GROUPS):
                results[:, done, group] = attended[group]
            out_copy(done).start()
            keep_copy(done).start()

    def head(at, first):
        @pl.when(is_mid)
        def _():
            for which in range(2):
                fetched(at, which)

        fetched(at, 2)
        for part in range(PARTS):
            pass_across(at, part)
            behind = part - SKEW
            if not first or at * PARTS + behind >= 0:
                pass_out(at + behind // PARTS, behind % PARTS)
            if part == PARTS - 1:
                compute(at, None if first else at - LAG)

    for at in range(LAG):
        head(at, True)

    @pl.loop(LAG, half)
    def _(at):
        head(at, False)

    for number in range(half * PARTS - SKEW, half * PARTS):
        pass_out(number // PARTS, number % PARTS)
        if number % PARTS == PARTS - 1:
            compute(None, number // PARTS)

    whole = pl.ds(0, half * size)
    for which in range(3):
        side = sources[which].at[:, :, whole]
        remote(side, side, swap_send.at[which], out_recv, twin).wait_send()

    @pl.when(is_end)
    def _():
        remote(outer, outer, own_send, out_recv, near).wait_send()

    @pl.when(is_mid)
    def _():
        remote(crossing, inner, cross_send, out_recv, across).wait_send()
        remote(ending, inner, end_send, out_recv, near).wait_send()

    pltpu.make_async_copy(results.at[0], results.at[1], out_sem).wait()
    remote(results.at[1], results.at[1], out_send, out_recv, twin).wait()


def pair_shards(query_vectors, key_vectors, value_vectors, request_of_slot):
    rows = ROWS * COLS // GROUPS
    half = HEADS // 2
    flat = [tensor.reshape(GROUPS, rows, HEADS * HS) for tensor in (query_vectors, key_vectors, value_vectors)]
    vmem = pl.BlockSpec(memory_space=pltpu.VMEM)
    hbm = pl.BlockSpec(memory_space=pltpu.HBM)
    bank = pltpu.VMEM((half * 4, GROUPS, rows, HS), jnp.bfloat16)
    line = pltpu.VMEM((half, 1, GROUPS * 2 * rows), jnp.float32)
    one = pltpu.SemaphoreType.DMA
    three = pltpu.SemaphoreType.DMA((3, half // CHUNK))
    units = pltpu.SemaphoreType.DMA((half * PARTS,))
    scores = (2 * ROWS * COLS) ** 2 * half
    out = pl.pallas_call(
        pair_kernel,
        out_shape=jax.ShapeDtypeStruct((GROUPS, rows, HEADS * HS), jnp.bfloat16),
        in_specs=[hbm, hbm, hbm, hbm],
        out_specs=vmem,
        scratch_shapes=[
            pltpu.SMEM(request_of_slot.shape, jnp.int32),
            pltpu.VMEM((2, GROUPS, rows, half * HS), jnp.bfloat16),
            pltpu.VMEM((2, 2, GROUPS, rows, half * HS), jnp.bfloat16),
            bank, bank, bank, bank,
            pltpu.VMEM((4, GROUPS, rows, HS), jnp.bfloat16),
            pltpu.VMEM((2 * rows, 2 * rows), jnp.float32),
            pltpu.VMEM((2, half, GROUPS, rows, HS), jnp.bfloat16),
            pltpu.VMEM((half, HS, GROUPS * 2 * rows), jnp.float32),
            line, line,
            one, three, pltpu.SemaphoreType.DMA((3,)), three, one, units, one, units, one, one, one, one,
        ],
        compiler_params=pltpu.CompilerParams(
            collective_id=0, has_side_effects=True, vmem_limit_bytes=VMEM_LIMIT
        ),
        cost_estimate=pl.CostEstimate(
            flops=6 * scores * HS, bytes_accessed=8 * ROWS * COLS * HEADS * HS, transcendentals=2 * scores
        ),
    )(request_of_slot, *flat)
    return out.reshape(1, ROWS, COLS, HEADS * HS)


def solution(mesh):
    slot_count = mesh.shape["view"] // 4
    shards = pair_shards if slot_count == 4 else general_shards
    return jax.shard_map(
        shards,
        mesh=mesh,
        in_specs=(
            P(("groups", "view"), None, None, None),
            P(("groups", "view"), None, None, None),
            P(("groups", "view"), None, None, None),
            P("groups"),
        ),
        out_specs=P(("groups", "view"), None, None, None),
        check_vma=False,
    )
```

```python
import jax
import jax.numpy as jnp
from jax import lax
from jax.experimental import pallas as pl
from jax.experimental.pallas import tpu as pltpu
from jax.sharding import PartitionSpec as P

HEADS = 32
HS = 128
ROWS = 16
COLS = 8
LOG2E = 1.4426950408889634
VMEM_LIMIT = 209 * 256 * 1024


NEG_FILL = -1e30


def partner(value, axis, distance):
    return lax.ppermute(value, axis, [(i, i ^ 1 << distance) for i in range(lax.axis_size(axis))])


def masked_softmax(scores, allowed):
    scores = jnp.where(allowed, scores, NEG_FILL)
    maximum = jnp.max(scores, axis=-1)
    raised = jnp.exp(scores - maximum[..., None])
    totals = jnp.sum(raised, axis=-1)
    return (maximum, totals, raised.astype(jnp.bfloat16))


def combine(first_part, second_part):
    highest = jnp.maximum(first_part[0], second_part[0])
    first_scale = jnp.exp(first_part[0] - highest)
    second_scale = jnp.exp(second_part[0] - highest)
    denominator = first_part[1] * first_scale + second_part[1] * second_scale
    numerator = first_part[2] * first_scale[..., None] + second_part[2] * second_scale[..., None]
    return (numerator / denominator[..., None]).astype(jnp.bfloat16)


def into_rows(tensor, row_blocks, head_groups):
    trailing = tensor.shape[3:]
    block_rows = tensor.shape[0] // row_blocks
    width_cols = tensor.shape[1]
    group_heads = tensor.shape[2] // head_groups
    shaped = tensor.reshape(
        (row_blocks, block_rows, width_cols, head_groups, group_heads) + trailing
    )
    permuted = (0, 3, 1, 2, 4) + tuple(range(5, 5 + len(trailing)))
    return shaped.transpose(permuted).reshape(
        (row_blocks * head_groups, block_rows, width_cols, group_heads) + trailing
    )


def into_tokens(tensor, row_blocks, head_groups):
    trailing = tensor.shape[4:]
    block_rows = tensor.shape[1]
    width_cols = tensor.shape[2]
    group_heads = tensor.shape[3]
    shaped = tensor.reshape(
        (row_blocks, head_groups, block_rows, width_cols, group_heads) + trailing
    )
    permuted = (0, 2, 3, 1, 4) + tuple(range(5, 5 + len(trailing)))
    return shaped.transpose(permuted).reshape(
        (row_blocks * block_rows * width_cols, head_groups * group_heads) + trailing
    )


def general_shards(query_vectors, key_vectors, value_vectors, request_of_slot):
    scaling = HS ** (-0.5)
    token_count = ROWS * COLS
    partner_key, partner_value = partner((key_vectors, value_vectors), "view", 0)
    head_blocks = 4
    block_heads = HEADS // head_blocks
    own_query = query_vectors.reshape(token_count, head_blocks, block_heads, HS)
    both_keys = jnp.concatenate(
        [
            key_vectors.reshape(token_count, head_blocks, block_heads, HS),
            partner_key.reshape(token_count, head_blocks, block_heads, HS),
        ],
        axis=0,
    )
    both_values = jnp.concatenate(
        [
            value_vectors.reshape(token_count, head_blocks, block_heads, HS),
            partner_value.reshape(token_count, head_blocks, block_heads, HS),
        ],
        axis=0,
    )
    query_row = jnp.arange(token_count) // COLS
    key_row = jnp.arange(2 * token_count) % token_count // COLS
    local_allowed = query_row[:, None] != key_row[None, :]

    def local_block(triple):
        block_scores = (
            jnp.einsum("nhx,khx->hnk", triple[0], triple[1], preferred_element_type=jnp.float32)
            * scaling
        )
        block_peak, block_total, block_weights = masked_softmax(block_scores, local_allowed[None])
        block_sum = jnp.einsum(
            "hnk,khx->nhx", block_weights, triple[2], preferred_element_type=jnp.float32
        )
        return (block_peak.T, block_total.T, block_sum)

    block_peaks, block_totals, block_sums = lax.map(
        local_block,
        (
            jnp.moveaxis(own_query, 1, 0),
            jnp.moveaxis(both_keys, 1, 0),
            jnp.moveaxis(both_values, 1, 0),
        ),
    )
    local_peak = jnp.moveaxis(block_peaks, 0, 1).reshape(token_count, HEADS)
    local_total = jnp.moveaxis(block_totals, 0, 1).reshape(token_count, HEADS)
    local_sum = jnp.moveaxis(block_sums, 0, 1).reshape(token_count, HEADS, HS)
    device_count = lax.axis_size("view")
    slot_count = device_count // 4
    pass_images = device_count // 2
    head_groups = 8
    row_blocks = device_count // head_groups
    block_rows = ROWS // row_blocks
    slot_request = jnp.broadcast_to(
        request_of_slot[:, None], (request_of_slot.shape[0], 2 * COLS)
    ).reshape(-1)
    row_allowed = slot_request[:, None] == slot_request[None, :]

    def arrange(tensor):
        shaped = tensor.reshape(slot_count, 2, 2, block_rows, COLS, HS).transpose(1, 3, 0, 2, 4, 5)
        return shaped.reshape(2 * block_rows, pass_images * COLS, HS)

    def restore(tensor):
        trailing = tensor.shape[2:]
        shaped = tensor.reshape((2, block_rows, slot_count, 2, COLS) + trailing)
        permuted = (2, 0, 3, 1, 4) + tuple(range(5, 5 + len(trailing)))
        return shaped.transpose(permuted).reshape((device_count, block_rows, COLS) + trailing)

    def one_head(triple):
        row_scores = (
            jnp.einsum(
                "bnx,bkx->bnk",
                arrange(triple[0]),
                arrange(triple[1]),
                preferred_element_type=jnp.float32,
            )
            * scaling
        )
        row_peak, row_total, row_weights = masked_softmax(row_scores, row_allowed[None])
        row_sum = jnp.einsum(
            "bnk,bkx->bnx", row_weights, arrange(triple[2]), preferred_element_type=jnp.float32
        )
        return (restore(row_peak), restore(row_total), restore(row_sum))

    query_rows = into_rows(query_vectors.reshape(ROWS, COLS, HEADS, HS), row_blocks, head_groups)
    key_rows = into_rows(key_vectors.reshape(ROWS, COLS, HEADS, HS), row_blocks, head_groups)
    value_rows = into_rows(value_vectors.reshape(ROWS, COLS, HEADS, HS), row_blocks, head_groups)
    by_head = (
        jnp.moveaxis(
            lax.all_to_all(query_rows, "view", split_axis=0, concat_axis=0, tiled=True), 3, 0
        ),
        jnp.moveaxis(
            lax.all_to_all(key_rows, "view", split_axis=0, concat_axis=0, tiled=True), 3, 0
        ),
        jnp.moveaxis(
            lax.all_to_all(value_rows, "view", split_axis=0, concat_axis=0, tiled=True), 3, 0
        ),
    )
    row_peaks, row_totals, row_sums = lax.map(one_head, by_head)
    peak_part = jnp.moveaxis(row_peaks, 0, 3)
    total_part = jnp.moveaxis(row_totals, 0, 3)
    sum_part = jnp.moveaxis(row_sums, 0, 3)
    row_peak = lax.all_to_all(peak_part, "view", split_axis=0, concat_axis=0, tiled=True)
    row_total = lax.all_to_all(total_part, "view", split_axis=0, concat_axis=0, tiled=True)
    row_sum = lax.all_to_all(sum_part, "view", split_axis=0, concat_axis=0, tiled=True)
    row_peak = into_tokens(row_peak, row_blocks, head_groups)
    row_total = into_tokens(row_total, row_blocks, head_groups)
    row_sum = into_tokens(row_sum, row_blocks, head_groups)
    attended = combine((local_peak, local_total, local_sum), (row_peak, row_total, row_sum))
    return attended.reshape(1, ROWS, COLS, HEADS * HS)


PARTS = 4
SKEW = 6
CHUNK = 4
LAG = 2
GROUPS = 2


def pair_kernel(
    req_hbm, q_ref, k_ref, v_ref, o_ref,
    req_ref, queries, kv, outer, inner, crossing, ending, chosen, bias, results, sums, peaks, totals,
    req_sem, load_sem, swap_send, swap_recv, own_send, outer_recv, cross_send, inner_recv, end_send, out_send, out_recv, out_sem,
):
    half, size, _ = sums.shape
    rows = queries.shape[2]
    block = 2 * rows
    chunks = half // CHUNK
    me = lax.axis_index("view")
    domain = me % 2
    slot = me // 4
    other = 1 - domain
    twin = me + other - domain
    upper = slot // 2
    end_slot = 3 * upper
    mid_slot = 1 + upper
    is_end = slot == end_slot
    is_mid = slot == mid_slot
    near = me + 4 * (end_slot + mid_slot - 2 * slot)
    across = me + 4 * (3 - 2 * slot)

    def remote(src, dst, send, recv, device):
        return pltpu.make_async_remote_copy(
            src_ref=src, dst_ref=dst, send_sem=send, recv_sem=recv,
            device_id={"view": device}, device_id_type=pl.DeviceIdType.MESH,
        )

    def lanes(at, group):
        return pl.ds(pl.multiple_of((group * half + at) * size, size), size)

    sources = (k_ref, v_ref, q_ref)

    def wide(chunk, group):
        return pl.ds(pl.multiple_of((group * half + chunk * CHUNK) * size, CHUNK * size), CHUNK * size)

    def place(chunk, which, whose):
        columns = wide(chunk, 0)
        return queries.at[whose, :, :, columns] if which == 2 else kv.at[which, whose, :, :, columns]

    def load(chunk, which):
        return pltpu.make_async_copy(
            sources[which].at[:, :, wide(chunk, domain)], place(chunk, which, 0), load_sem.at[which, chunk]
        )

    def swap(chunk, which):
        return remote(
            sources[which].at[:, :, wide(chunk, other)], place(chunk, which, 1),
            swap_send.at[which], swap_recv.at[which, chunk], twin,
        )

    def own_copy(at, part):
        n = at * PARTS + part
        return remote(
            kv.at[part % 2, part // 2, :, :, lanes(at, 0)], outer.at[n], own_send, outer_recv.at[n], near
        )

    def cross_copy(n):
        return remote(crossing.at[n], inner.at[n], cross_send, inner_recv.at[n], across)

    def end_copy(n):
        return remote(ending.at[n], inner.at[n], end_send, inner_recv.at[n], near)

    def out_copy(at):
        return remote(results.at[1, at], o_ref.at[:, :, lanes(at, domain)], out_send, out_recv, twin)

    def keep_copy(at):
        return pltpu.make_async_copy(results.at[0, at], o_ref.at[:, :, lanes(at, domain)], out_sem)

    request = pltpu.make_async_copy(req_hbm, req_ref, req_sem)
    request.start()
    barrier = pltpu.get_barrier_semaphore()
    for device in (twin, near):
        pl.semaphore_signal(barrier, inc=1, device_id={"view": device}, device_id_type=pl.DeviceIdType.MESH)

    @pl.when(is_mid)
    def _():
        pl.semaphore_signal(barrier, inc=1, device_id={"view": across}, device_id_type=pl.DeviceIdType.MESH)

    for chunk in range(chunks):
        for which in range(3):
            load(chunk, which).start()

    @pl.when(is_mid)
    def _():
        pl.semaphore_wait(barrier, 3)

    @pl.when(is_end)
    def _():
        pl.semaphore_wait(barrier, 2)

    for which in range(2):
        swap(0, which).start()

    @pl.when(is_end)
    def _():
        for which in range(2):
            load(0, which).wait()
            own_copy(0, which).start()

    swap(0, 2).start()
    for chunk in range(1, chunks):
        for which in range(3):
            swap(chunk, which).start()

    def fetched(at, which):
        @pl.when(at % CHUNK == 0)
        def _():
            load(at // CHUNK, which).wait()
            swap(at // CHUNK, which).wait_recv()

    @pl.when(is_end)
    def _():
        for which in range(2):
            swap(0, which).wait_recv()
            own_copy(0, 2 + which).start()

        @pl.loop(1, half)
        def _(at):
            for which in range(2):
                fetched(at, which)
            for part in range(PARTS):
                own_copy(at, part).start()

    request.wait()
    mine = req_ref[slot]
    end_same = (req_ref[end_slot] == mine).astype(jnp.int32)
    mid_same = (req_ref[mid_slot] == mine).astype(jnp.int32)
    far_same = jnp.maximum(
        (req_ref[3 - end_slot] == mine).astype(jnp.int32), (req_ref[3 - mid_slot] == mine).astype(jnp.int32)
    )
    near_same = jnp.minimum(end_same, mid_same)
    paired = jnp.maximum(near_same, far_same)

    query_row = lax.broadcasted_iota(jnp.int32, bias.shape, 0) % rows // COLS
    key_row = lax.broadcasted_iota(jnp.int32, bias.shape, 1) % rows // COLS
    bias[...] = jnp.where(paired > 0, jnp.where(query_row == key_row, 0.0, NEG_FILL), NEG_FILL)

    def own_unit(at, part):
        return kv[part % 2, part // 2, :, :, lanes(at, 0)]

    def pass_across(at, part):
        @pl.when(is_mid)
        def _():
            n = at * PARTS + part
            own_copy(at, part).wait_recv()
            crossing[n] = jnp.where(far_same > 0, own_unit(at, part), outer[n])
            cross_copy(n).start()

    def pass_out(at, part):
        n = at * PARTS + part
        cross_copy(n).wait_recv()

        @pl.when(is_mid)
        def _():
            ending[n] = jnp.where(near_same > 0, own_unit(at, part), inner[n])
            end_copy(n).start()

    scaling = size ** (-0.5) * LOG2E

    def scores_of(keys, asking):
        return (
            lax.dot_general(keys, asking, (((1,), (1,)), ((), ())), preferred_element_type=jnp.float32) * scaling
        )

    def weighted(raised, values):
        return lax.dot_general(
            values, raised.astype(jnp.bfloat16), (((0,), (0,)), ((), ())), preferred_element_type=jnp.float32
        )

    def own_part(at):
        asking = queries[:, :, :, lanes(at, 0)]
        scores = scores_of(
            kv[0, :, :, :, lanes(at, 0)].reshape(GROUPS * block, size),
            jnp.concatenate([asking[:, group].reshape(block, size) for group in range(GROUPS)], axis=0),
        )
        peak = jnp.max(scores, axis=0, keepdims=True)
        raised = jnp.exp2(scores - peak)
        total = jnp.sum(raised, axis=0, keepdims=True)
        return peak, total, weighted(raised, kv[1, :, :, :, lanes(at, 0)].reshape(GROUPS * block, size))

    def choose(at):
        @pl.when(is_mid)
        def _():
            chosen[...] = jnp.where(near_same > 0, outer[pl.ds(at * 4, 4)], inner[pl.ds(at * 4, 4)])

        @pl.when(is_end)
        def _():
            chosen[...] = inner[pl.ds(at * 4, 4)]

    def pair_part(at):
        def both(which, group):
            return jnp.concatenate([chosen[which, group], chosen[2 + which, group]], axis=0)

        attended = []
        for group in range(GROUPS):
            columns = slice(group * block, (group + 1) * block)
            scores = scores_of(both(0, group), queries[:, group, :, lanes(at, 0)].reshape(block, size)) + bias[...]
            own_peak = peaks[at, :, columns]
            peak = jnp.maximum(own_peak, jnp.max(scores, axis=0, keepdims=True))
            raised = jnp.exp2(scores - peak)
            kept = jnp.exp2(own_peak - peak)
            total = totals[at, :, columns] * kept + jnp.sum(raised, axis=0, keepdims=True)
            summed = sums[at, :, columns] * kept + weighted(raised, both(1, group))
            attended.append((summed * (1.0 / total)).T.astype(jnp.bfloat16).reshape(2, rows, size))
        return attended

    def compute(own, done):
        if done is not None:
            choose(done)
            attended = pair_part(done)
        if own is not None:
            peaks_own, totals_own, sums_own = own_part(own)
            peaks[own] = peaks_own
            totals[own] = totals_own
            sums[own] = sums_own
        if done is not None:
            for group in range(GROUPS):
                results[:, done, group] = attended[group]
            out_copy(done).start()
            keep_copy(done).start()

    def head(at, first):
        @pl.when(is_mid)
        def _():
            for which in range(2):
                fetched(at, which)

        fetched(at, 2)
        for part in range(PARTS):
            pass_across(at, part)
            behind = part - SKEW
            if not first or at * PARTS + behind >= 0:
                pass_out(at + behind // PARTS, behind % PARTS)
            if part == PARTS - 1:
                compute(at, None if first else at - LAG)

    for at in range(LAG):
        head(at, True)

    @pl.loop(LAG, half)
    def _(at):
        head(at, False)

    for number in range(half * PARTS - SKEW, half * PARTS):
        pass_out(number // PARTS, number % PARTS)
        if number % PARTS == PARTS - 1:
            compute(None, number // PARTS)

    whole = pl.ds(0, half * size)
    for which in range(3):
        side = sources[which].at[:, :, whole]
        remote(side, side, swap_send.at[which], out_recv, twin).wait_send()

    @pl.when(is_end)
    def _():
        remote(outer, outer, own_send, out_recv, near).wait_send()

    @pl.when(is_mid)
    def _():
        remote(crossing, inner, cross_send, out_recv, across).wait_send()
        remote(ending, inner, end_send, out_recv, near).wait_send()

    pltpu.make_async_copy(results.at[0], results.at[1], out_sem).wait()
    remote(results.at[1], results.at[1], out_send, out_recv, twin).wait()


def pair_shards(query_vectors, key_vectors, value_vectors, request_of_slot):
    rows = ROWS * COLS // GROUPS
    half = HEADS // 2
    flat = [tensor.reshape(GROUPS, rows, HEADS * HS) for tensor in (query_vectors, key_vectors, value_vectors)]
    vmem = pl.BlockSpec(memory_space=pltpu.VMEM)
    hbm = pl.BlockSpec(memory_space=pltpu.HBM)
    bank = pltpu.VMEM((half * 4, GROUPS, rows, HS), jnp.bfloat16)
    line = pltpu.VMEM((half, 1, GROUPS * 2 * rows), jnp.float32)
    one = pltpu.SemaphoreType.DMA
    three = pltpu.SemaphoreType.DMA((3, half // CHUNK))
    units = pltpu.SemaphoreType.DMA((half * PARTS,))
    scores = (2 * ROWS * COLS) ** 2 * half
    out = pl.pallas_call(
        pair_kernel,
        out_shape=jax.ShapeDtypeStruct((GROUPS, rows, HEADS * HS), jnp.bfloat16),
        in_specs=[hbm, hbm, hbm, hbm],
        out_specs=vmem,
        scratch_shapes=[
            pltpu.SMEM(request_of_slot.shape, jnp.int32),
            pltpu.VMEM((2, GROUPS, rows, half * HS), jnp.bfloat16),
            pltpu.VMEM((2, 2, GROUPS, rows, half * HS), jnp.bfloat16),
            bank, bank, bank, bank,
            pltpu.VMEM((4, GROUPS, rows, HS), jnp.bfloat16),
            pltpu.VMEM((2 * rows, 2 * rows), jnp.float32),
            pltpu.VMEM((2, half, GROUPS, rows, HS), jnp.bfloat16),
            pltpu.VMEM((half, HS, GROUPS * 2 * rows), jnp.float32),
            line, line,
            one, three, pltpu.SemaphoreType.DMA((3,)), three, one, units, one, units, one, one, one, one,
        ],
        compiler_params=pltpu.CompilerParams(
            collective_id=0, has_side_effects=True, vmem_limit_bytes=VMEM_LIMIT
        ),
        cost_estimate=pl.CostEstimate(
            flops=6 * scores * HS, bytes_accessed=8 * ROWS * COLS * HEADS * HS, transcendentals=2 * scores
        ),
    )(request_of_slot, *flat)
    return out.reshape(1, ROWS, COLS, HEADS * HS)


def solution(mesh):
    slot_count = mesh.shape["view"] // 4
    shards = pair_shards if slot_count == 4 else general_shards
    return jax.shard_map(
        shards,
        mesh=mesh,
        in_specs=(
            P(("groups", "view"), None, None, None),
            P(("groups", "view"), None, None, None),
            P(("groups", "view"), None, None, None),
            P("groups"),
        ),
        out_specs=P(("groups", "view"), None, None, None),
        check_vma=False,
    )
```

```python
import jax
import jax.numpy as jnp
from jax import lax
from jax.experimental import pallas as pl
from jax.experimental.pallas import tpu as pltpu
from jax.sharding import PartitionSpec as P

HEADS = 32
HS = 128
ROWS = 16
COLS = 8
LOG2E = 1.4426950408889634
VMEM_LIMIT = 209 * 256 * 1024


NEG_FILL = -1e30


def partner(value, axis, distance):
    return lax.ppermute(value, axis, [(i, i ^ 1 << distance) for i in range(lax.axis_size(axis))])


def masked_softmax(scores, allowed):
    scores = jnp.where(allowed, scores, NEG_FILL)
    maximum = jnp.max(scores, axis=-1)
    raised = jnp.exp(scores - maximum[..., None])
    totals = jnp.sum(raised, axis=-1)
    return (maximum, totals, raised.astype(jnp.bfloat16))


def combine(first_part, second_part):
    highest = jnp.maximum(first_part[0], second_part[0])
    first_scale = jnp.exp(first_part[0] - highest)
    second_scale = jnp.exp(second_part[0] - highest)
    denominator = first_part[1] * first_scale + second_part[1] * second_scale
    numerator = first_part[2] * first_scale[..., None] + second_part[2] * second_scale[..., None]
    return (numerator / denominator[..., None]).astype(jnp.bfloat16)


def into_rows(tensor, row_blocks, head_groups):
    trailing = tensor.shape[3:]
    block_rows = tensor.shape[0] // row_blocks
    width_cols = tensor.shape[1]
    group_heads = tensor.shape[2] // head_groups
    shaped = tensor.reshape(
        (row_blocks, block_rows, width_cols, head_groups, group_heads) + trailing
    )
    permuted = (0, 3, 1, 2, 4) + tuple(range(5, 5 + len(trailing)))
    return shaped.transpose(permuted).reshape(
        (row_blocks * head_groups, block_rows, width_cols, group_heads) + trailing
    )


def into_tokens(tensor, row_blocks, head_groups):
    trailing = tensor.shape[4:]
    block_rows = tensor.shape[1]
    width_cols = tensor.shape[2]
    group_heads = tensor.shape[3]
    shaped = tensor.reshape(
        (row_blocks, head_groups, block_rows, width_cols, group_heads) + trailing
    )
    permuted = (0, 2, 3, 1, 4) + tuple(range(5, 5 + len(trailing)))
    return shaped.transpose(permuted).reshape(
        (row_blocks * block_rows * width_cols, head_groups * group_heads) + trailing
    )


def general_shards(query_vectors, key_vectors, value_vectors, request_of_slot):
    scaling = HS ** (-0.5)
    token_count = ROWS * COLS
    partner_key, partner_value = partner((key_vectors, value_vectors), "view", 0)
    head_blocks = 4
    block_heads = HEADS // head_blocks
    own_query = query_vectors.reshape(token_count, head_blocks, block_heads, HS)
    both_keys = jnp.concatenate(
        [
            key_vectors.reshape(token_count, head_blocks, block_heads, HS),
            partner_key.reshape(token_count, head_blocks, block_heads, HS),
        ],
        axis=0,
    )
    both_values = jnp.concatenate(
        [
            value_vectors.reshape(token_count, head_blocks, block_heads, HS),
            partner_value.reshape(token_count, head_blocks, block_heads, HS),
        ],
        axis=0,
    )
    query_row = jnp.arange(token_count) // COLS
    key_row = jnp.arange(2 * token_count) % token_count // COLS
    local_allowed = query_row[:, None] != key_row[None, :]

    def local_block(triple):
        block_scores = (
            jnp.einsum("nhx,khx->hnk", triple[0], triple[1], preferred_element_type=jnp.float32)
            * scaling
        )
        block_peak, block_total, block_weights = masked_softmax(block_scores, local_allowed[None])
        block_sum = jnp.einsum(
            "hnk,khx->nhx", block_weights, triple[2], preferred_element_type=jnp.float32
        )
        return (block_peak.T, block_total.T, block_sum)

    block_peaks, block_totals, block_sums = lax.map(
        local_block,
        (
            jnp.moveaxis(own_query, 1, 0),
            jnp.moveaxis(both_keys, 1, 0),
            jnp.moveaxis(both_values, 1, 0),
        ),
    )
    local_peak = jnp.moveaxis(block_peaks, 0, 1).reshape(token_count, HEADS)
    local_total = jnp.moveaxis(block_totals, 0, 1).reshape(token_count, HEADS)
    local_sum = jnp.moveaxis(block_sums, 0, 1).reshape(token_count, HEADS, HS)
    device_count = lax.axis_size("view")
    slot_count = device_count // 4
    pass_images = device_count // 2
    head_groups = 8
    row_blocks = device_count // head_groups
    block_rows = ROWS // row_blocks
    slot_request = jnp.broadcast_to(
        request_of_slot[:, None], (request_of_slot.shape[0], 2 * COLS)
    ).reshape(-1)
    row_allowed = slot_request[:, None] == slot_request[None, :]

    def arrange(tensor):
        shaped = tensor.reshape(slot_count, 2, 2, block_rows, COLS, HS).transpose(1, 3, 0, 2, 4, 5)
        return shaped.reshape(2 * block_rows, pass_images * COLS, HS)

    def restore(tensor):
        trailing = tensor.shape[2:]
        shaped = tensor.reshape((2, block_rows, slot_count, 2, COLS) + trailing)
        permuted = (2, 0, 3, 1, 4) + tuple(range(5, 5 + len(trailing)))
        return shaped.transpose(permuted).reshape((device_count, block_rows, COLS) + trailing)

    def one_head(triple):
        row_scores = (
            jnp.einsum(
                "bnx,bkx->bnk",
                arrange(triple[0]),
                arrange(triple[1]),
                preferred_element_type=jnp.float32,
            )
            * scaling
        )
        row_peak, row_total, row_weights = masked_softmax(row_scores, row_allowed[None])
        row_sum = jnp.einsum(
            "bnk,bkx->bnx", row_weights, arrange(triple[2]), preferred_element_type=jnp.float32
        )
        return (restore(row_peak), restore(row_total), restore(row_sum))

    query_rows = into_rows(query_vectors.reshape(ROWS, COLS, HEADS, HS), row_blocks, head_groups)
    key_rows = into_rows(key_vectors.reshape(ROWS, COLS, HEADS, HS), row_blocks, head_groups)
    value_rows = into_rows(value_vectors.reshape(ROWS, COLS, HEADS, HS), row_blocks, head_groups)
    by_head = (
        jnp.moveaxis(
            lax.all_to_all(query_rows, "view", split_axis=0, concat_axis=0, tiled=True), 3, 0
        ),
        jnp.moveaxis(
            lax.all_to_all(key_rows, "view", split_axis=0, concat_axis=0, tiled=True), 3, 0
        ),
        jnp.moveaxis(
            lax.all_to_all(value_rows, "view", split_axis=0, concat_axis=0, tiled=True), 3, 0
        ),
    )
    row_peaks, row_totals, row_sums = lax.map(one_head, by_head)
    peak_part = jnp.moveaxis(row_peaks, 0, 3)
    total_part = jnp.moveaxis(row_totals, 0, 3)
    sum_part = jnp.moveaxis(row_sums, 0, 3)
    row_peak = lax.all_to_all(peak_part, "view", split_axis=0, concat_axis=0, tiled=True)
    row_total = lax.all_to_all(total_part, "view", split_axis=0, concat_axis=0, tiled=True)
    row_sum = lax.all_to_all(sum_part, "view", split_axis=0, concat_axis=0, tiled=True)
    row_peak = into_tokens(row_peak, row_blocks, head_groups)
    row_total = into_tokens(row_total, row_blocks, head_groups)
    row_sum = into_tokens(row_sum, row_blocks, head_groups)
    attended = combine((local_peak, local_total, local_sum), (row_peak, row_total, row_sum))
    return attended.reshape(1, ROWS, COLS, HEADS * HS)


PARTS = 4
SKEW = 4
CHUNK = 4
LAG = 1
GROUPS = 2


def pair_kernel(
    req_hbm, q_ref, k_ref, v_ref, o_ref,
    req_ref, queries, kv, outer, inner, crossing, ending, chosen, bias, results, sums, peaks, totals,
    req_sem, load_sem, swap_send, swap_recv, own_send, outer_recv, cross_send, inner_recv, end_send, out_send, out_recv, out_sem,
):
    half, size, _ = sums.shape
    rows = queries.shape[2]
    block = 2 * rows
    chunks = half // CHUNK
    me = lax.axis_index("view")
    domain = me % 2
    slot = me // 4
    other = 1 - domain
    twin = me + other - domain
    upper = slot // 2
    end_slot = 3 * upper
    mid_slot = 1 + upper
    is_end = slot == end_slot
    is_mid = slot == mid_slot
    near = me + 4 * (end_slot + mid_slot - 2 * slot)
    across = me + 4 * (3 - 2 * slot)

    def remote(src, dst, send, recv, device):
        return pltpu.make_async_remote_copy(
            src_ref=src, dst_ref=dst, send_sem=send, recv_sem=recv,
            device_id={"view": device}, device_id_type=pl.DeviceIdType.MESH,
        )

    def lanes(at, group):
        return pl.ds(pl.multiple_of((group * half + at) * size, size), size)

    sources = (k_ref, v_ref, q_ref)

    def wide(chunk, group):
        return pl.ds(pl.multiple_of((group * half + chunk * CHUNK) * size, CHUNK * size), CHUNK * size)

    def place(chunk, which, whose):
        columns = wide(chunk, 0)
        return queries.at[whose, :, :, columns] if which == 2 else kv.at[which, whose, :, :, columns]

    def load(chunk, which):
        return pltpu.make_async_copy(
            sources[which].at[:, :, wide(chunk, domain)], place(chunk, which, 0), load_sem.at[which, chunk]
        )

    def swap(chunk, which):
        return remote(
            sources[which].at[:, :, wide(chunk, other)], place(chunk, which, 1),
            swap_send.at[which], swap_recv.at[which, chunk], twin,
        )

    def own_copy(at, part):
        n = at * PARTS + part
        return remote(
            kv.at[part % 2, part // 2, :, :, lanes(at, 0)], outer.at[n], own_send, outer_recv.at[n], near
        )

    def cross_copy(n):
        return remote(crossing.at[n], inner.at[n], cross_send, inner_recv.at[n], across)

    def end_copy(n):
        return remote(ending.at[n], inner.at[n], end_send, inner_recv.at[n], near)

    def out_copy(at):
        return remote(results.at[1, at], o_ref.at[:, :, lanes(at, domain)], out_send, out_recv, twin)

    def keep_copy(at):
        return pltpu.make_async_copy(results.at[0, at], o_ref.at[:, :, lanes(at, domain)], out_sem)

    request = pltpu.make_async_copy(req_hbm, req_ref, req_sem)
    request.start()
    barrier = pltpu.get_barrier_semaphore()
    for device in (twin, near):
        pl.semaphore_signal(barrier, inc=1, device_id={"view": device}, device_id_type=pl.DeviceIdType.MESH)

    @pl.when(is_mid)
    def _():
        pl.semaphore_signal(barrier, inc=1, device_id={"view": across}, device_id_type=pl.DeviceIdType.MESH)

    for chunk in range(chunks):
        for which in range(3):
            load(chunk, which).start()

    @pl.when(is_mid)
    def _():
        pl.semaphore_wait(barrier, 3)

    @pl.when(is_end)
    def _():
        pl.semaphore_wait(barrier, 2)

    for which in range(2):
        swap(0, which).start()

    @pl.when(is_end)
    def _():
        for which in range(2):
            load(0, which).wait()
            own_copy(0, which).start()

    swap(0, 2).start()

    def exchange_next(at):
        @pl.when((at % CHUNK == CHUNK // 2) & (at < half - CHUNK))
        def _():
            for which in range(3):
                swap(at // CHUNK + 1, which).start()

    def fetched(at, which):
        @pl.when(at % CHUNK == 0)
        def _():
            load(at // CHUNK, which).wait()
            swap(at // CHUNK, which).wait_recv()

    @pl.when(is_end)
    def _():
        for which in range(2):
            swap(0, which).wait_recv()
            own_copy(0, 2 + which).start()

        @pl.loop(1, half)
        def _(at):
            for which in range(2):
                fetched(at, which)
            for part in range(PARTS):
                own_copy(at, part).start()
            exchange_next(at)

    request.wait()
    mine = req_ref[slot]
    end_same = (req_ref[end_slot] == mine).astype(jnp.int32)
    mid_same = (req_ref[mid_slot] == mine).astype(jnp.int32)
    far_same = jnp.maximum(
        (req_ref[3 - end_slot] == mine).astype(jnp.int32), (req_ref[3 - mid_slot] == mine).astype(jnp.int32)
    )
    near_same = jnp.minimum(end_same, mid_same)
    paired = jnp.maximum(near_same, far_same)

    query_row = lax.broadcasted_iota(jnp.int32, bias.shape, 0) % rows // COLS
    key_row = lax.broadcasted_iota(jnp.int32, bias.shape, 1) % rows // COLS
    bias[...] = jnp.where(paired > 0, jnp.where(query_row == key_row, 0.0, NEG_FILL), NEG_FILL)

    def own_unit(at, part):
        return kv[part % 2, part // 2, :, :, lanes(at, 0)]

    def pass_across(at, part):
        @pl.when(is_mid)
        def _():
            n = at * PARTS + part
            own_copy(at, part).wait_recv()
            crossing[n] = jnp.where(far_same > 0, own_unit(at, part), outer[n])
            cross_copy(n).start()

    def pass_out(at, part):
        n = at * PARTS + part
        cross_copy(n).wait_recv()

        @pl.when(is_mid)
        def _():
            ending[n] = jnp.where(near_same > 0, own_unit(at, part), inner[n])
            end_copy(n).start()

    scaling = size ** (-0.5) * LOG2E

    def scores_of(keys, asking):
        return (
            lax.dot_general(keys, asking, (((1,), (1,)), ((), ())), preferred_element_type=jnp.float32) * scaling
        )

    def weighted(raised, values):
        return lax.dot_general(
            values, raised.astype(jnp.bfloat16), (((0,), (0,)), ((), ())), preferred_element_type=jnp.float32
        )

    def own_part(at):
        asking = queries[:, :, :, lanes(at, 0)]
        scores = scores_of(
            kv[0, :, :, :, lanes(at, 0)].reshape(GROUPS * block, size),
            jnp.concatenate([asking[:, group].reshape(block, size) for group in range(GROUPS)], axis=0),
        )
        peak = jnp.max(scores, axis=0, keepdims=True)
        raised = jnp.exp2(scores - peak)
        total = jnp.sum(raised, axis=0, keepdims=True)
        return peak, total, weighted(raised, kv[1, :, :, :, lanes(at, 0)].reshape(GROUPS * block, size))

    def choose(at):
        @pl.when(is_mid)
        def _():
            chosen[...] = jnp.where(near_same > 0, outer[pl.ds(at * 4, 4)], inner[pl.ds(at * 4, 4)])

        @pl.when(is_end)
        def _():
            chosen[...] = inner[pl.ds(at * 4, 4)]

    def pair_part(at):
        def both(which, group):
            return jnp.concatenate([chosen[which, group], chosen[2 + which, group]], axis=0)

        attended = []
        for group in range(GROUPS):
            columns = slice(group * block, (group + 1) * block)
            scores = scores_of(both(0, group), queries[:, group, :, lanes(at, 0)].reshape(block, size)) + bias[...]
            own_peak = peaks[at, :, columns]
            peak = jnp.maximum(own_peak, jnp.max(scores, axis=0, keepdims=True))
            raised = jnp.exp2(scores - peak)
            kept = jnp.exp2(own_peak - peak)
            total = totals[at, :, columns] * kept + jnp.sum(raised, axis=0, keepdims=True)
            summed = sums[at, :, columns] * kept + weighted(raised, both(1, group))
            attended.append((summed * (1.0 / total)).T.astype(jnp.bfloat16).reshape(2, rows, size))
        return attended

    def compute(own, done):
        if done is not None:
            choose(done)
            attended = pair_part(done)
        if own is not None:
            peaks_own, totals_own, sums_own = own_part(own)
            peaks[own] = peaks_own
            totals[own] = totals_own
            sums[own] = sums_own
        if done is not None:
            for group in range(GROUPS):
                results[:, done, group] = attended[group]
            out_copy(done).start()
            keep_copy(done).start()

    def head(at, first):
        @pl.when(is_mid)
        def _():
            exchange_next(at)
            for which in range(2):
                fetched(at, which)

        fetched(at, 2)
        for part in range(PARTS):
            pass_across(at, part)
            behind = part - SKEW
            if not first or at * PARTS + behind >= 0:
                pass_out(at + behind // PARTS, behind % PARTS)
            if part == PARTS - 1:
                compute(at, None if first else at - LAG)

    for at in range(LAG):
        head(at, True)

    @pl.loop(LAG, half)
    def _(at):
        head(at, False)

    for number in range(half * PARTS - SKEW, half * PARTS):
        pass_out(number // PARTS, number % PARTS)
        if number % PARTS == PARTS - 1:
            compute(None, number // PARTS)

    whole = pl.ds(0, half * size)
    for which in range(3):
        side = sources[which].at[:, :, whole]
        remote(side, side, swap_send.at[which], out_recv, twin).wait_send()

    @pl.when(is_end)
    def _():
        remote(outer, outer, own_send, out_recv, near).wait_send()

    @pl.when(is_mid)
    def _():
        remote(crossing, inner, cross_send, out_recv, across).wait_send()
        remote(ending, inner, end_send, out_recv, near).wait_send()

    pltpu.make_async_copy(results.at[0], results.at[1], out_sem).wait()
    remote(results.at[1], results.at[1], out_send, out_recv, twin).wait()


def pair_shards(query_vectors, key_vectors, value_vectors, request_of_slot):
    rows = ROWS * COLS // GROUPS
    half = HEADS // 2
    flat = [tensor.reshape(GROUPS, rows, HEADS * HS) for tensor in (query_vectors, key_vectors, value_vectors)]
    vmem = pl.BlockSpec(memory_space=pltpu.VMEM)
    hbm = pl.BlockSpec(memory_space=pltpu.HBM)
    bank = pltpu.VMEM((half * 4, GROUPS, rows, HS), jnp.bfloat16)
    line = pltpu.VMEM((half, 1, GROUPS * 2 * rows), jnp.float32)
    one = pltpu.SemaphoreType.DMA
    three = pltpu.SemaphoreType.DMA((3, half // CHUNK))
    units = pltpu.SemaphoreType.DMA((half * PARTS,))
    scores = (2 * ROWS * COLS) ** 2 * half
    out = pl.pallas_call(
        pair_kernel,
        out_shape=jax.ShapeDtypeStruct((GROUPS, rows, HEADS * HS), jnp.bfloat16),
        in_specs=[hbm, hbm, hbm, hbm],
        out_specs=vmem,
        scratch_shapes=[
            pltpu.SMEM(request_of_slot.shape, jnp.int32),
            pltpu.VMEM((2, GROUPS, rows, half * HS), jnp.bfloat16),
            pltpu.VMEM((2, 2, GROUPS, rows, half * HS), jnp.bfloat16),
            bank, bank, bank, bank,
            pltpu.VMEM((4, GROUPS, rows, HS), jnp.bfloat16),
            pltpu.VMEM((2 * rows, 2 * rows), jnp.float32),
            pltpu.VMEM((2, half, GROUPS, rows, HS), jnp.bfloat16),
            pltpu.VMEM((half, HS, GROUPS * 2 * rows), jnp.float32),
            line, line,
            one, three, pltpu.SemaphoreType.DMA((3,)), three, one, units, one, units, one, one, one, one,
        ],
        compiler_params=pltpu.CompilerParams(
            collective_id=0, has_side_effects=True, vmem_limit_bytes=VMEM_LIMIT
        ),
        cost_estimate=pl.CostEstimate(
            flops=6 * scores * HS, bytes_accessed=8 * ROWS * COLS * HEADS * HS, transcendentals=2 * scores
        ),
    )(request_of_slot, *flat)
    return out.reshape(1, ROWS, COLS, HEADS * HS)


def solution(mesh):
    slot_count = mesh.shape["view"] // 4
    shards = pair_shards if slot_count == 4 else general_shards
    return jax.shard_map(
        shards,
        mesh=mesh,
        in_specs=(
            P(("groups", "view"), None, None, None),
            P(("groups", "view"), None, None, None),
            P(("groups", "view"), None, None, None),
            P("groups"),
        ),
        out_specs=P(("groups", "view"), None, None, None),
        check_vma=False,
    )
```

```python
import jax
import jax.numpy as jnp
from jax import lax
from jax.experimental import pallas as pl
from jax.experimental.pallas import tpu as pltpu
from jax.sharding import PartitionSpec as P

HEADS = 32
HS = 128
ROWS = 16
COLS = 8
LOG2E = 1.4426950408889634
VMEM_LIMIT = 209 * 256 * 1024


NEG_FILL = -1e30


def partner(value, axis, distance):
    return lax.ppermute(value, axis, [(i, i ^ 1 << distance) for i in range(lax.axis_size(axis))])


def masked_softmax(scores, allowed):
    scores = jnp.where(allowed, scores, NEG_FILL)
    maximum = jnp.max(scores, axis=-1)
    raised = jnp.exp(scores - maximum[..., None])
    totals = jnp.sum(raised, axis=-1)
    return (maximum, totals, raised.astype(jnp.bfloat16))


def combine(first_part, second_part):
    highest = jnp.maximum(first_part[0], second_part[0])
    first_scale = jnp.exp(first_part[0] - highest)
    second_scale = jnp.exp(second_part[0] - highest)
    denominator = first_part[1] * first_scale + second_part[1] * second_scale
    numerator = first_part[2] * first_scale[..., None] + second_part[2] * second_scale[..., None]
    return (numerator / denominator[..., None]).astype(jnp.bfloat16)


def into_rows(tensor, row_blocks, head_groups):
    trailing = tensor.shape[3:]
    block_rows = tensor.shape[0] // row_blocks
    width_cols = tensor.shape[1]
    group_heads = tensor.shape[2] // head_groups
    shaped = tensor.reshape(
        (row_blocks, block_rows, width_cols, head_groups, group_heads) + trailing
    )
    permuted = (0, 3, 1, 2, 4) + tuple(range(5, 5 + len(trailing)))
    return shaped.transpose(permuted).reshape(
        (row_blocks * head_groups, block_rows, width_cols, group_heads) + trailing
    )


def into_tokens(tensor, row_blocks, head_groups):
    trailing = tensor.shape[4:]
    block_rows = tensor.shape[1]
    width_cols = tensor.shape[2]
    group_heads = tensor.shape[3]
    shaped = tensor.reshape(
        (row_blocks, head_groups, block_rows, width_cols, group_heads) + trailing
    )
    permuted = (0, 2, 3, 1, 4) + tuple(range(5, 5 + len(trailing)))
    return shaped.transpose(permuted).reshape(
        (row_blocks * block_rows * width_cols, head_groups * group_heads) + trailing
    )


def general_shards(query_vectors, key_vectors, value_vectors, request_of_slot):
    scaling = HS ** (-0.5)
    token_count = ROWS * COLS
    partner_key, partner_value = partner((key_vectors, value_vectors), "view", 0)
    head_blocks = 4
    block_heads = HEADS // head_blocks
    own_query = query_vectors.reshape(token_count, head_blocks, block_heads, HS)
    both_keys = jnp.concatenate(
        [
            key_vectors.reshape(token_count, head_blocks, block_heads, HS),
            partner_key.reshape(token_count, head_blocks, block_heads, HS),
        ],
        axis=0,
    )
    both_values = jnp.concatenate(
        [
            value_vectors.reshape(token_count, head_blocks, block_heads, HS),
            partner_value.reshape(token_count, head_blocks, block_heads, HS),
        ],
        axis=0,
    )
    query_row = jnp.arange(token_count) // COLS
    key_row = jnp.arange(2 * token_count) % token_count // COLS
    local_allowed = query_row[:, None] != key_row[None, :]

    def local_block(triple):
        block_scores = (
            jnp.einsum("nhx,khx->hnk", triple[0], triple[1], preferred_element_type=jnp.float32)
            * scaling
        )
        block_peak, block_total, block_weights = masked_softmax(block_scores, local_allowed[None])
        block_sum = jnp.einsum(
            "hnk,khx->nhx", block_weights, triple[2], preferred_element_type=jnp.float32
        )
        return (block_peak.T, block_total.T, block_sum)

    block_peaks, block_totals, block_sums = lax.map(
        local_block,
        (
            jnp.moveaxis(own_query, 1, 0),
            jnp.moveaxis(both_keys, 1, 0),
            jnp.moveaxis(both_values, 1, 0),
        ),
    )
    local_peak = jnp.moveaxis(block_peaks, 0, 1).reshape(token_count, HEADS)
    local_total = jnp.moveaxis(block_totals, 0, 1).reshape(token_count, HEADS)
    local_sum = jnp.moveaxis(block_sums, 0, 1).reshape(token_count, HEADS, HS)
    device_count = lax.axis_size("view")
    slot_count = device_count // 4
    pass_images = device_count // 2
    head_groups = 8
    row_blocks = device_count // head_groups
    block_rows = ROWS // row_blocks
    slot_request = jnp.broadcast_to(
        request_of_slot[:, None], (request_of_slot.shape[0], 2 * COLS)
    ).reshape(-1)
    row_allowed = slot_request[:, None] == slot_request[None, :]

    def arrange(tensor):
        shaped = tensor.reshape(slot_count, 2, 2, block_rows, COLS, HS).transpose(1, 3, 0, 2, 4, 5)
        return shaped.reshape(2 * block_rows, pass_images * COLS, HS)

    def restore(tensor):
        trailing = tensor.shape[2:]
        shaped = tensor.reshape((2, block_rows, slot_count, 2, COLS) + trailing)
        permuted = (2, 0, 3, 1, 4) + tuple(range(5, 5 + len(trailing)))
        return shaped.transpose(permuted).reshape((device_count, block_rows, COLS) + trailing)

    def one_head(triple):
        row_scores = (
            jnp.einsum(
                "bnx,bkx->bnk",
                arrange(triple[0]),
                arrange(triple[1]),
                preferred_element_type=jnp.float32,
            )
            * scaling
        )
        row_peak, row_total, row_weights = masked_softmax(row_scores, row_allowed[None])
        row_sum = jnp.einsum(
            "bnk,bkx->bnx", row_weights, arrange(triple[2]), preferred_element_type=jnp.float32
        )
        return (restore(row_peak), restore(row_total), restore(row_sum))

    query_rows = into_rows(query_vectors.reshape(ROWS, COLS, HEADS, HS), row_blocks, head_groups)
    key_rows = into_rows(key_vectors.reshape(ROWS, COLS, HEADS, HS), row_blocks, head_groups)
    value_rows = into_rows(value_vectors.reshape(ROWS, COLS, HEADS, HS), row_blocks, head_groups)
    by_head = (
        jnp.moveaxis(
            lax.all_to_all(query_rows, "view", split_axis=0, concat_axis=0, tiled=True), 3, 0
        ),
        jnp.moveaxis(
            lax.all_to_all(key_rows, "view", split_axis=0, concat_axis=0, tiled=True), 3, 0
        ),
        jnp.moveaxis(
            lax.all_to_all(value_rows, "view", split_axis=0, concat_axis=0, tiled=True), 3, 0
        ),
    )
    row_peaks, row_totals, row_sums = lax.map(one_head, by_head)
    peak_part = jnp.moveaxis(row_peaks, 0, 3)
    total_part = jnp.moveaxis(row_totals, 0, 3)
    sum_part = jnp.moveaxis(row_sums, 0, 3)
    row_peak = lax.all_to_all(peak_part, "view", split_axis=0, concat_axis=0, tiled=True)
    row_total = lax.all_to_all(total_part, "view", split_axis=0, concat_axis=0, tiled=True)
    row_sum = lax.all_to_all(sum_part, "view", split_axis=0, concat_axis=0, tiled=True)
    row_peak = into_tokens(row_peak, row_blocks, head_groups)
    row_total = into_tokens(row_total, row_blocks, head_groups)
    row_sum = into_tokens(row_sum, row_blocks, head_groups)
    attended = combine((local_peak, local_total, local_sum), (row_peak, row_total, row_sum))
    return attended.reshape(1, ROWS, COLS, HEADS * HS)


PARTS = 4
SKEW = 5
CHUNK = 4
LAG = 2
GROUPS = 2


def pair_kernel(
    req_hbm, q_ref, k_ref, v_ref, o_ref,
    req_ref, queries, kv, outer, inner, crossing, ending, chosen, bias, results, sums, peaks, totals,
    req_sem, load_sem, swap_send, swap_recv, own_send, outer_recv, cross_send, inner_recv, end_send, out_send, out_recv, out_sem,
):
    half, size, _ = sums.shape
    rows = queries.shape[2]
    block = 2 * rows
    chunks = half // CHUNK
    me = lax.axis_index("view")
    domain = me % 2
    slot = me // 4
    other = 1 - domain
    twin = me + other - domain
    upper = slot // 2
    end_slot = 3 * upper
    mid_slot = 1 + upper
    is_end = slot == end_slot
    is_mid = slot == mid_slot
    near = me + 4 * (end_slot + mid_slot - 2 * slot)
    across = me + 4 * (3 - 2 * slot)

    def remote(src, dst, send, recv, device):
        return pltpu.make_async_remote_copy(
            src_ref=src, dst_ref=dst, send_sem=send, recv_sem=recv,
            device_id={"view": device}, device_id_type=pl.DeviceIdType.MESH,
        )

    def lanes(at, group):
        return pl.ds(pl.multiple_of((group * half + at) * size, size), size)

    sources = (k_ref, v_ref, q_ref)

    def wide(chunk, group):
        return pl.ds(pl.multiple_of((group * half + chunk * CHUNK) * size, CHUNK * size), CHUNK * size)

    def place(chunk, which, whose):
        columns = wide(chunk, 0)
        return queries.at[whose, :, :, columns] if which == 2 else kv.at[which, whose, :, :, columns]

    def load(chunk, which):
        return pltpu.make_async_copy(
            sources[which].at[:, :, wide(chunk, domain)], place(chunk, which, 0), load_sem.at[which, chunk]
        )

    def swap(chunk, which):
        return remote(
            sources[which].at[:, :, wide(chunk, other)], place(chunk, which, 1),
            swap_send.at[which], swap_recv.at[which, chunk], twin,
        )

    def own_copy(at, part):
        n = at * PARTS + part
        return remote(
            kv.at[part % 2, part // 2, :, :, lanes(at, 0)], outer.at[n], own_send, outer_recv.at[n], near
        )

    def cross_copy(n):
        return remote(crossing.at[n], inner.at[n], cross_send, inner_recv.at[n], across)

    def end_copy(n):
        return remote(ending.at[n], inner.at[n], end_send, inner_recv.at[n], near)

    def out_copy(at):
        return remote(results.at[1, at], o_ref.at[:, :, lanes(at, domain)], out_send, out_recv, twin)

    def keep_copy(at):
        return pltpu.make_async_copy(results.at[0, at], o_ref.at[:, :, lanes(at, domain)], out_sem)

    request = pltpu.make_async_copy(req_hbm, req_ref, req_sem)
    request.start()
    barrier = pltpu.get_barrier_semaphore()
    for device in (twin, near):
        pl.semaphore_signal(barrier, inc=1, device_id={"view": device}, device_id_type=pl.DeviceIdType.MESH)

    @pl.when(is_mid)
    def _():
        pl.semaphore_signal(barrier, inc=1, device_id={"view": across}, device_id_type=pl.DeviceIdType.MESH)

    for chunk in range(chunks):
        for which in range(3):
            load(chunk, which).start()

    @pl.when(is_mid)
    def _():
        pl.semaphore_wait(barrier, 3)

    @pl.when(is_end)
    def _():
        pl.semaphore_wait(barrier, 2)

    for which in range(2):
        swap(0, which).start()

    @pl.when(is_end)
    def _():
        for which in range(2):
            load(0, which).wait()
            own_copy(0, which).start()

    swap(0, 2).start()

    def exchange_next(at):
        @pl.when((at % CHUNK == CHUNK // 2) & (at < half - CHUNK))
        def _():
            for which in range(3):
                swap(at // CHUNK + 1, which).start()

    def fetched(at, which):
        @pl.when(at % CHUNK == 0)
        def _():
            load(at // CHUNK, which).wait()
            swap(at // CHUNK, which).wait_recv()

    @pl.when(is_end)
    def _():
        for which in range(2):
            swap(0, which).wait_recv()
            own_copy(0, 2 + which).start()

        @pl.loop(1, half)
        def _(at):
            for which in range(2):
                fetched(at, which)
            for part in range(PARTS):
                own_copy(at, part).start()
            exchange_next(at)

    request.wait()
    mine = req_ref[slot]
    end_same = (req_ref[end_slot] == mine).astype(jnp.int32)
    mid_same = (req_ref[mid_slot] == mine).astype(jnp.int32)
    far_same = jnp.maximum(
        (req_ref[3 - end_slot] == mine).astype(jnp.int32), (req_ref[3 - mid_slot] == mine).astype(jnp.int32)
    )
    near_same = jnp.minimum(end_same, mid_same)
    paired = jnp.maximum(near_same, far_same)

    query_row = lax.broadcasted_iota(jnp.int32, bias.shape, 0) % rows // COLS
    key_row = lax.broadcasted_iota(jnp.int32, bias.shape, 1) % rows // COLS
    bias[...] = jnp.where(paired > 0, jnp.where(query_row == key_row, 0.0, NEG_FILL), NEG_FILL)

    def own_unit(at, part):
        return kv[part % 2, part // 2, :, :, lanes(at, 0)]

    def pass_across(at, part):
        @pl.when(is_mid)
        def _():
            n = at * PARTS + part
            own_copy(at, part).wait_recv()
            crossing[n] = jnp.where(far_same > 0, own_unit(at, part), outer[n])
            cross_copy(n).start()

    def pass_out(at, part):
        n = at * PARTS + part
        cross_copy(n).wait_recv()

        @pl.when(is_mid)
        def _():
            ending[n] = jnp.where(near_same > 0, own_unit(at, part), inner[n])
            end_copy(n).start()

    scaling = size ** (-0.5) * LOG2E

    def scores_of(keys, asking):
        return (
            lax.dot_general(keys, asking, (((1,), (1,)), ((), ())), preferred_element_type=jnp.float32) * scaling
        )

    def weighted(raised, values):
        return lax.dot_general(
            values, raised.astype(jnp.bfloat16), (((0,), (0,)), ((), ())), preferred_element_type=jnp.float32
        )

    def own_part(at):
        asking = queries[:, :, :, lanes(at, 0)]
        scores = scores_of(
            kv[0, :, :, :, lanes(at, 0)].reshape(GROUPS * block, size),
            jnp.concatenate([asking[:, group].reshape(block, size) for group in range(GROUPS)], axis=0),
        )
        peak = jnp.max(scores, axis=0, keepdims=True)
        raised = jnp.exp2(scores - peak)
        total = jnp.sum(raised, axis=0, keepdims=True)
        return peak, total, weighted(raised, kv[1, :, :, :, lanes(at, 0)].reshape(GROUPS * block, size))

    def choose(at):
        @pl.when(is_mid)
        def _():
            chosen[...] = jnp.where(near_same > 0, outer[pl.ds(at * 4, 4)], inner[pl.ds(at * 4, 4)])

        @pl.when(is_end)
        def _():
            chosen[...] = inner[pl.ds(at * 4, 4)]

    def pair_part(at):
        def both(which, group):
            return jnp.concatenate([chosen[which, group], chosen[2 + which, group]], axis=0)

        attended = []
        for group in range(GROUPS):
            columns = slice(group * block, (group + 1) * block)
            scores = scores_of(both(0, group), queries[:, group, :, lanes(at, 0)].reshape(block, size)) + bias[...]
            own_peak = peaks[at, :, columns]
            peak = jnp.maximum(own_peak, jnp.max(scores, axis=0, keepdims=True))
            raised = jnp.exp2(scores - peak)
            kept = jnp.exp2(own_peak - peak)
            total = totals[at, :, columns] * kept + jnp.sum(raised, axis=0, keepdims=True)
            summed = sums[at, :, columns] * kept + weighted(raised, both(1, group))
            attended.append((summed * (1.0 / total)).T.astype(jnp.bfloat16).reshape(2, rows, size))
        return attended

    def compute(own, done):
        if done is not None:
            choose(done)
            attended = pair_part(done)
        if own is not None:
            peaks_own, totals_own, sums_own = own_part(own)
            peaks[own] = peaks_own
            totals[own] = totals_own
            sums[own] = sums_own
        if done is not None:
            for group in range(GROUPS):
                results[:, done, group] = attended[group]
            out_copy(done).start()
            keep_copy(done).start()

    def head(at, first):
        @pl.when(is_mid)
        def _():
            exchange_next(at)
            for which in range(2):
                fetched(at, which)

        fetched(at, 2)
        for part in range(PARTS):
            pass_across(at, part)
            behind = part - SKEW
            if not first or at * PARTS + behind >= 0:
                pass_out(at + behind // PARTS, behind % PARTS)
            if part == PARTS - 1:
                compute(at, None if first else at - LAG)

    for at in range(LAG):
        head(at, True)

    @pl.loop(LAG, half)
    def _(at):
        head(at, False)

    for number in range(half * PARTS - SKEW, half * PARTS):
        pass_out(number // PARTS, number % PARTS)
        if number % PARTS == PARTS - 1:
            compute(None, number // PARTS)

    whole = pl.ds(0, half * size)
    for which in range(3):
        side = sources[which].at[:, :, whole]
        remote(side, side, swap_send.at[which], out_recv, twin).wait_send()

    @pl.when(is_end)
    def _():
        remote(outer, outer, own_send, out_recv, near).wait_send()

    @pl.when(is_mid)
    def _():
        remote(crossing, inner, cross_send, out_recv, across).wait_send()
        remote(ending, inner, end_send, out_recv, near).wait_send()

    pltpu.make_async_copy(results.at[0], results.at[1], out_sem).wait()
    remote(results.at[1], results.at[1], out_send, out_recv, twin).wait()


def pair_shards(query_vectors, key_vectors, value_vectors, request_of_slot):
    rows = ROWS * COLS // GROUPS
    half = HEADS // 2
    flat = [tensor.reshape(GROUPS, rows, HEADS * HS) for tensor in (query_vectors, key_vectors, value_vectors)]
    vmem = pl.BlockSpec(memory_space=pltpu.VMEM)
    hbm = pl.BlockSpec(memory_space=pltpu.HBM)
    bank = pltpu.VMEM((half * 4, GROUPS, rows, HS), jnp.bfloat16)
    line = pltpu.VMEM((half, 1, GROUPS * 2 * rows), jnp.float32)
    one = pltpu.SemaphoreType.DMA
    three = pltpu.SemaphoreType.DMA((3, half // CHUNK))
    units = pltpu.SemaphoreType.DMA((half * PARTS,))
    scores = (2 * ROWS * COLS) ** 2 * half
    out = pl.pallas_call(
        pair_kernel,
        out_shape=jax.ShapeDtypeStruct((GROUPS, rows, HEADS * HS), jnp.bfloat16),
        in_specs=[hbm, hbm, hbm, hbm],
        out_specs=vmem,
        scratch_shapes=[
            pltpu.SMEM(request_of_slot.shape, jnp.int32),
            pltpu.VMEM((2, GROUPS, rows, half * HS), jnp.bfloat16),
            pltpu.VMEM((2, 2, GROUPS, rows, half * HS), jnp.bfloat16),
            bank, bank, bank, bank,
            pltpu.VMEM((4, GROUPS, rows, HS), jnp.bfloat16),
            pltpu.VMEM((2 * rows, 2 * rows), jnp.float32),
            pltpu.VMEM((2, half, GROUPS, rows, HS), jnp.bfloat16),
            pltpu.VMEM((half, HS, GROUPS * 2 * rows), jnp.float32),
            line, line,
            one, three, pltpu.SemaphoreType.DMA((3,)), three, one, units, one, units, one, one, one, one,
        ],
        compiler_params=pltpu.CompilerParams(
            collective_id=0, has_side_effects=True, vmem_limit_bytes=VMEM_LIMIT
        ),
        cost_estimate=pl.CostEstimate(
            flops=6 * scores * HS, bytes_accessed=8 * ROWS * COLS * HEADS * HS, transcendentals=2 * scores
        ),
    )(request_of_slot, *flat)
    return out.reshape(1, ROWS, COLS, HEADS * HS)


def solution(mesh):
    slot_count = mesh.shape["view"] // 4
    shards = pair_shards if slot_count == 4 else general_shards
    return jax.shard_map(
        shards,
        mesh=mesh,
        in_specs=(
            P(("groups", "view"), None, None, None),
            P(("groups", "view"), None, None, None),
            P(("groups", "view"), None, None, None),
            P("groups"),
        ),
        out_specs=P(("groups", "view"), None, None, None),
        check_vma=False,
    )
```
